32 devices in a mesh: seq: 8 (over y, x, core), tp: 4 (over z).
Axes of the slice: x: 2, y: 2, z: 4, core: 2. Of those that a mesh axis runs over, the one named last changes fastest.
Arguments:
- tokens: bfloat16 [16384, 1024], P(('seq', 'tp')), may hold values from -6 to 6
- w_qkv: bfloat16 [1024, 3, 1024], P(None, None, 'tp'), may hold values from -0.1875 to 0.1875
- w_out: bfloat16 [1024, 1024], P('tp'), may hold values from -3 to 3
- w_up: bfloat16 [1024, 4096], P(None, 'tp'), may hold values from -0.1875 to 0.1875
- w_down: bfloat16 [4096, 1024], P('tp'), may hold values from -0.09375 to 0.09375
- gain_one: float32 [1024], replicated, may hold values from 0.1 to 1.9
- gain_two: float32 [1024], replicated, may hold values from 0.1 to 1.9
- cotangent: bfloat16 [16384, 1024], P(('seq', 'tp')), may hold values from -6 to 6
- bucket: int32 [8], P('seq'), may hold values from 0 to 1, as said below
- lengths: int32 [8, 4], P('seq'), may hold values from 0 to 2048, as said below
Outputs:
- mixed: bfloat16 [16384, 1024], P(('seq', 'tp'))
- tokens_grad: bfloat16 [16384, 1024], P(('seq', 'tp'))
- grad_qkv: float32 [1024, 3, 1024], P(None, None, 'tp')
- grad_out: float32 [1024, 1024], P('tp')
- grad_up: float32 [1024, 4096], P(None, 'tp')
- grad_down: float32 [4096, 1024], P('tp')
- grad_gain_one: float32 [1024], replicated
- grad_gain_two: float32 [1024], replicated
The draws below stay inside these ranges and needn't reach their ends.
Inputs may be any that keep to these rules, and one draw needn't show every extreme that they name: Every draw has groups of both buckets; bucket 1 means one sequence of 2048 positions, bucket 0 means 4 sequences of 512 positions. `lengths`: for a group of bucket 1 the first entry is its sequence's length, from 1024 to 2048, and the others are 0; for bucket 0 each entry is from 256 to 512; padding stands at the end of a sequence, and some group holds a sequence of full length 2048.
All inputs are finite; a program needn't handle non-finite values.
Results may differ from the reference program's by a relative error of at most 0.014.
Values may be sent and summed in bfloat16 or wider, within the bound.
No kernel may reach another device: no remote copies, remote signals or barrier semaphores. Data moves between devices by JAX's collectives and lax.ppermute only.
A program may use at most 192 MiB of HBM per device.

```python
from functools import partial
import jax
import jax.numpy as jnp
from jax import lax

D = 1024
HEADS = 16
HEAD = 64
FF = 4096
SLOTS = 4
GROUP_TOK = 2048
GROUPS = 8
TOKENS = 16384


def group_layout(key):
    folded = jax.random.fold_in(key, 1234)
    kind_key, pick_key, slot_key, long_key = jax.random.split(folded, 4)
    group_index = jnp.arange(GROUPS, dtype=jnp.int32)
    bucket_ids = jax.random.randint(kind_key, (GROUPS,), 0, 2, dtype=jnp.int32)
    chosen = jax.random.randint(pick_key, (), 0, GROUPS, dtype=jnp.int32)
    bucket_ids = jnp.where(group_index == chosen, 1, bucket_ids)
    bucket_ids = jnp.where(group_index == (chosen + 1) % GROUPS, 0, bucket_ids)
    slot_rows = GROUP_TOK // SLOTS
    slot_lengths = jax.random.randint(slot_key, (GROUPS, SLOTS), slot_rows // 2, slot_rows + 1, dtype=jnp.int32)
    long_lengths = jax.random.randint(long_key, (GROUPS,), GROUP_TOK // 2, GROUP_TOK + 1, dtype=jnp.int32)
    long_lengths = jnp.where(group_index == chosen, GROUP_TOK, long_lengths)
    column = jnp.arange(SLOTS, dtype=jnp.int32)
    single = jnp.where(column[None, :] == 0, long_lengths[:, None], 0)
    lengths_out = jnp.where(bucket_ids[:, None] == 1, single, slot_lengths)
    return (bucket_ids.astype(jnp.int32), lengths_out.astype(jnp.int32))


def draw_bucket(key, part):
    return group_layout(key)[0]


def draw_lengths(key, part):
    return group_layout(key)[1]


def levels(key, extent, shards, smallest, largest):
    factor_of, own = 1.0, jax.random.fold_in(key, 6)
    for axis_at, blocks in shards:
        heights = jnp.exp(jax.random.uniform(jax.random.fold_in(own, axis_at), (blocks,), jnp.float32, smallest / len(shards), largest / len(shards)))
        factor_of = factor_of * jnp.repeat(heights, extent[axis_at] // blocks).reshape([-1 if axis == axis_at else 1 for axis in range(len(extent))])
    return factor_of


def noise(rng, shape, scale, most, shards=(), held_as=jnp.bfloat16):
    factor_of = levels(rng, shape, shards, -0.22, 0.18) if shards else 1.0
    entries = jax.random.normal(rng, shape, jnp.float32) * scale * factor_of
    return jnp.minimum(jnp.maximum(entries, -most), most).astype(held_as)


def setup_inputs(seed: int = 0) -> dict:
    splits = jax.random.split(jax.random.key(seed), 11)
    tokens = noise(splits[0], (TOKENS, D), 1.0, 6.0, ((0, 32),))
    w_qkv = noise(splits[1], (D, 3, D), D ** -0.5, 0.1875, ((2, 4),))
    w_out = noise(splits[2], (D, D), (max(D // 256, 1)) ** -0.5, 3.0, ((0, 4),))
    w_up = noise(splits[3], (D, FF), D ** -0.5, 0.1875, ((1, 4),))
    w_down = noise(splits[4], (FF, D), FF ** -0.5, 0.09375, ((0, 4),))
    gain_one = jnp.clip(1.0 + 0.18 * jax.random.normal(splits[5], (D,), jnp.float32), 0.1, 1.9)
    gain_two = jnp.clip(1.0 + 0.18 * jax.random.normal(splits[6], (D,), jnp.float32), 0.1, 1.9)
    cotangent = noise(splits[7], (TOKENS, D), 1.0, 6.0, ((0, 32),))
    bucket = draw_bucket(jax.random.fold_in(splits[10], 71), 0)
    lengths = draw_lengths(jax.random.fold_in(splits[10], 71), 0)
    return {"tokens": tokens, "w_qkv": w_qkv, "w_out": w_out, "w_up": w_up, "w_down": w_down, "gain_one": gain_one, "gain_two": gain_two, "cotangent": cotangent, "bucket": bucket, "lengths": lengths}


ln_eps = 1e-05
highest = lax.Precision.HIGHEST

@jax.custom_vjp
def low(v):
    return lax.optimization_barrier(v.astype(jnp.bfloat16)).astype(jnp.float32)

@jax.custom_vjp
def low_back(v):
    return v

def low_keep(v):
    return (low(v), None)

def low_pass(kept, grad):
    return (grad,)

def back_keep(v):
    return (v, None)

def back_low(kept, grad):
    return (low(grad),)
low.defvjp(low_keep, low_pass)
low_back.defvjp(back_keep, back_low)

def layer_norm(values, gain):
    centre = values - lax.optimization_barrier(jnp.mean(values, axis=-1, keepdims=True))
    spread = lax.optimization_barrier(jnp.mean(centre * centre, axis=-1, keepdims=True))
    return centre * lax.rsqrt(spread + ln_eps) * gain

def group_mask(bucket_id, slot_lengths, row_count):
    slot_rows = row_count // SLOTS
    position = jnp.arange(row_count, dtype=jnp.int32)
    whole_group = bucket_id == 1
    segment = jnp.where(whole_group, 0, position // slot_rows).astype(jnp.int32)
    inside = jnp.where(whole_group, position, position % slot_rows)
    chosen = segment[:, None] == jnp.arange(SLOTS, dtype=jnp.int32)[None, :]
    limit = lax.optimization_barrier(jnp.sum(jnp.where(chosen, slot_lengths[None, :], 0), axis=1))
    return (segment, inside < limit)

def attention(queries, keys_all, values_all, segment, valid):
    row_count = queries.shape[0]
    block_rows = min(512, row_count)
    block_count = row_count // block_rows
    score_scale = HEAD ** (-0.5)
    query_blocks = queries.reshape(block_count, block_rows, HEADS, HEAD)
    segment_blocks = segment.reshape(block_count, block_rows)

    def one_block(member):
        block_queries, block_segment = member
        scores = jnp.einsum('qhe,khe->hqk', block_queries, keys_all, precision=highest) * score_scale
        allowed = (block_segment[:, None] == segment[None, :]) & valid[None, :]
        scores = low_back(jnp.where(allowed[None], scores, -1000000000.0))
        log_total = jax.nn.logsumexp(scores, axis=-1, keepdims=True)
        weights = low(jnp.exp(scores - log_total))
        return jnp.einsum('hqk,khe->qhe', weights, values_all, precision=highest)
    mixed_blocks = lax.map(jax.checkpoint(one_block), (query_blocks, segment_blocks))
    return mixed_blocks.reshape(row_count, HEADS, HEAD)

def forward(inputs, w_qkv, w_out, w_up, w_down, gain_one, gain_two, segment, valid):
    row_count = inputs.shape[0]
    projected = jnp.einsum('rd,dcn->rcn', inputs, w_qkv, precision=highest)
    projected = low(low_back(projected))
    queries = projected[:, 0].reshape(row_count, HEADS, HEAD)
    keys_all = projected[:, 1].reshape(row_count, HEADS, HEAD)
    values_all = projected[:, 2].reshape(row_count, HEADS, HEAD)
    attended = attention(queries, keys_all, values_all, segment, valid).reshape(row_count, D)
    attended = low(low_back(attended))
    branch = low_back(jnp.dot(attended, w_out, precision=highest))
    normed = layer_norm(inputs + branch, gain_one)
    expanded = low_back(jnp.dot(low(normed), w_up, precision=highest))
    activated = low(jax.nn.gelu(expanded, approximate=False))
    shrunk = low_back(jnp.dot(activated, w_down, precision=highest))
    return layer_norm(normed + shrunk, gain_two)

def reference(tokens, w_qkv, w_out, w_up, w_down, gain_one, gain_two, cotangent, bucket, lengths):
    weight_arrays = (w_qkv.astype(jnp.float32), w_out.astype(jnp.float32), w_up.astype(jnp.float32), w_down.astype(jnp.float32), gain_one.astype(jnp.float32), gain_two.astype(jnp.float32))
    token_groups = tokens.reshape(GROUPS, GROUP_TOK, D)
    cot_groups = cotangent.reshape(GROUPS, GROUP_TOK, D)

    def one_group(totals, member):
        group_tokens, group_cot, bucket_id, slot_lengths = member
        segment, valid = group_mask(bucket_id, slot_lengths, GROUP_TOK)
        layer = partial(forward, segment=segment, valid=valid)
        outputs, pullback = jax.vjp(layer, group_tokens.astype(jnp.float32), weight_arrays[0], weight_arrays[1], weight_arrays[2], weight_arrays[3], weight_arrays[4], weight_arrays[5])
        gradients = pullback(group_cot.astype(jnp.float32))
        totals = tuple((total + grad for total, grad in zip(totals, gradients[1:])))
        return (totals, (outputs.astype(jnp.bfloat16), gradients[0].astype(jnp.bfloat16)))
    initial = tuple((jnp.zeros(weight_array.shape, jnp.float32) for weight_array in weight_arrays))
    gradient_sums, (mixed, token_grads) = lax.scan(one_group, initial, (token_groups, cot_groups, bucket, lengths))
    return (mixed.reshape(TOKENS, D), token_grads.reshape(TOKENS, D), gradient_sums[0], gradient_sums[1], gradient_sums[2], gradient_sums[3], gradient_sums[4], gradient_sums[5])
```

```python
import functools

import jax
import jax.numpy as jnp
from jax import lax
from jax.experimental import pallas as pl
from jax.experimental.pallas import tpu as pltpu
from jax.sharding import PartitionSpec as P

HEAD = 64
SLOTS = 4
BF = jnp.bfloat16
F32 = jnp.float32
LOG2E = 1.4426950408889634
LN_EPS = 1e-5
NT = (((1,), (1,)), ((), ()))
NN = (((1,), (0,)), ((), ()))
TN = (((0,), (0,)), ((), ()))

PAIR = [(0, 1), (1, 0), (2, 3), (3, 2)]
MIDDLE = [(1, 2), (2, 1)]
OUTWARD = [(1, 0), (2, 3)]
INWARD = [(0, 1), (3, 2)]


def mm(a, b, dims, out=F32):
    return lax.dot_general(a, b, dims, preferred_element_type=F32).astype(out)


def along(array, pairs):
    return lax.ppermute(array, "tp", pairs)


def line_gather(own, middle):
    near = along(own, PAIR)
    far = along(own, MIDDLE)
    second = along(near, MIDDLE)
    second_end = along(far, OUTWARD)
    third_end = along(second, OUTWARD)
    return [
        own,
        near,
        jnp.where(middle, second, second_end),
        jnp.where(middle, far, third_end),
    ]


def line_scatter(parts):
    first, near, second, third = parts
    up = lambda a: a.astype(F32)
    from_third = along(third, INWARD)
    from_second = along(second, INWARD)
    second_sum = (up(second) + up(from_third)).astype(BF)
    near_in = along(second_sum, MIDDLE)
    third_sum = (up(third) + up(from_second)).astype(BF)
    near_sum = (up(near) + up(near_in)).astype(BF)
    far_in = along(third_sum, MIDDLE)
    last = along(near_sum, PAIR)
    return up(first) + up(last) + up(far_in)


class Plane:
    def __init__(self, size):
        self.size = size

    def swap(self, array, bit):
        return lax.ppermute(array, "seq", [(i, i ^ bit) for i in range(self.size)])

    def gather(self, own):
        half = own.shape[0] // 2
        by_x = self.swap(own, 2)
        by_y = self.swap(own, 4)
        diag = (self.swap(by_y[:half], 2), self.swap(by_x[half:], 4))
        other = [self.swap(a, 1) for a in (own, by_x, by_y) + diag]
        diag, other_diag = jnp.concatenate(diag), jnp.concatenate(other[3:])
        return [own, other[0], by_x, other[1], by_y, other[2], diag, other_diag]

    def reduce(self, pieces):
        up = lambda a: a.astype(F32)
        came = [self.swap(pieces[i], 1) for i in (7, 5, 3, 1)][::-1]
        own, by_x, by_y, diag = [
            (up(pieces[2 * i]) + up(came[i])).astype(BF) for i in range(4)
        ]
        axis = diag.ndim - 2
        half = diag.shape[axis] // 2
        cut = lambda a, at: lax.slice_in_dim(a, at * half, (at + 1) * half, axis=axis)
        diag_x = self.swap(cut(diag, 0), 2)
        diag_y = self.swap(cut(diag, 1), 4)
        y_first = (up(cut(by_y, 0)) + up(diag_x)).astype(BF)
        x_second = (up(cut(by_x, 1)) + up(diag_y)).astype(BF)
        by_y = jnp.concatenate([y_first, cut(by_y, 1)], axis=axis)
        by_x = jnp.concatenate([cut(by_x, 0), x_second], axis=axis)
        total = up(own) + up(self.swap(by_x, 2)) + up(self.swap(by_y, 4))
        total = total.astype(BF)
        bit = 8
        while bit < self.size:
            total = (up(total) + up(self.swap(total, bit))).astype(BF)
            bit *= 2
        return total


def forward_kernel(q_ref, k_ref, v_ref, bias_ref, out_ref, lse_ref):
    scale = HEAD**-0.5
    rows = q_ref.shape[0]
    lane = lax.broadcasted_iota(jnp.int32, (1, 2 * HEAD), 1)
    bias = bias_ref[...]
    sub = 256
    for at in range(rows // sub):
        span = pl.ds(at * sub, sub)
        q = q_ref[span, :]
        outs, lses = [], []
        for head in range(2):
            mine = (lane < HEAD) == (head == 0)
            k = jnp.where(mine, k_ref[...], jnp.zeros((), BF))
            v = jnp.where(mine, v_ref[...], jnp.zeros((), BF))
            s = lax.dot_general(q, k, NT, preferred_element_type=F32)
            s = s * scale + bias
            top = jnp.max(s, axis=1, keepdims=True)
            p = jnp.exp(s - top)
            total = jnp.sum(p, axis=1, keepdims=True)
            o = lax.dot_general(p.astype(BF), v, NN, preferred_element_type=F32)
            outs.append(o / total)
            lses.append(top + jnp.log(total))
        out_ref[span, :] = (outs[0] + outs[1]).astype(BF)
        wide = jnp.where(lane < HEAD, lses[0], lses[1])
        flat = jnp.transpose(wide)
        lse_ref[0, :, span] = jnp.concatenate(
            [flat[0:1], flat[HEAD : HEAD + 1]], axis=0
        )


def attention_forward(q, kv, bias):
    rows, width = q.shape
    keys = kv.shape[0]
    pairs = width // (2 * HEAD)
    wide = 2 * HEAD
    return pl.pallas_call(
        forward_kernel,
        grid=(pairs,),
        in_specs=[
            pl.BlockSpec((rows, wide), lambda h: (0, h)),
            pl.BlockSpec((keys, wide), lambda h: (0, h)),
            pl.BlockSpec((keys, wide), lambda h: (0, h + pairs)),
            pl.BlockSpec((1, keys), lambda h: (0, 0)),
        ],
        out_specs=[
            pl.BlockSpec((rows, wide), lambda h: (0, h)),
            pl.BlockSpec((1, 2, rows), lambda h: (h, 0, 0)),
        ],
        out_shape=[
            jax.ShapeDtypeStruct((rows, width), BF),
            jax.ShapeDtypeStruct((pairs, 2, rows), F32),
        ],
        compiler_params=pltpu.CompilerParams(vmem_limit_bytes=48 * 2**20),
        cost_estimate=pl.CostEstimate(
            flops=16 * rows * keys * width, bytes_accessed=10 * keys * width, transcendentals=0
        ),
        name="attention_forward",
    )(q, kv, kv, bias)


def backward_kernel(
    q_ref, k_ref, v_ref, go_ref, lse_ref, inner_ref, bias_ref, gq_ref, gk_ref, gv_ref
):
    scale = HEAD**-0.5
    rows = q_ref.shape[0]
    keys = k_ref.shape[0]
    lane = lax.broadcasted_iota(jnp.int32, (1, 2 * HEAD), 1)
    q, go = q_ref[...], go_ref[...]
    sub = 512
    zero = jnp.zeros((), BF)
    total_q = jnp.zeros((rows, 2 * HEAD), F32)
    for at in range(keys // sub):
        span = pl.ds(at * sub, sub)
        bias = bias_ref[span, 0:1]
        total_k = jnp.zeros((sub, 2 * HEAD), F32)
        total_v = jnp.zeros((sub, 2 * HEAD), F32)
        for head in range(2):
            mine = (lane < HEAD) == (head == 0)
            k = jnp.where(mine, k_ref[span, :], zero)
            v = jnp.where(mine, v_ref[span, :], zero)
            s = lax.dot_general(k, q, NT, preferred_element_type=F32)
            p = jnp.exp(s * scale + (bias - lse_ref[0, head : head + 1, :]))
            gp = lax.dot_general(v, go, NT, preferred_element_type=F32)
            gs = (p * (gp - inner_ref[0, head : head + 1, :])).astype(BF)
            total_v += lax.dot_general(
                p.astype(BF), jnp.where(mine, go, zero), NN, preferred_element_type=F32
            )
            total_k += lax.dot_general(
                gs, jnp.where(mine, q, zero), NN, preferred_element_type=F32
            )
            total_q += lax.dot_general(gs, k, TN, preferred_element_type=F32)
        gk_ref[span, :] = (total_k * scale).astype(BF)
        gv_ref[span, :] = total_v.astype(BF)
    gq_ref[...] = (total_q * scale).astype(BF)


def attention_backward(q, kv, go, lse, inner, bias):
    rows, width = q.shape
    keys = kv.shape[0]
    pairs = width // (2 * HEAD)
    wide = 2 * HEAD
    return pl.pallas_call(
        backward_kernel,
        grid=(pairs,),
        in_specs=[
            pl.BlockSpec((rows, wide), lambda h: (0, h)),
            pl.BlockSpec((keys, wide), lambda h: (0, h)),
            pl.BlockSpec((keys, wide), lambda h: (0, h + pairs)),
            pl.BlockSpec((rows, wide), lambda h: (0, h)),
            pl.BlockSpec((1, 2, rows), lambda h: (h, 0, 0)),
            pl.BlockSpec((1, 2, rows), lambda h: (h, 0, 0)),
            pl.BlockSpec((keys, 128), lambda h: (0, 0)),
        ],
        out_specs=[
            pl.BlockSpec((rows, wide), lambda h: (0, h)),
            pl.BlockSpec((keys, wide), lambda h: (0, h)),
            pl.BlockSpec((keys, wide), lambda h: (0, h)),
        ],
        out_shape=[
            jax.ShapeDtypeStruct((rows, width), BF),
            jax.ShapeDtypeStruct((keys, width), BF),
            jax.ShapeDtypeStruct((keys, width), BF),
        ],
        compiler_params=pltpu.CompilerParams(vmem_limit_bytes=48 * 2**20),
        cost_estimate=pl.CostEstimate(
            flops=40 * rows * keys * width, bytes_accessed=14 * keys * width, transcendentals=0
        ),
        name="attention_backward",
    )(q, kv, kv, go, lse, inner, bias)


def centred(values):
    centre = values - jnp.mean(values, axis=-1, keepdims=True)
    root = lax.rsqrt(jnp.mean(centre * centre, axis=-1, keepdims=True) + LN_EPS)
    return centre * root, root


def norm_pull(grad, gain, unit, root):
    scaled = grad * gain
    mean = jnp.mean(scaled, axis=-1, keepdims=True)
    slope = jnp.mean(scaled * unit, axis=-1, keepdims=True)
    return root * (scaled - mean - unit * slope), jnp.sum(grad * unit, axis=0)


def gelu_pair(values):
    cdf = 0.5 * lax.erfc(values * -(0.5**0.5))
    pdf = jnp.exp(-0.5 * values * values) * 0.3989422804014327
    return (values * cdf).astype(BF), (cdf + values * pdf).astype(BF)


def per_device(
    seq_size, tokens, w_qkv, w_out, w_up, w_down, gain_one, gain_two, cotangent, bucket, lengths
):
    rows, width = tokens.shape
    t = lax.axis_index("tp")
    s8 = lax.axis_index("seq") % 8
    middle = (t == 1) | (t == 2)
    plane = Plane(seq_size)
    hid = w_out.shape[0]
    ff = w_down.shape[0]
    qp, fp = hid // 8, ff // 8

    attn_own = jnp.stack([w_qkv[:, 0].T, w_qkv[:, 1].T, w_qkv[:, 2].T, w_out])
    ff_own = jnp.stack([w_up.T, w_down])

    def piece(stacked, size):
        kinds = stacked.shape[0]
        part = lax.dynamic_slice_in_dim(stacked, s8 * size, size, axis=1)
        return part.reshape(kinds * size, width)

    attn_blocks = line_gather(piece(attn_own, qp), middle)
    token_blocks = line_gather(tokens, middle)
    ff_blocks = line_gather(piece(ff_own, fp), middle)

    attn_far = plane.gather(jnp.concatenate(attn_blocks[1:]))
    ff_far = plane.gather(jnp.concatenate(ff_blocks[1:]))
    attn_far = jnp.stack([a.reshape(3, 4, qp, width) for a in attn_far])
    attn_far = attn_far.reshape(4, 2, 3, 4, qp, width).transpose(3, 0, 2, 1, 4, 5)
    w_attn = jnp.concatenate([attn_own, attn_far.reshape(4, 3 * hid, width)], axis=1)
    ff_far = jnp.stack([a.reshape(3, 2, fp, width) for a in ff_far])
    ff_far = ff_far.transpose(2, 0, 1, 3, 4).reshape(2, 3 * ff, width)
    w_ff = jnp.concatenate([ff_own, ff_far], axis=1)
    wq, wkv, wo = w_attn[0], w_attn[1:3].reshape(2 * width, width), w_attn[3]
    wu, wd = w_ff[0], w_ff[1]

    whole = bucket[0] == 1
    place = jnp.arange(rows, dtype=jnp.int32)
    limits = []
    for j in range(4):
        block = t ^ j
        alone = lengths[0, block] if j == 0 else 0
        limits.append(jnp.where(whole, lengths[0, 0] - block * rows, alone))
    seen = jnp.concatenate([place < limit for limit in limits])
    bias = jnp.where(seen, 0.0, -1e9).astype(F32)
    bias_cols = jnp.broadcast_to(bias[:, None], (4 * rows, 128))

    gathered = jnp.concatenate(token_blocks)
    q = mm(tokens, wq, NT, BF)
    kv = mm(gathered, wkv, NT, BF)
    attended, lse = attention_forward(q, kv, bias[None])
    first_sum = tokens.astype(F32) + mm(attended, wo, NN)
    unit_one, root_one = centred(first_sum)
    normed = unit_one * gain_one
    normed_low = normed.astype(BF)
    activated, slope = gelu_pair(mm(normed_low, wu, NT))
    unit_two, root_two = centred(normed + mm(activated, wd, NN))
    mixed = (unit_two * gain_two).astype(BF)

    grad_second, gain_grad_two = norm_pull(cotangent.astype(F32), gain_two, unit_two, root_two)
    grad_second_low = grad_second.astype(BF)
    grad_down = mm(activated, grad_second_low, TN, BF)
    grad_expanded = (mm(grad_second_low, wd, NT) * slope.astype(F32)).astype(BF)
    grad_up = mm(grad_expanded, normed_low, TN, BF)

    def reduced(grads, kinds, size, split):
        own = grads[:, : 8 * size].reshape(kinds, 8, size, width)
        own = jnp.stack(
            [lax.dynamic_index_in_dim(own, s8 ^ i, axis=1, keepdims=False) for i in range(8)]
        )
        if split:
            far = grads[:, 8 * size :].reshape(kinds, 4, 3, 2, size, width)
            far = far.transpose(1, 3, 2, 0, 4, 5).reshape(8, 3, kinds, size, width)
        else:
            far = grads[:, 8 * size :].reshape(kinds, 8, 3, size, width)
            far = far.transpose(1, 2, 0, 3, 4)
        pieces = jnp.concatenate([own[:, None], far], axis=1)
        pieces = pieces.reshape(8, 4, kinds * size, width)
        mine = plane.reduce([pieces[i] for i in range(8)])
        total = line_scatter([mine[j] for j in range(4)]).astype(BF)
        all_eight = jnp.stack(plane.gather(total))
        ordered = jnp.stack(
            [lax.dynamic_index_in_dim(all_eight, s8 ^ i, keepdims=False) for i in range(8)]
        )
        ordered = ordered.reshape(8, kinds, size, width).transpose(1, 0, 2, 3)
        return ordered.reshape(kinds, 8 * size, width)

    ff_sum = reduced(jnp.stack([grad_up, grad_down]), 2, fp, False)

    grad_normed = grad_second + mm(grad_expanded, wu, NN)
    grad_first, gain_grad_one = norm_pull(grad_normed, gain_one, unit_one, root_one)
    grad_first_low = grad_first.astype(BF)
    grad_out = mm(attended, grad_first_low, TN, BF)
    go = mm(grad_first_low, wo, NT, BF)
    inner = (go.astype(F32) * attended.astype(F32)).reshape(rows, width // HEAD, HEAD).sum(-1)
    inner = inner.T.reshape(width // (2 * HEAD), 2, rows)
    gq, gk, gv = attention_backward(q, kv, go, lse, inner, bias_cols)
    wk, wv = w_attn[1], w_attn[2]
    parts = []
    for j in range(4):
        span = slice(j * rows, (j + 1) * rows)
        part = mm(gk[span], wk, NN) + mm(gv[span], wv, NN)
        if j == 0:
            part = part + mm(gq, wq, NN) + grad_first
        parts.append(part if j == 0 else part.astype(BF))
    tokens_grad = line_scatter(parts).astype(BF)
    grad_q = mm(gq, tokens, TN, BF)
    grad_k = mm(gk, gathered, TN, BF)
    grad_v = mm(gv, gathered, TN, BF)
    attn_sum = reduced(jnp.stack([grad_q, grad_k, grad_v, grad_out]), 4, qp, True)

    gains = jnp.stack([gain_grad_one, gain_grad_two])
    bit = 1
    while bit < seq_size:
        gains = gains + plane.swap(gains, bit)
        bit *= 2
    gains = gains + along(gains, [(i, i ^ 1) for i in range(4)])
    gains = gains + along(gains, [(i, i ^ 2) for i in range(4)])

    attn_sum, ff_sum = attn_sum.astype(F32), ff_sum.astype(F32)
    return (
        mixed,
        tokens_grad,
        attn_sum[:3].transpose(2, 0, 1),
        attn_sum[3],
        ff_sum[0].T,
        ff_sum[1],
        gains[0],
        gains[1],
    )


def solution(mesh):
    rows = P(("seq", "tp"), None)
    weights = (P(None, None, "tp"), P("tp", None), P(None, "tp"), P("tp", None), P(), P())
    return jax.shard_map(
        functools.partial(per_device, mesh.shape["seq"]),
        mesh=mesh,
        in_specs=(rows,) + weights + (rows, P("seq"), P("seq", None)),
        out_specs=(rows, rows) + weights,
        check_vma=False,
    )
```

```python
import functools

import jax
import jax.numpy as jnp
from jax import lax
from jax.experimental import pallas as pl
from jax.experimental.pallas import tpu as pltpu
from jax.sharding import PartitionSpec as P

HEAD = 64
SLOTS = 4
BF = jnp.bfloat16
F32 = jnp.float32
LOG2E = 1.4426950408889634
LN_EPS = 1e-5
LIGHT = pl.CostEstimate(flops=10**9, bytes_accessed=10**6, transcendentals=0)
NT = (((1,), (1,)), ((), ()))
NN = (((1,), (0,)), ((), ()))
TN = (((0,), (0,)), ((), ()))

PAIR = [(0, 1), (1, 0), (2, 3), (3, 2)]
MIDDLE = [(1, 2), (2, 1)]
OUTWARD = [(1, 0), (2, 3)]


def mm(a, b, dims, out=F32):
    return lax.dot_general(a, b, dims, preferred_element_type=F32).astype(out)


def along(array, pairs):
    return lax.ppermute(array, "tp", pairs)


def fence(*arrays):
    return lax.optimization_barrier(arrays)


class Plane:
    def __init__(self, size):
        self.size = size

    def swap(self, array, bit):
        return lax.ppermute(array, "seq", [(i, i ^ bit) for i in range(self.size)])

    def higher(self, total):
        bit = 8
        while bit < self.size:
            total = (total.astype(F32) + self.swap(total, bit).astype(F32)).astype(BF)
            bit *= 2
        return total


def forward_kernel(q_ref, *refs):
    blocks = (len(refs) - 5) // 2
    k_refs, v_refs = refs[:blocks], refs[blocks : 2 * blocks]
    bias_ref, out_ref, lse_ref = refs[2 * blocks], refs[-2], refs[-1]
    scale = HEAD**-0.5 * LOG2E
    rows = q_ref.shape[0]
    lane = lax.broadcasted_iota(jnp.int32, (1, 2 * HEAD), 1)
    zero = jnp.zeros((), BF)
    keys = jnp.concatenate([ref[...] for ref in k_refs])
    values = jnp.concatenate([ref[...] for ref in v_refs])
    bias = bias_ref[...]
    sub = 256
    mine = [(lane < HEAD) == (head == 0) for head in range(2)]
    k = [jnp.where(m, keys, zero) for m in mine]
    v = [jnp.where(m, values, zero) for m in mine]
    for at in range(rows // sub):
        span = pl.ds(at * sub, sub)
        q = q_ref[span, :]
        outs, lses = [], []
        for head in range(2):
            s = lax.dot_general(q, k[head], NT, preferred_element_type=F32)
            s = s * scale + bias
            top = jnp.max(s, axis=1, keepdims=True)
            p = jnp.exp2(s - top)
            total = jnp.sum(p, axis=1, keepdims=True)
            o = lax.dot_general(p.astype(BF), v[head], NN, preferred_element_type=F32)
            outs.append(o / total)
            lses.append(top + jnp.log2(total))
        out_ref[span, :] = (outs[0] + outs[1]).astype(BF)
        wide = jnp.where(lane < HEAD, lses[0], lses[1])
        flat = jnp.transpose(wide)
        lse_ref[0, :, span] = jnp.concatenate(
            [flat[0:1], flat[HEAD : HEAD + 1]], axis=0
        )


def attention_forward(q, kvs, bias, first, count, held):
    rows, width = q.shape
    keys = bias.shape[1]
    pairs = width // (2 * HEAD)
    wide = 2 * HEAD
    at = lambda shift: lambda h: (0, h + first + shift)
    return pl.pallas_call(
        forward_kernel,
        grid=(count,),
        in_specs=[pl.BlockSpec((rows, wide), at(0))]
        + [pl.BlockSpec((kv.shape[0], wide), at(0)) for kv in kvs]
        + [pl.BlockSpec((kv.shape[0], wide), at(pairs)) for kv in kvs]
        + [pl.BlockSpec((1, keys), lambda h: (0, 0))]
        + [pl.BlockSpec(memory_space=pl.ANY)] * 2,
        out_specs=[
            pl.BlockSpec((rows, wide), at(0)),
            pl.BlockSpec((1, 2, rows), lambda h: (h + first, 0, 0)),
        ],
        out_shape=[
            jax.ShapeDtypeStruct((rows, width), BF),
            jax.ShapeDtypeStruct((pairs, 2, rows), F32),
        ],
        input_output_aliases={2 * len(kvs) + 2: 0, 2 * len(kvs) + 3: 1},
        compiler_params=pltpu.CompilerParams(vmem_limit_bytes=48 * 2**20),
        cost_estimate=LIGHT,
        name="attention_forward",
    )(q, *kvs, *kvs, bias, *held)


def backward_kernel(
    q_ref, k_ref, v_ref, go_ref, lse_ref, inner_ref, bias_ref, wkv_ref, *refs
):
    add_ref = refs[0] if len(refs) == 9 else None
    gq_ref, keep_k_ref, keep_v_ref, send_ref, part_ref, all_ref = refs[-6:]
    step, pairs = pl.program_id(0), pl.num_programs(0)
    scale = HEAD**-0.5
    wide = 2 * HEAD
    keys = k_ref.shape[0]
    lane = lax.broadcasted_iota(jnp.int32, (1, wide), 1)
    q, go = q_ref[...], go_ref[...]
    zero = jnp.zeros((), BF)
    mine = [(lane < HEAD) == (head == 0) for head in range(2)]
    qs = [jnp.where(m, q, zero) for m in mine]
    gos = [jnp.where(m, go, zero) for m in mine]
    total_q = [0.0, 0.0]
    gks, gvs = [], []
    sub = 512
    for at in range(keys // sub):
        span = pl.ds(at * sub, sub)
        bias = bias_ref[span, 0:1]
        keys_t = k_ref[span, :].T
        total_k, total_v = 0.0, 0.0
        for head in range(2):
            k = jnp.where(mine[head], k_ref[span, :], zero)
            v = jnp.where(mine[head], v_ref[span, :], zero)
            s = lax.dot_general(k, q, NT, preferred_element_type=F32)
            p = jnp.exp2(s * (scale * LOG2E) + (bias - lse_ref[0, head : head + 1, :]))
            gp = lax.dot_general(v, go, NT, preferred_element_type=F32)
            gs = (p * (gp - inner_ref[0, head : head + 1, :])).astype(BF)
            total_v += lax.dot_general(p.astype(BF), gos[head], NN, preferred_element_type=F32)
            total_k += lax.dot_general(gs, qs[head], NN, preferred_element_type=F32)
            own_keys = keys_t[head * HEAD : (head + 1) * HEAD]
            total_q[head] += lax.dot_general(own_keys, gs, NN, preferred_element_type=F32)
        gks.append((total_k * scale).astype(BF))
        gvs.append(total_v.astype(BF))
    gk, gv = jnp.concatenate(gks), jnp.concatenate(gvs)
    gq = jnp.concatenate(total_q).T * scale
    gq_ref[...] = gq if add_ref is None else gq + add_ref[...]
    half = pairs // 2

    @pl.when(step < half)
    def _():
        keep_k_ref[...] = gk
        keep_v_ref[...] = gv

    @pl.when(step >= half)
    def _():
        send_ref[0] = gk
        send_ref[1] = gv

    lanes = pl.multiple_of(step * wide, wide)
    all_ref[:, pl.ds(lanes, wide)] = gk
    all_ref[:, pl.ds(pl.multiple_of(lanes + q_width(part_ref), wide), wide)] = gv

    @pl.when(step == pairs - 1)
    def _():
        for at in range(keys // 256):
            span = pl.ds(at * 256, 256)
            part = lax.dot_general(
                all_ref[span, :], wkv_ref[...], NN, preferred_element_type=F32
            )
            part_ref[span, :] = part.astype(BF)


def q_width(part_ref):
    return part_ref.shape[1]


def attention_backward(q, kv, go, lse, inner, bias, wkv, block, blocks, held):
    rows, width = q.shape
    keys = kv.shape[0]
    pairs = width // (2 * HEAD)
    wide = 2 * HEAD
    half = pairs // 2
    by_pair = pl.BlockSpec((rows, wide), lambda h: (0, h))
    stats = pl.BlockSpec((1, 2, rows), lambda h: (h, 0, 0))
    whole = pl.BlockSpec(memory_space=pl.ANY)
    keep = pl.BlockSpec((keys, wide), lambda h: (block, jnp.minimum(h, half - 1)))
    send = pl.BlockSpec((2, keys, wide), lambda h: (0, 0, jnp.maximum(h - half, 0)))
    return pl.pallas_call(
        backward_kernel,
        grid=(pairs,),
        in_specs=[
            by_pair,
            pl.BlockSpec((keys, wide), lambda h: (0, h)),
            pl.BlockSpec((keys, wide), lambda h: (0, h + pairs)),
            by_pair,
            stats,
            stats,
            pl.BlockSpec((keys, 128), lambda h: (0, 0)),
            pl.BlockSpec((2 * width, width), lambda h: (0, 0)),
        ]
        + ([by_pair, whole, whole] if held else []),
        out_specs=[by_pair, keep, keep, send, pl.BlockSpec((keys, width), lambda h: (0, 0))],
        out_shape=[
            jax.ShapeDtypeStruct((rows, width), F32),
            jax.ShapeDtypeStruct((blocks * keys, width // 2), BF),
            jax.ShapeDtypeStruct((blocks * keys, width // 2), BF),
            jax.ShapeDtypeStruct((2, keys, width // 2), BF),
            jax.ShapeDtypeStruct((keys, width), BF),
        ],
        scratch_shapes=[pltpu.VMEM((keys, 2 * width), BF)],
        input_output_aliases={9: 1, 10: 2} if held else {},
        compiler_params=pltpu.CompilerParams(vmem_limit_bytes=48 * 2**20),
        cost_estimate=LIGHT,
        name="attention_backward",
    )(q, kv, kv, go, lse, inner, bias, wkv, *(held or ()))


def gelu_tile(x):
    size = jnp.abs(x)
    t = 1.0 / (1.0 + size * (0.3275911 * 0.5**0.5))
    poly = t * (
        0.127414796
        + t * (-0.142248368 + t * (0.7107068705 + t * (-0.7265760135 + t * 0.5307027145)))
    )
    bell = jnp.exp2(x * x * (-0.5 * LOG2E))
    tail = poly * bell
    cdf = jnp.where(x >= 0, 1.0 - tail, tail)
    return (x * cdf).astype(BF), (cdf + x * (bell * 0.3989422804014327)).astype(BF)


def head_grads_kernel(
    first, big_ref, came_ref, came_two_ref, small_ref, small_peer_ref,
    rows_ref, rows_two_ref, peer_ref, peer_two_ref, right_ref, right_peer_ref, *out_refs
):
    def outer(left, right):
        return lax.dot_general(left, right[...], TN, preferred_element_type=F32)

    keys = rows_ref.shape[0]
    total = outer(big_ref[:keys, :], rows_ref) + outer(big_ref[keys:, :], rows_two_ref)
    total += outer(came_ref[0], peer_ref) + outer(came_two_ref[0], peer_two_ref)
    total = total.astype(BF)
    other = outer(small_ref[...], right_ref) + outer(small_peer_ref[...], right_peer_ref)
    kinds = [total, other.astype(BF)] if first else [other.astype(BF), total]
    size = HEAD // 2
    for at in range(total.shape[0] // (4 * size)):
        for kind in range(2):
            for chunk in range(4):
                source = (at * 4 + (chunk & 1) * 2 + (chunk >> 1)) * size
                place = (at * 2 + kind) * size
                out_refs[chunk][place : place + size, :] = kinds[kind][source : source + size, :]


def head_grads(first, big, came, small, small_peer, rows, peer, right, right_peer):
    keys, width = rows[0].shape
    own = right.shape[0]
    core = width // 2
    wide = core // 2
    which = 1 if first else 0
    whole = lambda a: pl.BlockSpec(a.shape, lambda g: (0, 0))
    columns = lambda n: pl.BlockSpec((n, wide), lambda g: (0, g))
    arrived = pl.BlockSpec((1, keys, wide), lambda g: (which, 0, g))
    return pl.pallas_call(
        functools.partial(head_grads_kernel, first),
        grid=(core // wide,),
        in_specs=[columns(2 * keys), arrived, arrived, columns(own), columns(own)]
        + [whole(a) for a in (*rows, *peer, right, right_peer)],
        out_specs=[pl.BlockSpec((wide // 2, width), lambda g: (g, 0))] * 4,
        out_shape=[jax.ShapeDtypeStruct((core // 2, width), BF)] * 4,
        compiler_params=pltpu.CompilerParams(vmem_limit_bytes=48 * 2**20),
        cost_estimate=LIGHT,
        name="head_grads",
    )(big, *came, small, small_peer, *rows, *peer, right, right_peer)


def rows_kernel(moves, n_held, n_out, *refs):
    n_in = len(refs) - n_held - n_out - 1
    ins, outs, sems = refs[:n_in], refs[-1 - n_out : -1], refs[-1]
    copies = []
    for n, (source, at, count, out, place) in enumerate(moves):
        copies.append(
            pltpu.make_async_copy(
                ins[source].at[pl.ds(at, count), :],
                outs[out].at[pl.ds(place, count), :],
                sems.at[n],
            )
        )
    for copy in copies:
        copy.start()
    for copy in copies:
        copy.wait()


def put_rows(moves, shape, n_out, held=()):
    arrays, listed = [], []
    for array, at, count, out, place in moves:
        known = [n for n, a in enumerate(arrays) if a is array]
        if not known:
            arrays.append(array)
        listed.append((known[0] if known else len(arrays) - 1, at, count, out, place))
    whole = pl.BlockSpec(memory_space=pl.ANY)
    return pl.pallas_call(
        functools.partial(rows_kernel, listed, len(held), n_out),
        in_specs=[pl.BlockSpec(memory_space=pltpu.VMEM)] * len(arrays) + [whole] * len(held),
        out_specs=[whole] * n_out,
        out_shape=[jax.ShapeDtypeStruct(shape, BF)] * n_out,
        scratch_shapes=[pltpu.SemaphoreType.DMA((len(listed),))],
        input_output_aliases={len(arrays) + n: n for n in range(len(held))},
        compiler_params=pltpu.CompilerParams(vmem_limit_bytes=32 * 2**20),
        cost_estimate=LIGHT,
        name="put_rows",
    )(*arrays, *held)


def totals_kernel(at_ref, *refs):
    *ins, out_ref = refs
    size = ins[0].shape[0]
    for n in range(2):
        a, b, c = [ref[...].astype(F32) for ref in ins[3 * n : 3 * n + 3]]
        out_ref[n * size : (n + 1) * size, :] = (a + b + c).astype(BF)


def totals(ones, twos, t):
    rows, width = ones[0].shape
    size = rows // 4
    return pl.pallas_call(
        totals_kernel,
        grid_spec=pltpu.PrefetchScalarGridSpec(
            num_scalar_prefetch=1,
            grid=(4,),
            in_specs=[pl.BlockSpec((size, width), lambda u, at: (at[0] ^ u, 0))] * 6,
            out_specs=pl.BlockSpec((2 * size, width), lambda u, at: (u, 0)),
        ),
        out_shape=jax.ShapeDtypeStruct((2 * rows, width), BF),
        cost_estimate=LIGHT,
        name="totals",
    )(t[None].astype(jnp.int32), *ones, *twos)


def outer_kernel(left_ref, right_ref, left_two_ref, right_two_ref, *out_refs):
    total = lax.dot_general(left_ref[...], right_ref[...], TN, preferred_element_type=F32)
    total += lax.dot_general(
        left_two_ref[...], right_two_ref[...], TN, preferred_element_type=F32
    )
    total = total.astype(BF)
    each = pl.num_programs(0) // len(out_refs)
    for n, out_ref in enumerate(out_refs):

        @pl.when(pl.program_id(0) // each == n)
        def _():
            out_ref[...] = total


def outer_four(left, right, left_two, right_two):
    rows, hidden = left.shape
    width = right.shape[1]
    tile = 256
    each = hidden // (4 * tile)
    columns = pl.BlockSpec((rows, tile), lambda i: (0, i))
    whole = pl.BlockSpec((rows, width), lambda i: (0, 0))
    place = lambda n: lambda i: (jnp.clip(i - n * each, 0, each - 1), 0)
    return pl.pallas_call(
        outer_kernel,
        grid=(hidden // tile,),
        in_specs=[columns, whole, columns, whole],
        out_specs=[pl.BlockSpec((tile, width), place(n)) for n in range(4)],
        out_shape=[jax.ShapeDtypeStruct((hidden // 4, width), BF)] * 4,
        compiler_params=pltpu.CompilerParams(vmem_limit_bytes=32 * 2**20),
        cost_estimate=LIGHT,
        name="outer_four",
    )(left, right, left_two, right_two)


def reverse(i):
    return ((i & 1) << 2) | (i & 2) | (i >> 2)


def placed_kernel(flips, order, at_ref, *refs):
    *pieces, out_ref, whole_ref = refs
    for i, piece in enumerate(pieces):
        place = order(at_ref[0] ^ i)
        size = piece.shape[0]
        whole_ref[pl.ds(pl.multiple_of(place * size, size), size), :] = piece[...].astype(F32)
    out = whole_ref[...]
    out = out.T if flips else out
    out_ref[...] = out.reshape(out_ref.shape)


def placed(pieces, kinds, size, order, s8, flips):
    width = pieces[0][0].shape[1]
    tile = 256
    rows = 8 * size
    if kinds > 1:
        out_shape = (kinds, width, rows)
        out_spec = pl.BlockSpec((1, tile, rows), lambda n, c: (n, c, 0))
    elif flips:
        out_shape, out_spec = (width, rows), pl.BlockSpec((tile, rows), lambda n, c: (c, 0))
    else:
        out_shape, out_spec = (rows, width), pl.BlockSpec((rows, tile), lambda n, c: (0, c))
    part = lambda first: pl.BlockSpec((size, tile), lambda n, c: (n + first, c))
    return pl.pallas_call(
        functools.partial(placed_kernel, flips, order),
        grid=(kinds, width // tile),
        in_specs=[pl.BlockSpec(memory_space=pltpu.SMEM)] + [part(first) for _, first in pieces],
        out_specs=out_spec,
        out_shape=jax.ShapeDtypeStruct(out_shape, F32),
        scratch_shapes=[pltpu.VMEM((rows, tile), F32)],
        compiler_params=pltpu.CompilerParams(vmem_limit_bytes=32 * 2**20),
        name="placed",
    )(s8[None].astype(jnp.int32), *[array for array, _ in pieces])


def centred(values):
    centre = values - jnp.mean(values, axis=-1, keepdims=True)
    root = lax.rsqrt(jnp.mean(centre * centre, axis=-1, keepdims=True) + LN_EPS)
    return centre * root, root


def norm_pull(grad, gain, unit, root):
    scaled = grad * gain
    mean = jnp.mean(scaled, axis=-1, keepdims=True)
    slope = jnp.mean(scaled * unit, axis=-1, keepdims=True)
    return root * (scaled - mean - unit * slope), jnp.sum(grad * unit, axis=0)


def per_device(
    seq_size, tokens, w_qkv, w_out, w_up, w_down, gain_one, gain_two, cotangent, bucket, lengths
):
    rows, width = tokens.shape
    t = lax.axis_index("tp")
    middle = (t == 1) | (t == 2)
    s8 = lax.axis_index("seq") % 8
    plane = Plane(seq_size)
    swap = plane.swap
    hid = w_out.shape[0]
    ff = w_down.shape[0]
    qp, fp = hid // 8, ff // 8
    up = lambda a: a.astype(F32)
    across = lambda a, j: along(a, [(i, i ^ j) for i in range(4)])

    w_attn_own = jnp.concatenate([w_qkv.transpose(1, 2, 0), w_out[None]])

    def attn_piece(i):
        return lax.dynamic_slice_in_dim(w_attn_own, reverse(s8 ^ i) * qp, qp, axis=1)

    def up_piece(i):
        return lax.dynamic_slice_in_dim(w_up, (s8 ^ i) * fp, fp, axis=1).T

    def down_piece(i):
        return lax.dynamic_slice_in_dim(w_down, (s8 ^ i) * fp, fp, axis=0)

    attn_own = attn_piece(0).reshape(4 * qp, width)
    up_own = jnp.concatenate([up_piece(2 * i) for i in range(4)])
    down_own = jnp.concatenate([down_piece(2 * i) for i in range(4)])
    ff_own = jnp.concatenate([up_own[:fp], down_own[:fp]])

    upper = rows // 2
    gathered = [
        lax.all_gather(tokens[n * upper : (n + 1) * upper], "tp", axis=0, tiled=True)
        for n in range(2)
    ]
    a_far = [across(attn_own, j) for j in (1, 2, 3)]
    a_far = fence(*a_far)
    attn_three = jnp.concatenate(a_far)
    half = attn_three.shape[0] // 2
    a_x, a_y = swap(attn_three, 2), swap(attn_three, 4)
    attn_three, a_x, a_y = fence(attn_three, a_x, a_y)
    a_d1, a_d2 = swap(a_y[:half], 2), swap(a_x[half:], 4)
    others = [swap(attn_three, 1), swap(a_x, 1), swap(a_y, 1)]
    a_d1, a_d2, *others = fence(a_d1, a_d2, *others)
    others += fence(swap(a_d1, 1), swap(a_d2, 1))

    four = [attn_three, a_x, a_y, a_d1, a_d2]
    pieces = []
    for i in range(8):
        part = others if i & 1 else four
        far = part[i >> 1] if i < 6 else jnp.concatenate(part[3:])
        pieces.append(jnp.concatenate([attn_piece(i)[None], far.reshape(3, 4, qp, width)]))
    w_attn = jnp.stack(pieces).reshape(2, 2, 2, 4, 4, qp, width).transpose(4, 2, 3, 1, 0, 5, 6)
    w_attn = w_attn.reshape(4, width, width)
    wq, wk, wv, wo = [w_attn[n] for n in range(4)]
    wkv = w_attn[1:3].reshape(2 * width, width)

    whole = bucket[0] == 1
    place = jnp.arange(rows, dtype=jnp.int32)
    seen = []
    for u in range(4):
        alone = jnp.where(t == u, lengths[0, u], 0)
        limit = jnp.where(whole, lengths[0, 0] - u * rows, alone)
        seen.append((place < limit).reshape(2, upper))
    bias = jnp.where(jnp.stack(seen, axis=1), 0.0, -1e9).astype(F32).reshape(4 * rows)
    bias_cols = jnp.broadcast_to(bias[:, None], (4 * rows, 128))

    q = mm(tokens, wq, NT, BF)
    tokens_peer = swap(tokens, 1)
    upper_kv = mm(gathered[0], wkv, NT, BF)
    upper_kv, q, tokens_peer, ff_own, up_own, down_own, *gathered = fence(
        upper_kv, q, tokens_peer, ff_own, up_own, down_own, *gathered
    )
    f_one, f_far = along(ff_own, PAIR), along(ff_own, MIDDLE)
    kvs = fence(upper_kv, mm(gathered[1], wkv, NT, BF))
    held = (jnp.zeros((rows, width), BF), jnp.zeros((width // (2 * HEAD), 2, rows), F32))
    bias_row = bias[None]
    held = attention_forward(q, kvs, bias_row, 0, 2, held)
    f_one, f_far, *held = fence(f_one, f_far, *held)
    f_two, f_two_end = along(f_one, MIDDLE), along(f_far, OUTWARD)
    one_x, one_y = swap(f_one, 2), swap(f_one, 4)
    held = attention_forward(q, kvs, bias_row, 2, 2, held)
    f_two, f_two_end, one_x, one_y, *held = fence(f_two, f_two_end, one_x, one_y, *held)
    f_three_end = along(f_two, OUTWARD)
    f_two = jnp.where(middle, f_two, f_two_end)
    one_d1, one_d2 = swap(one_y[:fp], 2), swap(one_x[fp:], 4)
    two_x, two_y = swap(f_two, 2), swap(f_two, 4)
    held = attention_forward(q, kvs, bias_row, 4, 2, held)
    f_three_end, one_d1, one_d2, two_x, two_y, *held = fence(
        f_three_end, one_d1, one_d2, two_x, two_y, *held
    )
    f_three = jnp.where(middle, f_far, f_three_end)
    two_d1, two_d2 = swap(two_y[:fp], 2), swap(two_x[fp:], 4)
    three_x, three_y = swap(f_three, 2), swap(f_three, 4)

    def moves(j, block):
        own, by_x, by_y, d1, d2 = block
        for i, (a, b, at) in enumerate(((own,) * 2 + (fp,), (by_x,) * 2 + (fp,), (by_y,) * 2 + (fp,), (d1, d2, 0))):
            yield (a, 0, fp, 0, (4 * i + j) * fp)
            yield (b, at, fp, 1, (4 * i + j) * fp)

    own = []
    for i in range(4):
        own.append((up_own, i * fp, fp, 0, 4 * i * fp))
        own.append((down_own, i * fp, fp, 1, 4 * i * fp))
    one = moves(1, (f_one, one_x, one_y, one_d1, one_d2))
    w_ff = put_rows([*own, *one], (ff * 2, width), 2)
    w_ff = fence(*w_ff, *held)
    w_ff, held = w_ff[:2], w_ff[2:]
    held = attention_forward(q, kvs, bias_row, 6, 2, held)
    two_d1, two_d2, three_x, three_y, *held = fence(two_d1, two_d2, three_x, three_y, *held)
    three_d1, three_d2 = swap(three_y[:fp], 2), swap(three_x[fp:], 4)
    attended, lse = held
    first_sum = up(tokens) + mm(attended, wo, NN)
    unit_one, root_one = centred(first_sum)
    normed = unit_one * gain_one
    normed_low = normed.astype(BF)

    two = moves(2, (f_two, two_x, two_y, two_d1, two_d2))
    three = moves(3, (f_three, three_x, three_y, three_d1, three_d2))
    wu, wd = put_rows([*two, *three], (ff * 2, width), 2, w_ff)

    normed_peer = swap(normed_low, 1)
    gathered_peer = [swap(part, 1) for part in gathered]
    attended_peer = swap(attended[:, width // 2 :], 1)
    act, slope = gelu_tile(mm(normed_low, wu, NT))
    act_peer, slope_peer = gelu_tile(mm(normed_peer, wu, NT))
    shrunk_peer = swap(mm(act_peer, wd, NN, BF), 1)
    unit_two, root_two = centred(normed + mm(act, wd, NN) + up(shrunk_peer))
    mixed = (unit_two * gain_two).astype(BF)

    grad_second, gain_grad_two = norm_pull(up(cotangent), gain_two, unit_two, root_two)
    second_low = grad_second.astype(BF)
    second_peer = swap(second_low, 1)
    grad_exp = (mm(second_low, wd, NT) * up(slope)).astype(BF)
    grad_exp_peer = (mm(second_peer, wd, NT) * up(slope_peer)).astype(BF)
    normed_part_peer = swap(mm(grad_exp_peer, wu, NN, BF), 1)
    normed_part = mm(grad_exp, wu, NN)
    twos = outer_four(act, second_low, act_peer, second_peer)
    normed_part, normed_part_peer, *twos = fence(normed_part, normed_part_peer, *twos)
    diag_y, two_y = swap(twos[3], 4), swap(twos[2], 4)
    ones = outer_four(grad_exp, normed_low, grad_exp_peer, normed_peer)
    grad_normed = grad_second + normed_part + up(normed_part_peer)
    normed_part, *ones = fence(normed_part, *ones)
    diag_x, one_x = swap(ones[3], 2), swap(ones[1], 2)
    grad_first, gain_grad_one = norm_pull(grad_normed, gain_one, unit_one, root_one)
    first_low = grad_first.astype(BF)
    first_peer = swap(first_low, 1)
    go = mm(first_low, wo, NT, BF)
    inner = (up(go) * up(attended)).reshape(rows, width // HEAD, HEAD).sum(-1)
    inner = inner.T.reshape(width // (2 * HEAD), 2, rows)
    core = width // 2
    inner, go, first_peer, attended_peer, *gathered_peer = fence(
        inner, go, first_peer, attended_peer, *gathered_peer
    )

    def pull(n, held):
        keys = bias_cols[2 * n * rows : 2 * (n + 1) * rows]
        *held, send, part = attention_backward(
            q, kvs[n], go, lse, inner, keys, wkv, n, 2, held
        )
        return held, send, part

    def line_sum(part):
        return lax.psum_scatter(part, "tp", scatter_dimension=0, tiled=True)

    gains = jnp.stack([gain_grad_one, gain_grad_two])
    gains_came = swap(gains, 1)
    held, send, part = pull(0, None)
    diag_x, diag_y, one_x, two_y, send, part, gains_came, *held = fence(
        diag_x, diag_y, one_x, two_y, send, part, gains_came, *held
    )
    upper_sum = line_sum(part)
    came = [swap(send, 1)]
    gains = gains + gains_came
    gains_came = swap(gains, 2)
    two_x = (up(twos[1]) + up(diag_y)).astype(BF)
    one_y = (up(ones[2]) + up(diag_x)).astype(BF)
    two_x, one_y, *held = fence(two_x, one_y, *held)
    two_x, one_y = swap(two_x, 2), swap(one_y, 4)
    held, send, part = pull(1, held)
    two_x, one_y, came[0], send, part, gains_came, upper_sum, *held = fence(
        two_x, one_y, came[0], send, part, gains_came, upper_sum, *held
    )
    gq, gk, gv = held
    gq = gq.astype(BF)
    came.append(swap(send, 1))
    gq_peer = swap(gq[:, core:], 1)
    gains = gains + gains_came
    gains_came = swap(gains, 4)
    ff_total = line_sum(
        plane.higher(totals((ones[0], one_x, one_y), (twos[0], two_x, two_y), t))
    )
    first = mm(gq, wq, NN) + grad_first
    came[1], gq_peer, gains_came, first = fence(came[1], gq_peer, gains_came, first)
    gains = gains + gains_came
    gains_came = across(gains, 1)
    a_twos = fence(
        *head_grads(
            True, gv, came, attended, attended_peer, gathered, gathered_peer, first_low, first_peer
        )
    )
    a_diag_y, a_two_y = swap(a_twos[3], 4), swap(a_twos[2], 4)
    a_ones = head_grads(
        False, gk, came, gq, gq_peer, gathered, gathered_peer, tokens, tokens_peer
    )
    a_diag_y, gains_came, *a_ones = fence(a_diag_y, gains_came, *a_ones)
    gains = gains + gains_came
    gains_came = across(gains, 2)
    a_diag_x, a_one_x = swap(a_ones[3], 2), swap(a_ones[1], 2)
    a_two_x = (up(a_twos[1]) + up(a_diag_y)).astype(BF)
    a_two_x, a_diag_x, gains_came = fence(a_two_x, a_diag_x, gains_came)
    gains = gains + gains_came
    bit = 8
    while bit < seq_size:
        gains = gains + swap(gains, bit)
        bit *= 2
    a_two_x = swap(a_two_x, 2)
    a_one_y = swap((up(a_ones[2]) + up(a_diag_x)).astype(BF), 4)
    ff_total, part = fence(ff_total.astype(BF), part)
    lower_sum = line_sum(part)
    a_two_x, a_one_y, a_one_x, a_two_y = fence(a_two_x, a_one_y, a_one_x, a_two_y)
    vo_mine = plane.higher((up(a_twos[0]) + up(a_two_x) + up(a_two_y)).astype(BF))
    qk_mine = plane.higher((up(a_ones[0]) + up(a_one_x) + up(a_one_y)).astype(BF))
    qk_mine, vo_mine = qk_mine.reshape(4, 2 * qp, width), vo_mine.reshape(4, 2 * qp, width)
    a_mine = fence(*[jnp.concatenate([qk_mine[j], vo_mine[j]]) for j in range(4)])
    a_came = [across(a_mine[j], j) for j in (1, 2, 3)]
    f_x, f_y = swap(ff_total, 2), swap(ff_total, 4)
    f_core = [swap(ff_total, 1)]
    f_x, f_y, *f_core = fence(f_x, f_y, *f_core)
    f_d1, f_d2 = swap(f_y[:fp], 2), swap(f_x[fp:], 4)
    f_core += [swap(f_x, 1), swap(f_y, 1)]
    a_came = fence(*a_came)
    a_total = fence(sum((up(a) for a in a_came), up(a_mine[0])).astype(BF))[0]
    a_four = [a_total, swap(a_total, 2), swap(a_total, 4), swap(a_total, 6)]
    a_core = [swap(a_total, 1)]
    f_core += [swap(f_d1, 1), swap(f_d2, 1)]
    f_four = [ff_total, f_x, f_y, f_d1, f_d2]
    ups, downs = [], []
    for i in range(8):
        part = f_core if i & 1 else f_four
        ups.append((part[i >> 1], 0))
        downs.append((part[i >> 1], 1) if i < 6 else (part[4], 0))
    plain = lambda i: i
    grad_up = placed(ups, 1, fp, plain, s8, True)
    grad_down = placed(downs, 1, fp, plain, s8, False)
    grad_up, grad_down, *a_four = fence(grad_up, grad_down, *a_four)
    a_core += [swap(a, 1) for a in a_four[1:]]
    a_all = [(a_core if i & 1 else a_four)[i >> 1] for i in range(8)]
    grad_qkv = placed([(a, 0) for a in a_all], 3, qp, reverse, s8, True)
    grad_out = placed([(a, 3) for a in a_all], 1, qp, reverse, s8, False)

    tokens_grad = (first + up(jnp.concatenate([upper_sum, lower_sum]))).astype(BF)
    return (
        mixed,
        tokens_grad,
        grad_qkv.transpose(1, 0, 2),
        grad_out,
        grad_up,
        grad_down,
        gains[0],
        gains[1],
    )


def solution(mesh):
    rows = P(("seq", "tp"), None)
    weights = (P(None, None, "tp"), P("tp", None), P(None, "tp"), P("tp", None), P(), P())
    return jax.shard_map(
        functools.partial(per_device, mesh.shape["seq"]),
        mesh=mesh,
        in_specs=(rows,) + weights + (rows, P("seq"), P("seq", None)),
        out_specs=(rows, rows) + weights,
        check_vma=False,
    )
```

```python
import functools

import jax
import jax.numpy as jnp
from jax import lax
from jax.experimental import pallas as pl
from jax.experimental.pallas import tpu as pltpu
from jax.sharding import PartitionSpec as P

HEAD = 64
SLOTS = 4
BF = jnp.bfloat16
F32 = jnp.float32
LOG2E = 1.4426950408889634
LN_EPS = 1e-5
LIGHT = pl.CostEstimate(flops=10**9, bytes_accessed=10**6, transcendentals=0)
NT = (((1,), (1,)), ((), ()))
NN = (((1,), (0,)), ((), ()))
TN = (((0,), (0,)), ((), ()))

PAIR = [(0, 1), (1, 0), (2, 3), (3, 2)]
MIDDLE = [(1, 2), (2, 1)]
OUTWARD = [(1, 0), (2, 3)]


def mm(a, b, dims, out=F32):
    return lax.dot_general(a, b, dims, preferred_element_type=F32).astype(out)


def along(array, pairs):
    return lax.ppermute(array, "tp", pairs)


def fence(*arrays):
    return lax.optimization_barrier(arrays)


class Plane:
    def __init__(self, size):
        self.size = size

    def swap(self, array, bit):
        return lax.ppermute(array, "seq", [(i, i ^ bit) for i in range(self.size)])

    def higher(self, total):
        bit = 8
        while bit < self.size:
            total = (total.astype(F32) + self.swap(total, bit).astype(F32)).astype(BF)
            bit *= 2
        return total


def forward_kernel(blocks, q_ref, *refs):
    k_refs, v_refs = refs[:blocks], refs[blocks : 2 * blocks]
    bias_ref, out_ref, lse_ref = refs[2 * blocks], refs[-2], refs[-1]
    scale = HEAD**-0.5 * LOG2E
    rows = q_ref.shape[0]
    lane = lax.broadcasted_iota(jnp.int32, (1, 2 * HEAD), 1)
    zero = jnp.zeros((), BF)
    keys = jnp.concatenate([ref[...] for ref in k_refs])
    values = jnp.concatenate([ref[...] for ref in v_refs])
    bias = bias_ref[...]
    sub = 256
    mine = [(lane < HEAD) == (head == 0) for head in range(2)]
    k = [jnp.where(m, keys, zero) for m in mine]
    v = [jnp.where(m, values, zero) for m in mine]
    for at in range(rows // sub):
        span = pl.ds(at * sub, sub)
        q = q_ref[span, :]
        outs, lses = [], []
        for head in range(2):
            s = lax.dot_general(q, k[head], NT, preferred_element_type=F32)
            s = s * scale + bias
            top = jnp.max(s, axis=1, keepdims=True)
            p = jnp.exp2(s - top)
            total = jnp.sum(p, axis=1, keepdims=True)
            o = lax.dot_general(p.astype(BF), v[head], NN, preferred_element_type=F32)
            outs.append(o / total)
            lses.append(top + jnp.log2(total))
        out_ref[span, :] = (outs[0] + outs[1]).astype(BF)
        wide = jnp.where(lane < HEAD, lses[0], lses[1])
        flat = jnp.transpose(wide)
        lse_ref[0, :, span] = jnp.concatenate(
            [flat[0:1], flat[HEAD : HEAD + 1]], axis=0
        )


def attention_forward(q, kvs, bias, first, count, held=()):
    rows, width = q.shape
    keys = bias.shape[1]
    pairs = width // (2 * HEAD)
    wide = 2 * HEAD
    at = lambda shift: lambda h: (0, h + first + shift)
    return pl.pallas_call(
        functools.partial(forward_kernel, len(kvs)),
        grid=(count,),
        in_specs=[pl.BlockSpec((rows, wide), at(0))]
        + [pl.BlockSpec((kv.shape[0], wide), at(0)) for kv in kvs]
        + [pl.BlockSpec((kv.shape[0], wide), at(pairs)) for kv in kvs]
        + [pl.BlockSpec((1, keys), lambda h: (0, 0))]
        + [pl.BlockSpec(memory_space=pl.ANY)] * len(held),
        out_specs=[
            pl.BlockSpec((rows, wide), at(0)),
            pl.BlockSpec((1, 2, rows), lambda h: (h + first, 0, 0)),
        ],
        out_shape=[
            jax.ShapeDtypeStruct((rows, width), BF),
            jax.ShapeDtypeStruct((pairs, 2, rows), F32),
        ],
        input_output_aliases={2 * len(kvs) + 2 + n: n for n in range(len(held))},
        compiler_params=pltpu.CompilerParams(vmem_limit_bytes=24 * 2**20),
        cost_estimate=LIGHT,
        name="attention_forward",
    )(q, *kvs, *kvs, bias, *held)


def backward_kernel(
    q_ref, k_ref, v_ref, go_ref, att_ref, lse_ref, bias_ref, wkv_ref, *refs
):
    add_ref = refs[0] if len(refs) == 9 else None
    gq_ref, keep_k_ref, keep_v_ref, send_ref, part_ref, all_ref = refs[-6:]
    step, pairs = pl.program_id(0), pl.num_programs(0)
    scale = HEAD**-0.5
    wide = 2 * HEAD
    keys = k_ref.shape[0]
    lane = lax.broadcasted_iota(jnp.int32, (1, wide), 1)
    q, go = q_ref[...], go_ref[...]
    zero = jnp.zeros((), BF)
    mine = [(lane < HEAD) == (head == 0) for head in range(2)]
    qs = [jnp.where(m, q, zero) for m in mine]
    gos = [jnp.where(m, go, zero) for m in mine]
    product = go.T.astype(F32) * att_ref[...].T.astype(F32)
    inner = [
        jnp.sum(product[head * HEAD : (head + 1) * HEAD], axis=0, keepdims=True)
        for head in range(2)
    ]
    total_q = [0.0, 0.0]
    gks, gvs = [], []
    sub = 512
    for at in range(keys // sub):
        span = pl.ds(at * sub, sub)
        bias = bias_ref[span, 0:1]
        keys_t = k_ref[span, :].T
        total_k, total_v = 0.0, 0.0
        for head in range(2):
            k = jnp.where(mine[head], k_ref[span, :], zero)
            v = jnp.where(mine[head], v_ref[span, :], zero)
            s = lax.dot_general(k, q, NT, preferred_element_type=F32)
            p = jnp.exp2(s * (scale * LOG2E) + (bias - lse_ref[0, head : head + 1, :]))
            gp = lax.dot_general(v, go, NT, preferred_element_type=F32)
            gs = (p * (gp - inner[head])).astype(BF)
            total_v += lax.dot_general(p.astype(BF), gos[head], NN, preferred_element_type=F32)
            total_k += lax.dot_general(gs, qs[head], NN, preferred_element_type=F32)
            own_keys = keys_t[head * HEAD : (head + 1) * HEAD]
            total_q[head] += lax.dot_general(own_keys, gs, NN, preferred_element_type=F32)
        gks.append((total_k * scale).astype(BF))
        gvs.append(total_v.astype(BF))
    gk, gv = jnp.concatenate(gks), jnp.concatenate(gvs)
    gq = jnp.concatenate(total_q).T * scale
    gq_ref[...] = (gq if add_ref is None else gq + add_ref[...]).astype(gq_ref.dtype)
    half = pairs // 2

    @pl.when(step < half)
    def _():
        keep_k_ref[...] = gk
        keep_v_ref[...] = gv

    @pl.when(step >= half)
    def _():
        send_ref[0] = gk
        send_ref[1] = gv

    lanes = pl.multiple_of(step * wide, wide)
    all_ref[:, pl.ds(lanes, wide)] = gk
    all_ref[:, pl.ds(pl.multiple_of(lanes + q_width(part_ref), wide), wide)] = gv

    @pl.when(step == pairs - 1)
    def _():
        for at in range(keys // 256):
            span = pl.ds(at * 256, 256)
            part = lax.dot_general(
                all_ref[span, :], wkv_ref[...], NN, preferred_element_type=F32
            )
            part_ref[span, :] = part.astype(BF)


def q_width(part_ref):
    return part_ref.shape[1]


def attention_backward(q, kv, go, attended, lse, bias, wkv, block, blocks, held):
    rows, width = q.shape
    keys = kv.shape[0]
    pairs = width // (2 * HEAD)
    wide = 2 * HEAD
    half = pairs // 2
    by_pair = pl.BlockSpec((rows, wide), lambda h: (0, h))
    stats = pl.BlockSpec((1, 2, rows), lambda h: (h, 0, 0))
    whole = pl.BlockSpec(memory_space=pl.ANY)
    keep = pl.BlockSpec((keys, wide), lambda h: (block, jnp.minimum(h, half - 1)))
    send = pl.BlockSpec((2, keys, wide), lambda h: (0, 0, jnp.maximum(h - half, 0)))
    return pl.pallas_call(
        backward_kernel,
        grid=(pairs,),
        in_specs=[
            by_pair,
            pl.BlockSpec((keys, wide), lambda h: (0, h)),
            pl.BlockSpec((keys, wide), lambda h: (0, h + pairs)),
            by_pair,
            by_pair,
            stats,
            pl.BlockSpec((keys, 128), lambda h: (0, 0)),
            pl.BlockSpec((2 * width, width), lambda h: (0, 0), pipeline_mode=pl.Buffered(1)),
        ]
        + ([by_pair, whole, whole] if held else []),
        out_specs=[by_pair, keep, keep, send, pl.BlockSpec((keys, width), lambda h: (0, 0))],
        out_shape=[
            jax.ShapeDtypeStruct((rows, width), BF if held else F32),
            jax.ShapeDtypeStruct((blocks * keys, width // 2), BF),
            jax.ShapeDtypeStruct((blocks * keys, width // 2), BF),
            jax.ShapeDtypeStruct((2, keys, width // 2), BF),
            jax.ShapeDtypeStruct((keys, width), BF),
        ],
        scratch_shapes=[pltpu.VMEM((keys, 2 * width), BF)],
        input_output_aliases={9: 1, 10: 2} if held else {},
        compiler_params=pltpu.CompilerParams(vmem_limit_bytes=48 * 2**20),
        cost_estimate=LIGHT,
        name="attention_backward",
    )(q, kv, kv, go, attended, lse, bias, wkv, *(held or ()))


def gelu_tile(x):
    size = jnp.abs(x)
    t = 1.0 / (1.0 + size * (0.3275911 * 0.5**0.5))
    poly = t * (
        0.127414796
        + t * (-0.142248368 + t * (0.7107068705 + t * (-0.7265760135 + t * 0.5307027145)))
    )
    bell = jnp.exp2(x * x * (-0.5 * LOG2E))
    tail = poly * bell
    cdf = jnp.where(x >= 0, 1.0 - tail, tail)
    return (x * cdf).astype(BF), (cdf + x * (bell * 0.3989422804014327)).astype(BF)


def head_grads_kernel(
    first, big_ref, came_ref, came_two_ref, small_ref, small_peer_ref,
    rows_ref, rows_two_ref, peer_ref, peer_two_ref, right_ref, right_peer_ref, *out_refs
):
    def outer(left, right):
        return lax.dot_general(left, right[...], TN, preferred_element_type=F32)

    keys = rows_ref.shape[0]
    total = outer(big_ref[:keys, :], rows_ref) + outer(big_ref[keys:, :], rows_two_ref)
    total += outer(came_ref[0], peer_ref) + outer(came_two_ref[0], peer_two_ref)
    total = total.astype(BF)
    other = outer(small_ref[...], right_ref) + outer(small_peer_ref[...], right_peer_ref)
    kinds = [total, other.astype(BF)] if first else [other.astype(BF), total]
    size = HEAD // 2
    for at in range(total.shape[0] // (4 * size)):
        for kind in range(2):
            for chunk in range(4):
                source = (at * 4 + (chunk & 1) * 2 + (chunk >> 1)) * size
                place = (at * 2 + kind) * size
                out_refs[chunk][place : place + size, :] = kinds[kind][source : source + size, :]


def head_grads(first, big, came, small, small_peer, rows, peer, right, right_peer):
    keys, width = rows[0].shape
    own = right.shape[0]
    core = width // 2
    wide = core // 2
    which = 1 if first else 0
    whole = lambda a: pl.BlockSpec(a.shape, lambda g: (0, 0), pipeline_mode=pl.Buffered(1))
    columns = lambda n: pl.BlockSpec((n, wide), lambda g: (0, g))
    arrived = pl.BlockSpec((1, keys, wide), lambda g: (which, 0, g))
    return pl.pallas_call(
        functools.partial(head_grads_kernel, first),
        grid=(core // wide,),
        in_specs=[columns(2 * keys), arrived, arrived, columns(own), columns(own)]
        + [whole(a) for a in (*rows, *peer, right, right_peer)],
        out_specs=[pl.BlockSpec((wide // 2, width), lambda g: (g, 0))] * 4,
        out_shape=[jax.ShapeDtypeStruct((core // 2, width), BF)] * 4,
        compiler_params=pltpu.CompilerParams(vmem_limit_bytes=48 * 2**20),
        cost_estimate=LIGHT,
        name="head_grads",
    )(big, *came, small, small_peer, *rows, *peer, right, right_peer)


def rows_kernel(moves, n_held, n_out, *refs):
    n_in = len(refs) - n_held - n_out - 1
    ins, outs, sems = refs[:n_in], refs[-1 - n_out : -1], refs[-1]
    copies = []
    for n, (source, at, count, out, place) in enumerate(moves):
        copies.append(
            pltpu.make_async_copy(
                ins[source].at[pl.ds(at, count), :],
                outs[out].at[pl.ds(place, count), :],
                sems.at[n],
            )
        )
    for copy in copies:
        copy.start()
    for copy in copies:
        copy.wait()


def put_rows(moves, shape, n_out, held=()):
    arrays, listed = [], []
    for array, at, count, out, place in moves:
        known = [n for n, a in enumerate(arrays) if a is array]
        if not known:
            arrays.append(array)
        listed.append((known[0] if known else len(arrays) - 1, at, count, out, place))
    whole = pl.BlockSpec(memory_space=pl.ANY)
    return pl.pallas_call(
        functools.partial(rows_kernel, listed, len(held), n_out),
        in_specs=[pl.BlockSpec(memory_space=pltpu.VMEM)] * len(arrays) + [whole] * len(held),
        out_specs=[whole] * n_out,
        out_shape=[jax.ShapeDtypeStruct(shape, BF)] * n_out,
        scratch_shapes=[pltpu.SemaphoreType.DMA((len(listed),))],
        input_output_aliases={len(arrays) + n: n for n in range(len(held))},
        compiler_params=pltpu.CompilerParams(vmem_limit_bytes=32 * 2**20),
        cost_estimate=LIGHT,
        name="put_rows",
    )(*arrays, *held)


def totals_kernel(at_ref, *refs):
    *ins, out_ref = refs
    size = ins[0].shape[0]
    for n in range(2):
        a, b, c = [ref[...].astype(F32) for ref in ins[3 * n : 3 * n + 3]]
        out_ref[n * size : (n + 1) * size, :] = (a + b + c).astype(BF)


def totals(ones, twos, t):
    rows, width = ones[0].shape
    size = rows // 4
    return pl.pallas_call(
        totals_kernel,
        grid_spec=pltpu.PrefetchScalarGridSpec(
            num_scalar_prefetch=1,
            grid=(4,),
            in_specs=[pl.BlockSpec((size, width), lambda u, at: (at[0] ^ u, 0))] * 6,
            out_specs=pl.BlockSpec((2 * size, width), lambda u, at: (u, 0)),
        ),
        out_shape=jax.ShapeDtypeStruct((2 * rows, width), BF),
        cost_estimate=LIGHT,
        name="totals",
    )(t[None].astype(jnp.int32), *ones, *twos)


def outer_kernel(left_ref, right_ref, left_two_ref, right_two_ref, *out_refs):
    total = lax.dot_general(left_ref[...], right_ref[...], TN, preferred_element_type=F32)
    total += lax.dot_general(
        left_two_ref[...], right_two_ref[...], TN, preferred_element_type=F32
    )
    total = total.astype(BF)
    each = pl.num_programs(0) // len(out_refs)
    for n, out_ref in enumerate(out_refs):

        @pl.when(pl.program_id(0) // each == n)
        def _():
            out_ref[...] = total


def outer_four(left, right, left_two, right_two):
    rows, hidden = left.shape
    width = right.shape[1]
    tile = 512
    each = hidden // (4 * tile)
    columns = pl.BlockSpec((rows, tile), lambda i: (0, i))
    whole = pl.BlockSpec((rows, width), lambda i: (0, 0))
    place = lambda n: lambda i: (jnp.clip(i - n * each, 0, each - 1), 0)
    return pl.pallas_call(
        outer_kernel,
        grid=(hidden // tile,),
        in_specs=[columns, whole, columns, whole],
        out_specs=[pl.BlockSpec((tile, width), place(n)) for n in range(4)],
        out_shape=[jax.ShapeDtypeStruct((hidden // 4, width), BF)] * 4,
        compiler_params=pltpu.CompilerParams(vmem_limit_bytes=32 * 2**20),
        cost_estimate=LIGHT,
        name="outer_four",
    )(left, right, left_two, right_two)


def reverse(i):
    return ((i & 1) << 2) | (i & 2) | (i >> 2)


def heads_placed_kernel(at_ref, *refs):
    *pieces, turned_ref, plain_ref, whole_ref = refs
    step, last = pl.program_id(0), pl.num_programs(0) - 1
    for i, piece in enumerate(pieces):
        place = reverse(at_ref[0] ^ i)
        size = piece.shape[0]
        whole_ref[pl.ds(pl.multiple_of(place * size, size), size), :] = piece[...]

    @pl.when(step < last)
    def _():
        turned_ref[0] = whole_ref[...].T.astype(F32)

    @pl.when(step == last)
    def _():
        plain_ref[...] = whole_ref[...].astype(F32)


def heads_placed(pieces, s8):
    width = pieces[0].shape[1]
    size = pieces[0].shape[0] // 4
    rows = 8 * size
    return pl.pallas_call(
        heads_placed_kernel,
        grid=(4,),
        in_specs=[pl.BlockSpec(memory_space=pltpu.SMEM)]
        + [pl.BlockSpec((size, width), lambda n: (n, 0)) for _ in pieces],
        out_specs=[
            pl.BlockSpec((1, width, rows), lambda n: (jnp.minimum(n, 2), 0, 0)),
            pl.BlockSpec((rows, width), lambda n: (0, 0)),
        ],
        out_shape=[
            jax.ShapeDtypeStruct((3, width, rows), F32),
            jax.ShapeDtypeStruct((rows, width), F32),
        ],
        scratch_shapes=[pltpu.VMEM((rows, width), BF)],
        compiler_params=pltpu.CompilerParams(vmem_limit_bytes=32 * 2**20),
        cost_estimate=LIGHT,
        name="heads_placed",
    )(s8[None].astype(jnp.int32), *pieces)


def placed_kernel(flips, at_ref, *refs):
    *pieces, out_ref, whole_ref = refs
    for i, piece in enumerate(pieces):
        place = at_ref[0] ^ i
        size = piece.shape[0]
        whole_ref[pl.ds(pl.multiple_of(place * size, size), size), :] = piece[...]
    out = whole_ref[...]
    out = out.T if flips else out
    out_ref[...] = out.astype(F32)


def placed(pieces, size, s8, flips):
    width = pieces[0][0].shape[1]
    tile = 512
    rows = 8 * size
    if flips:
        out_shape, out_spec = (width, rows), pl.BlockSpec((tile, rows), lambda c: (c, 0))
    else:
        out_shape, out_spec = (rows, width), pl.BlockSpec((rows, tile), lambda c: (0, c))
    part = lambda first: pl.BlockSpec((size, tile), lambda c: (first, c))
    return pl.pallas_call(
        functools.partial(placed_kernel, flips),
        grid=(width // tile,),
        in_specs=[pl.BlockSpec(memory_space=pltpu.SMEM)] + [part(first) for _, first in pieces],
        out_specs=out_spec,
        out_shape=jax.ShapeDtypeStruct(out_shape, F32),
        scratch_shapes=[pltpu.VMEM((rows, tile), BF)],
        compiler_params=pltpu.CompilerParams(vmem_limit_bytes=32 * 2**20),
        cost_estimate=LIGHT,
        name="placed",
    )(s8[None].astype(jnp.int32), *[array for array, _ in pieces])


def centred(values):
    centre = values - jnp.mean(values, axis=-1, keepdims=True)
    root = lax.rsqrt(jnp.mean(centre * centre, axis=-1, keepdims=True) + LN_EPS)
    return centre * root, root


def norm_pull(grad, gain, unit, root):
    scaled = grad * gain
    mean = jnp.mean(scaled, axis=-1, keepdims=True)
    slope = jnp.mean(scaled * unit, axis=-1, keepdims=True)
    return root * (scaled - mean - unit * slope), jnp.sum(grad * unit, axis=0)


def per_device(
    seq_size, tokens, w_qkv, w_out, w_up, w_down, gain_one, gain_two, cotangent, bucket, lengths
):
    rows, width = tokens.shape
    t = lax.axis_index("tp")
    middle = (t == 1) | (t == 2)
    s8 = lax.axis_index("seq") % 8
    plane = Plane(seq_size)
    swap = plane.swap
    hid = w_out.shape[0]
    ff = w_down.shape[0]
    qp, fp = hid // 8, ff // 8
    up = lambda a: a.astype(F32)
    across = lambda a, j: along(a, [(i, i ^ j) for i in range(4)])

    w_attn_own = jnp.concatenate([w_qkv.transpose(1, 2, 0), w_out[None]])

    def attn_piece(i):
        return lax.dynamic_slice_in_dim(w_attn_own, reverse(s8 ^ i) * qp, qp, axis=1)

    def up_piece(i):
        return lax.dynamic_slice_in_dim(w_up, (s8 ^ i) * fp, fp, axis=1).T

    def down_piece(i):
        return lax.dynamic_slice_in_dim(w_down, (s8 ^ i) * fp, fp, axis=0)

    attn_own = attn_piece(0).reshape(4 * qp, width)
    up_own = jnp.concatenate([up_piece(2 * i) for i in range(4)])
    down_own = jnp.concatenate([down_piece(2 * i) for i in range(4)])
    ff_own = jnp.concatenate([up_own[:fp], down_own[:fp]])

    upper = rows // 2
    gathered = [
        lax.all_gather(tokens[n * upper : (n + 1) * upper], "tp", axis=0, tiled=True)
        for n in range(2)
    ]
    a_far = [across(attn_own, j) for j in (1, 2, 3)]
    whole = bucket[0] == 1
    place = jnp.arange(rows, dtype=jnp.int32)
    seen = []
    for u in range(4):
        alone = jnp.where(t == u, lengths[0, u], 0)
        limit = jnp.where(whole, lengths[0, 0] - u * rows, alone)
        seen.append((place < limit).reshape(2, upper))
    bias = jnp.where(jnp.stack(seen, axis=1), 0.0, -1e9).astype(F32).reshape(4 * rows)
    bias, *a_far = fence(bias, *a_far)
    bias_cols = jnp.broadcast_to(bias[:, None], (4 * rows, 128))

    attn_three = jnp.concatenate(a_far)
    half = attn_three.shape[0] // 2
    a_x, a_y = swap(attn_three, 2), swap(attn_three, 4)
    attn_three, a_x, a_y = fence(attn_three, a_x, a_y)
    a_d1, a_d2 = swap(a_y[:half], 2), swap(a_x[half:], 4)
    others = [swap(attn_three, 1), swap(a_x, 1), swap(a_y, 1)]
    a_d1, a_d2, *others = fence(a_d1, a_d2, *others)
    others += fence(swap(a_d1, 1), swap(a_d2, 1))

    four = [attn_three, a_x, a_y, a_d1, a_d2]
    pieces = []
    for i in range(8):
        part = others if i & 1 else four
        far = part[i >> 1] if i < 6 else jnp.concatenate(part[3:])
        pieces.append(jnp.concatenate([attn_piece(i)[None], far.reshape(3, 4, qp, width)]))
    w_attn = jnp.stack(pieces).reshape(2, 2, 2, 4, 4, qp, width).transpose(4, 2, 3, 1, 0, 5, 6)
    w_attn = w_attn.reshape(4, width, width)
    wq, wk, wv, wo = [w_attn[n] for n in range(4)]
    wkv = w_attn[1:3].reshape(2 * width, width)

    q = mm(tokens, wq, NT, BF)
    tokens_peer = swap(tokens, 1)
    upper_kv = mm(gathered[0], wkv, NT, BF)
    upper_kv, q, tokens_peer, ff_own, up_own, down_own, *gathered = fence(
        upper_kv, q, tokens_peer, ff_own, up_own, down_own, *gathered
    )
    f_one, f_far = along(ff_own, PAIR), along(ff_own, MIDDLE)
    f_one, f_far, *kvs = fence(f_one, f_far, upper_kv, mm(gathered[1], wkv, NT, BF))
    bias_row = bias[None]
    f_two, f_two_end = along(f_one, MIDDLE), along(f_far, OUTWARD)
    one_x, one_y = swap(f_one, 2), swap(f_one, 4)
    held = attention_forward(q, kvs, bias_row, 0, 2)
    f_two, f_two_end, one_x, one_y, *held = fence(f_two, f_two_end, one_x, one_y, *held)
    f_three_end = along(f_two, OUTWARD)
    f_two = jnp.where(middle, f_two, f_two_end)
    two_x, two_y = swap(f_two, 2), swap(f_two, 4)
    one_d1, one_d2 = swap(one_y[:fp], 2), swap(one_x[fp:], 4)
    held = attention_forward(q, kvs, bias_row, 2, 2, held)
    f_three_end, one_d1, one_d2, two_x, two_y, *held = fence(
        f_three_end, one_d1, one_d2, two_x, two_y, *held
    )
    f_three = jnp.where(middle, f_far, f_three_end)
    three_x, three_y = swap(f_three, 2), swap(f_three, 4)
    two_d1, two_d2 = swap(two_y[:fp], 2), swap(two_x[fp:], 4)

    def moves(j, block):
        own, by_x, by_y, d1, d2 = block
        last = (d1, d2, fp if d1 is d2 else 0)
        sources = [(own, own, fp), (by_x, by_x, fp), (by_y, by_y, fp), last]
        for i, (a, b, at) in enumerate(sources):
            yield (a, 0, fp, 0, (4 * i + j) * fp)
            yield (b, at, fp, 1, (4 * i + j) * fp)

    own = []
    for i in range(4):
        own.append((up_own, i * fp, fp, 0, 4 * i * fp))
        own.append((down_own, i * fp, fp, 1, 4 * i * fp))
    one = moves(1, (f_one, one_x, one_y, one_d1, one_d2))
    w_ff = put_rows([*own, *one], (ff * 2, width), 2)
    w_ff = fence(*w_ff, *held)
    w_ff, held = w_ff[:2], w_ff[2:]
    held = attention_forward(q, kvs, bias_row, 4, 2, held)
    two_d1, two_d2, three_x, three_y, *held = fence(two_d1, two_d2, three_x, three_y, *held)
    three_d1, three_d2 = swap(three_y[:fp], 2), swap(three_x[fp:], 4)
    held = attention_forward(q, kvs, bias_row, 6, 2, held)
    three_d1, three_d2, *held = fence(three_d1, three_d2, *held)
    attended, lse = held
    first_sum = up(tokens) + mm(attended, wo, NN)
    unit_one, root_one = centred(first_sum)
    normed = unit_one * gain_one
    normed_low = normed.astype(BF)

    two = moves(2, (f_two, two_x, two_y, two_d1, two_d2))
    three = moves(3, (f_three, three_x, three_y, three_d1, three_d2))
    wu, wd = put_rows([*two, *three], (ff * 2, width), 2, w_ff)

    normed_peer = swap(normed_low, 1)
    gathered_peer = [swap(part, 1) for part in gathered]
    attended_peer = swap(attended[:, width // 2 :], 1)
    act, slope = gelu_tile(mm(normed_low, wu, NT))
    act_peer, slope_peer = gelu_tile(mm(normed_peer, wu, NT))
    shrunk_peer = swap(mm(act_peer, wd, NN, BF), 1)
    unit_two, root_two = centred(normed + mm(act, wd, NN) + up(shrunk_peer))
    mixed = (unit_two * gain_two).astype(BF)

    grad_second, gain_grad_two = norm_pull(up(cotangent), gain_two, unit_two, root_two)
    second_low = grad_second.astype(BF)
    second_peer = swap(second_low, 1)
    grad_exp = (mm(second_low, wd, NT) * up(slope)).astype(BF)
    grad_exp_peer = (mm(second_peer, wd, NT) * up(slope_peer)).astype(BF)
    normed_part_peer = swap(mm(grad_exp_peer, wu, NN, BF), 1)
    normed_part = mm(grad_exp, wu, NN)
    twos = outer_four(act, second_low, act_peer, second_peer)
    normed_part, normed_part_peer, *twos = fence(normed_part, normed_part_peer, *twos)
    diag_y, two_y = swap(twos[3], 4), swap(twos[2], 4)
    ones = outer_four(grad_exp, normed_low, grad_exp_peer, normed_peer)
    grad_normed = grad_second + normed_part + up(normed_part_peer)
    normed_part, *ones = fence(normed_part, *ones)
    diag_x, one_x = swap(ones[3], 2), swap(ones[1], 2)
    grad_first, gain_grad_one = norm_pull(grad_normed, gain_one, unit_one, root_one)
    first_low = grad_first.astype(BF)
    first_peer = swap(first_low, 1)
    go = mm(first_low, wo, NT, BF)
    core = width // 2
    go, first_peer, attended_peer, *gathered_peer = fence(
        go, first_peer, attended_peer, *gathered_peer
    )

    def pull(n, held):
        keys = bias_cols[2 * n * rows : 2 * (n + 1) * rows]
        *held, send, part = attention_backward(
            q, kvs[n], go, attended, lse, keys, wkv, n, 2, held
        )
        return held, send, part

    def line_sum(part):
        return lax.psum_scatter(part, "tp", scatter_dimension=0, tiled=True)

    gains = jnp.stack([gain_grad_one, gain_grad_two])
    gains_came = across(gains, 1)
    held, send, part = pull(0, None)
    diag_x, diag_y, one_x, two_y, send, part, gains_came, *held = fence(
        diag_x, diag_y, one_x, two_y, send, part, gains_came, *held
    )
    upper_sum = line_sum(part)
    came = [swap(send, 1)]
    gains = gains + gains_came
    gains_came = across(gains, 2)
    two_x = (up(twos[1]) + up(diag_y)).astype(BF)
    one_y = (up(ones[2]) + up(diag_x)).astype(BF)
    two_x, one_y, *held = fence(two_x, one_y, *held)
    two_x, one_y = swap(two_x, 2), swap(one_y, 4)
    held, send, part = pull(1, held)
    two_x, one_y, came[0], send, part, gains_came, *held = fence(
        two_x, one_y, came[0], send, part, gains_came, *held
    )
    gq, gk, gv = held
    came.append(swap(send, 1))
    gq_peer = swap(gq[:, core:], 1)
    gains = gains + gains_came
    gains_came = swap(gains, 1)
    lower_sum = line_sum(part)
    ff_total = plane.higher(totals((ones[0], one_x, one_y), (twos[0], two_x, two_y), t))
    upper_sum, ff_total = fence(upper_sum, ff_total)
    ff_total = line_sum(ff_total)
    came[1], gq_peer, gains_came = fence(came[1], gq_peer, gains_came)
    gains = gains + gains_came
    a_twos = fence(
        *head_grads(
            True, gv, came, attended, attended_peer, gathered, gathered_peer, first_low, first_peer
        )
    )
    a_diag_y, a_two_y = swap(a_twos[3], 4), swap(a_twos[2], 4)
    a_ones = head_grads(
        False, gk, came, gq, gq_peer, gathered, gathered_peer, tokens, tokens_peer
    )
    a_diag_y, gq, *a_ones = fence(a_diag_y, gq, *a_ones)
    a_diag_x, a_one_x = swap(a_ones[3], 2), swap(a_ones[1], 2)
    gains_came = swap(gains, 2)
    a_two_x = (up(a_twos[1]) + up(a_diag_y)).astype(BF)
    first = mm(gq, wq, NN) + grad_first
    a_two_x, a_diag_x, first = fence(a_two_x, a_diag_x, first)
    a_one_y = (up(a_ones[2]) + up(a_diag_x)).astype(BF)
    a_two_x, a_one_y, ff_total = fence(a_two_x, a_one_y, ff_total)
    a_two_x, a_one_y = swap(a_two_x, 2), swap(a_one_y, 4)
    f_x, f_y = swap(ff_total, 2), swap(ff_total, 4)
    a_two_x, a_one_y, a_one_x, a_two_y, gains_came = fence(
        a_two_x, a_one_y, a_one_x, a_two_y, gains_came
    )
    gains = gains + gains_came
    gains_came = swap(gains, 4)
    vo_mine = plane.higher((up(a_twos[0]) + up(a_two_x) + up(a_two_y)).astype(BF))
    qk_mine = plane.higher((up(a_ones[0]) + up(a_one_x) + up(a_one_y)).astype(BF))
    qk_mine, vo_mine = qk_mine.reshape(4, 2 * qp, width), vo_mine.reshape(4, 2 * qp, width)
    a_mine = fence(*[jnp.concatenate([qk_mine[j], vo_mine[j]]) for j in range(4)])
    a_came = [across(a_mine[j], j) for j in (1, 2, 3)]
    f_core = [swap(ff_total, 1)]
    f_d1, f_d2 = swap(f_y[:fp], 2), swap(f_x[fp:], 4)
    f_core += [swap(f_x, 1), swap(f_y, 1)]
    *a_came, f_d1, f_d2, b0, b1, b2, gains_came = fence(*a_came, f_d1, f_d2, *f_core, gains_came)
    f_core = [b0, b1, b2]
    gains = gains + gains_came
    bit = 8
    while bit < seq_size:
        gains = gains + swap(gains, bit)
        bit *= 2
    a_total = fence(sum((up(a) for a in a_came), up(a_mine[0])).astype(BF))[0]
    a_four = [a_total, swap(a_total, 2), swap(a_total, 4), swap(a_total, 6)]
    a_core = [swap(a_total, 1)]
    f_core += [swap(f_d1, 1), swap(f_d2, 1)]
    f_four = [ff_total, f_x, f_y, f_d1, f_d2]
    ups, downs = [], []
    for i in range(8):
        part = f_core if i & 1 else f_four
        ups.append((part[i >> 1], 0))
        downs.append((part[i >> 1], 1) if i < 6 else (part[4], 0))
    grad_up = placed(ups, fp, s8, True)
    grad_down = placed(downs, fp, s8, False)
    tokens_grad = (first + up(jnp.concatenate([upper_sum, lower_sum]))).astype(BF)
    grad_up, grad_down, tokens_grad, *a_four = fence(grad_up, grad_down, tokens_grad, *a_four)
    a_core += [swap(a, 1) for a in a_four[1:]]
    a_all = [(a_core if i & 1 else a_four)[i >> 1] for i in range(8)]
    grad_qkv, grad_out = heads_placed(a_all, s8)
    return (
        mixed,
        tokens_grad,
        grad_qkv.transpose(1, 0, 2),
        grad_out,
        grad_up,
        grad_down,
        gains[0],
        gains[1],
    )


def solution(mesh):
    rows = P(("seq", "tp"), None)
    weights = (P(None, None, "tp"), P("tp", None), P(None, "tp"), P("tp", None), P(), P())
    return jax.shard_map(
        functools.partial(per_device, mesh.shape["seq"]),
        mesh=mesh,
        in_specs=(rows,) + weights + (rows, P("seq"), P("seq", None)),
        out_specs=(rows, rows) + weights,
        check_vma=False,
    )
```

```python
import functools

import jax
import jax.numpy as jnp
from jax import lax
from jax.experimental import pallas as pl
from jax.experimental.pallas import tpu as pltpu
from jax.sharding import PartitionSpec as P

HEAD = 64
SLOTS = 4
BF = jnp.bfloat16
F32 = jnp.float32
LOG2E = 1.4426950408889634
LN_EPS = 1e-5
LIGHT = pl.CostEstimate(flops=10**9, bytes_accessed=10**6, transcendentals=0)
NT = (((1,), (1,)), ((), ()))
NN = (((1,), (0,)), ((), ()))
TN = (((0,), (0,)), ((), ()))

PAIR = [(0, 1), (1, 0), (2, 3), (3, 2)]
MIDDLE = [(1, 2), (2, 1)]
OUTWARD = [(1, 0), (2, 3)]


def in_hbm(*arrays):
    return [pltpu.with_memory_space_constraint(a, pltpu.HBM) for a in arrays]


def mm(a, b, dims, out=F32):
    return lax.dot_general(a, b, dims, preferred_element_type=F32).astype(out)


def along(array, pairs):
    return lax.ppermute(array, "tp", pairs)


def fence(*arrays):
    return lax.optimization_barrier(arrays)


class Plane:
    def __init__(self, size):
        self.size = size

    def swap(self, array, bit):
        return lax.ppermute(array, "seq", [(i, i ^ bit) for i in range(self.size)])

    def higher(self, total):
        bit = 8
        while bit < self.size:
            total = (total.astype(F32) + self.swap(total, bit).astype(F32)).astype(BF)
            bit *= 2
        return total


def forward_kernel(blocks, q_ref, *refs):
    k_refs, v_refs = refs[:blocks], refs[blocks : 2 * blocks]
    bias_ref, out_ref, lse_ref = refs[2 * blocks], refs[-2], refs[-1]
    scale = HEAD**-0.5 * LOG2E
    rows = q_ref.shape[0]
    lane = lax.broadcasted_iota(jnp.int32, (1, 2 * HEAD), 1)
    zero = jnp.zeros((), BF)
    keys = jnp.concatenate([ref[...] for ref in k_refs])
    values = jnp.concatenate([ref[...] for ref in v_refs])
    bias = bias_ref[...]
    sub = 256
    mine = [(lane < HEAD) == (head == 0) for head in range(2)]
    k = [jnp.where(m, keys, zero) for m in mine]
    v = [jnp.where(m, values, zero) for m in mine]
    for at in range(rows // sub):
        span = pl.ds(at * sub, sub)
        q = q_ref[span, :]
        outs, lses = [], []
        for head in range(2):
            s = lax.dot_general(q, k[head], NT, preferred_element_type=F32)
            s = s * scale + bias
            top = jnp.max(s, axis=1, keepdims=True)
            p = jnp.exp2(s - top)
            total = jnp.sum(p, axis=1, keepdims=True)
            o = lax.dot_general(p.astype(BF), v[head], NN, preferred_element_type=F32)
            outs.append(o / total)
            lses.append(top + jnp.log2(total))
        out_ref[span, :] = (outs[0] + outs[1]).astype(BF)
        wide = jnp.where(lane < HEAD, lses[0], lses[1])
        flat = jnp.transpose(wide)
        lse_ref[0, :, span] = jnp.concatenate(
            [flat[0:1], flat[HEAD : HEAD + 1]], axis=0
        )


def attention_forward(q, kvs, bias, first, count, held=()):
    rows, width = q.shape
    keys = bias.shape[1]
    pairs = width // (2 * HEAD)
    wide = 2 * HEAD
    at = lambda shift: lambda h: (0, h + first + shift)
    return pl.pallas_call(
        functools.partial(forward_kernel, len(kvs)),
        grid=(count,),
        in_specs=[pl.BlockSpec((rows, wide), at(0))]
        + [pl.BlockSpec((kv.shape[0], wide), at(0)) for kv in kvs]
        + [pl.BlockSpec((kv.shape[0], wide), at(pairs)) for kv in kvs]
        + [pl.BlockSpec((1, keys), lambda h: (0, 0))]
        + [pl.BlockSpec(memory_space=pl.ANY)] * len(held),
        out_specs=[
            pl.BlockSpec((rows, wide), at(0)),
            pl.BlockSpec((1, 2, rows), lambda h: (h + first, 0, 0)),
        ],
        out_shape=[
            jax.ShapeDtypeStruct((rows, width), BF),
            jax.ShapeDtypeStruct((pairs, 2, rows), F32),
        ],
        input_output_aliases={2 * len(kvs) + 2 + n: n for n in range(len(held))},
        compiler_params=pltpu.CompilerParams(vmem_limit_bytes=24 * 2**20),
        cost_estimate=LIGHT,
        name="attention_forward",
    )(q, *kvs, *kvs, bias, *held)


def backward_kernel(
    q_ref, k_ref, v_ref, go_ref, att_ref, lse_ref, bias_ref, wkv_ref, *refs
):
    add_ref = refs[0] if len(refs) == 9 else None
    gq_ref, keep_k_ref, keep_v_ref, send_ref, part_ref, all_ref = refs[-6:]
    step, pairs = pl.program_id(0), pl.num_programs(0)
    scale = HEAD**-0.5
    wide = 2 * HEAD
    keys = k_ref.shape[0]
    lane = lax.broadcasted_iota(jnp.int32, (1, wide), 1)
    q, go = q_ref[...], go_ref[...]
    zero = jnp.zeros((), BF)
    mine = [(lane < HEAD) == (head == 0) for head in range(2)]
    qs = [jnp.where(m, q, zero) for m in mine]
    gos = [jnp.where(m, go, zero) for m in mine]
    product = go.T.astype(F32) * att_ref[...].T.astype(F32)
    inner = [
        jnp.sum(product[head * HEAD : (head + 1) * HEAD], axis=0, keepdims=True)
        for head in range(2)
    ]
    total_q = [0.0, 0.0]
    gks, gvs = [], []
    sub = 512
    for at in range(keys // sub):
        span = pl.ds(at * sub, sub)
        bias = bias_ref[span, 0:1]
        keys_t = k_ref[span, :].T
        total_k, total_v = 0.0, 0.0
        for head in range(2):
            k = jnp.where(mine[head], k_ref[span, :], zero)
            v = jnp.where(mine[head], v_ref[span, :], zero)
            s = lax.dot_general(k, q, NT, preferred_element_type=F32)
            p = jnp.exp2(s * (scale * LOG2E) + (bias - lse_ref[0, head : head + 1, :]))
            gp = lax.dot_general(v, go, NT, preferred_element_type=F32)
            gs = (p * (gp - inner[head])).astype(BF)
            total_v += lax.dot_general(p.astype(BF), gos[head], NN, preferred_element_type=F32)
            total_k += lax.dot_general(gs, qs[head], NN, preferred_element_type=F32)
            own_keys = keys_t[head * HEAD : (head + 1) * HEAD]
            total_q[head] += lax.dot_general(own_keys, gs, NN, preferred_element_type=F32)
        gks.append((total_k * scale).astype(BF))
        gvs.append(total_v.astype(BF))
    gk, gv = jnp.concatenate(gks), jnp.concatenate(gvs)
    gq = jnp.concatenate(total_q).T * scale
    gq_ref[...] = (gq if add_ref is None else gq + add_ref[...]).astype(gq_ref.dtype)
    half = pairs // 2

    @pl.when(step < half)
    def _():
        keep_k_ref[...] = gk
        keep_v_ref[...] = gv

    @pl.when(step >= half)
    def _():
        send_ref[0] = gk
        send_ref[1] = gv

    lanes = pl.multiple_of(step * wide, wide)
    all_ref[:, pl.ds(lanes, wide)] = gk
    all_ref[:, pl.ds(pl.multiple_of(lanes + q_width(part_ref), wide), wide)] = gv

    @pl.when(step == pairs - 1)
    def _():
        for at in range(keys // 256):
            span = pl.ds(at * 256, 256)
            part = lax.dot_general(
                all_ref[span, :], wkv_ref[...], NN, preferred_element_type=F32
            )
            part_ref[span, :] = part.astype(BF)


def q_width(part_ref):
    return part_ref.shape[1]


def attention_backward(q, kv, go, attended, lse, bias, wkv, block, blocks, held):
    rows, width = q.shape
    keys = kv.shape[0]
    pairs = width // (2 * HEAD)
    wide = 2 * HEAD
    half = pairs // 2
    by_pair = pl.BlockSpec((rows, wide), lambda h: (0, h))
    stats = pl.BlockSpec((1, 2, rows), lambda h: (h, 0, 0))
    whole = pl.BlockSpec(memory_space=pl.ANY)
    keep = pl.BlockSpec((keys, wide), lambda h: (block, jnp.minimum(h, half - 1)))
    send = pl.BlockSpec((2, keys, wide), lambda h: (0, 0, jnp.maximum(h - half, 0)))
    return pl.pallas_call(
        backward_kernel,
        grid=(pairs,),
        in_specs=[
            by_pair,
            pl.BlockSpec((keys, wide), lambda h: (0, h)),
            pl.BlockSpec((keys, wide), lambda h: (0, h + pairs)),
            by_pair,
            by_pair,
            stats,
            pl.BlockSpec((keys, 128), lambda h: (0, 0)),
            pl.BlockSpec((2 * width, width), lambda h: (0, 0), pipeline_mode=pl.Buffered(1)),
        ]
        + ([by_pair, whole, whole] if held else []),
        out_specs=[by_pair, keep, keep, send, pl.BlockSpec((keys, width), lambda h: (0, 0))],
        out_shape=[
            jax.ShapeDtypeStruct((rows, width), BF if held else F32),
            jax.ShapeDtypeStruct((blocks * keys, width // 2), BF),
            jax.ShapeDtypeStruct((blocks * keys, width // 2), BF),
            jax.ShapeDtypeStruct((2, keys, width // 2), BF),
            jax.ShapeDtypeStruct((keys, width), BF),
        ],
        scratch_shapes=[pltpu.VMEM((keys, 2 * width), BF)],
        input_output_aliases={9: 1, 10: 2} if held else {},
        compiler_params=pltpu.CompilerParams(vmem_limit_bytes=48 * 2**20),
        cost_estimate=LIGHT,
        name="attention_backward",
    )(*in_hbm(q, kv, kv, go, attended), lse, bias, *in_hbm(wkv, *(held or ())))


def gelu_tile(x):
    size = jnp.abs(x)
    t = 1.0 / (1.0 + size * (0.3275911 * 0.5**0.5))
    poly = t * (
        0.127414796
        + t * (-0.142248368 + t * (0.7107068705 + t * (-0.7265760135 + t * 0.5307027145)))
    )
    bell = jnp.exp2(x * x * (-0.5 * LOG2E))
    tail = poly * bell
    cdf = jnp.where(x >= 0, 1.0 - tail, tail)
    return (x * cdf).astype(BF), (cdf + x * (bell * 0.3989422804014327)).astype(BF)


def head_grads_kernel(many, *refs):
    ins, (x_ref, y_ref, near_x_ref, near_y_ref, own_ref) = refs[:-5], refs[-5:]

    def outer(left, right):
        return lax.dot_general(left, right, TN, preferred_element_type=F32)

    if many:
        big_refs, came_refs, row_refs = ins[:2], ins[2:4], ins[4:]
        keys = row_refs[0].shape[0]
        totals_of = []
        for kind in range(2):
            total = 0.0
            for n in range(2):
                part = slice(n * keys, (n + 1) * keys)
                total += outer(big_refs[kind][part, :], row_refs[n][...])
                total += outer(came_refs[n][kind], row_refs[2 + n][...])
            totals_of.append(total.astype(BF))
    else:
        totals_of = []
        for kind in range(2):
            left, left_peer, right, right_peer = [ref[...] for ref in ins[4 * kind : 4 * kind + 4]]
            totals_of.append((outer(left, right) + outer(left_peer, right_peer)).astype(BF))
    size = HEAD // 2

    def chunk(n):
        rows = []
        for at in range(totals_of[0].shape[0] // (4 * size)):
            source = (at * 4 + (n & 1) * 2 + (n >> 1)) * size
            rows += [total[source : source + size] for total in totals_of]
        return jnp.concatenate(rows)

    half = own_ref.shape[0]
    own_ref[...] = chunk(0)

    @pl.when(pl.program_id(0) == 0)
    def _():
        x_ref[:half, :] = chunk(3)
        x_ref[half:, :] = chunk(1)
        near_y_ref[...] = chunk(2)

    @pl.when(pl.program_id(0) == 1)
    def _():
        y_ref[:half, :] = chunk(3)
        y_ref[half:, :] = chunk(2)
        near_x_ref[...] = chunk(1)


def head_grads(columns, arrived, whole_arrays, many, order=None):
    width = whole_arrays[0].shape[1]
    wide = width // 4
    half = wide // 2
    by_column = [pl.BlockSpec((a.shape[0], wide), lambda g: (0, g)) for a in columns]
    by_kind = [pl.BlockSpec((2, a.shape[1], wide), lambda g: (0, 0, g)) for a in arrived]
    whole = [
        pl.BlockSpec(a.shape, lambda g: (0, 0), pipeline_mode=pl.Buffered(1))
        for a in whole_arrays
    ]
    args, specs = [*columns, *arrived, *whole_arrays], by_column + by_kind + whole
    if order:
        args, specs = [args[n] for n in order], [specs[n] for n in order]
    fixed = lambda rows: pl.BlockSpec((rows, width), lambda g: (0, 0))
    shape = lambda rows: jax.ShapeDtypeStruct((rows, width), BF)
    return pl.pallas_call(
        functools.partial(head_grads_kernel, many),
        grid=(2,),
        in_specs=specs,
        out_specs=[fixed(wide), fixed(wide), fixed(half), fixed(half)]
        + [pl.BlockSpec((half, width), lambda g: (g, 0))],
        out_shape=[shape(wide), shape(wide), shape(half), shape(half), shape(wide)],
        compiler_params=pltpu.CompilerParams(vmem_limit_bytes=48 * 2**20),
        cost_estimate=LIGHT,
        name="head_grads",
    )(*in_hbm(*args))


def rows_kernel(moves, n_held, n_out, *refs):
    n_in = len(refs) - n_held - n_out - 1
    ins, outs, sems = refs[:n_in], refs[-1 - n_out : -1], refs[-1]
    copies = []
    for n, (source, at, count, out, place) in enumerate(moves):
        copies.append(
            pltpu.make_async_copy(
                ins[source].at[pl.ds(at, count), :],
                outs[out].at[pl.ds(place, count), :],
                sems.at[n],
            )
        )
    for copy in copies:
        copy.start()
    for copy in copies:
        copy.wait()


def put_rows(moves, shape, n_out, held=()):
    arrays, listed = [], []
    for array, at, count, out, place in moves:
        known = [n for n, a in enumerate(arrays) if a is array]
        if not known:
            arrays.append(array)
        listed.append((known[0] if known else len(arrays) - 1, at, count, out, place))
    whole = pl.BlockSpec(memory_space=pl.ANY)
    return pl.pallas_call(
        functools.partial(rows_kernel, listed, len(held), n_out),
        in_specs=[pl.BlockSpec(memory_space=pltpu.VMEM)] * len(arrays) + [whole] * len(held),
        out_specs=[whole] * n_out,
        out_shape=[jax.ShapeDtypeStruct(shape, BF)] * n_out,
        scratch_shapes=[pltpu.SemaphoreType.DMA((len(listed),))],
        input_output_aliases={len(arrays) + n: n for n in range(len(held))},
        compiler_params=pltpu.CompilerParams(vmem_limit_bytes=32 * 2**20),
        cost_estimate=LIGHT,
        name="put_rows",
    )(*arrays, *held)


def totals_kernel(at_ref, *refs):
    *ins, out_ref = refs
    size = ins[0].shape[0]
    for n in range(2):
        a, b, c = [ref[...].astype(F32) for ref in ins[3 * n : 3 * n + 3]]
        out_ref[n * size : (n + 1) * size, :] = (a + b + c).astype(BF)


def totals(ones, twos, t):
    rows, width = ones[0].shape
    size = rows // 4
    return pl.pallas_call(
        totals_kernel,
        grid_spec=pltpu.PrefetchScalarGridSpec(
            num_scalar_prefetch=1,
            grid=(4,),
            in_specs=[pl.BlockSpec((size, width), lambda u, at: (at[0] ^ u, 0))] * 6,
            out_specs=pl.BlockSpec((2 * size, width), lambda u, at: (u, 0)),
        ),
        out_shape=jax.ShapeDtypeStruct((2 * rows, width), BF),
        cost_estimate=LIGHT,
        name="totals",
    )(t[None].astype(jnp.int32), *ones, *twos)


def outer_kernel(left_ref, right_ref, left_two_ref, right_two_ref, *out_refs):
    total = lax.dot_general(left_ref[...], right_ref[...], TN, preferred_element_type=F32)
    total += lax.dot_general(
        left_two_ref[...], right_two_ref[...], TN, preferred_element_type=F32
    )
    total = total.astype(BF)
    each = pl.num_programs(0) // len(out_refs)
    for n, out_ref in enumerate(out_refs):

        @pl.when(pl.program_id(0) // each == n)
        def _():
            out_ref[...] = total


def outer_four(left, right, left_two, right_two):
    rows, hidden = left.shape
    width = right.shape[1]
    tile = 512
    each = hidden // (4 * tile)
    columns = pl.BlockSpec((rows, tile), lambda i: (0, i))
    whole = pl.BlockSpec((rows, width), lambda i: (0, 0))
    place = lambda n: lambda i: (jnp.clip(i - n * each, 0, each - 1), 0)
    return pl.pallas_call(
        outer_kernel,
        grid=(hidden // tile,),
        in_specs=[columns, whole, columns, whole],
        out_specs=[pl.BlockSpec((tile, width), place(n)) for n in range(4)],
        out_shape=[jax.ShapeDtypeStruct((hidden // 4, width), BF)] * 4,
        compiler_params=pltpu.CompilerParams(vmem_limit_bytes=32 * 2**20),
        cost_estimate=LIGHT,
        name="outer_four",
    )(left, right, left_two, right_two)


def reverse(i):
    return ((i & 1) << 2) | (i & 2) | (i >> 2)


def heads_placed_kernel(at_ref, *refs):
    *pieces, turned_ref, plain_ref, whole_ref = refs
    step, last = pl.program_id(0), pl.num_programs(0) - 1
    for i, piece in enumerate(pieces):
        place = reverse(at_ref[0] ^ i)
        size = piece.shape[0]
        whole_ref[pl.ds(pl.multiple_of(place * size, size), size), :] = piece[...]

    @pl.when(step < last)
    def _():
        turned_ref[0] = whole_ref[...].T.astype(F32)

    @pl.when(step == last)
    def _():
        plain_ref[...] = whole_ref[...].astype(F32)


def heads_placed(pieces, s8):
    kind_at = lambda n: jnp.where(n == 0, 0, jnp.where(n == 3, 1, n + 1))
    width = pieces[0].shape[1]
    size = pieces[0].shape[0] // 4
    rows = 8 * size
    return pl.pallas_call(
        heads_placed_kernel,
        grid=(4,),
        in_specs=[pl.BlockSpec(memory_space=pltpu.SMEM)]
        + [pl.BlockSpec((size, width), lambda n: (kind_at(n), 0)) for _ in pieces],
        out_specs=[
            pl.BlockSpec((1, width, rows), lambda n: (jnp.minimum(n, 2), 0, 0)),
            pl.BlockSpec((rows, width), lambda n: (0, 0)),
        ],
        out_shape=[
            jax.ShapeDtypeStruct((3, width, rows), F32),
            jax.ShapeDtypeStruct((rows, width), F32),
        ],
        scratch_shapes=[pltpu.VMEM((rows, width), BF)],
        compiler_params=pltpu.CompilerParams(vmem_limit_bytes=32 * 2**20),
        cost_estimate=LIGHT,
        name="heads_placed",
    )(s8[None].astype(jnp.int32), *pieces)


def placed_kernel(flips, at_ref, *refs):
    *pieces, out_ref, whole_ref = refs
    for i, piece in enumerate(pieces):
        place = at_ref[0] ^ i
        size = piece.shape[0]
        whole_ref[pl.ds(pl.multiple_of(place * size, size), size), :] = piece[...]
    out = whole_ref[...]
    out = out.T if flips else out
    out_ref[...] = out.astype(F32)


def placed(pieces, size, s8, flips):
    width = pieces[0][0].shape[1]
    tile = 512
    rows = 8 * size
    if flips:
        out_shape, out_spec = (width, rows), pl.BlockSpec((tile, rows), lambda c: (c, 0))
    else:
        out_shape, out_spec = (rows, width), pl.BlockSpec((rows, tile), lambda c: (0, c))
    part = lambda first: pl.BlockSpec((size, tile), lambda c: (first, c))
    return pl.pallas_call(
        functools.partial(placed_kernel, flips),
        grid=(width // tile,),
        in_specs=[pl.BlockSpec(memory_space=pltpu.SMEM)] + [part(first) for _, first in pieces],
        out_specs=out_spec,
        out_shape=jax.ShapeDtypeStruct(out_shape, F32),
        scratch_shapes=[pltpu.VMEM((rows, tile), BF)],
        compiler_params=pltpu.CompilerParams(vmem_limit_bytes=32 * 2**20),
        cost_estimate=LIGHT,
        name="placed",
    )(s8[None].astype(jnp.int32), *[array for array, _ in pieces])


def centred(values):
    centre = values - jnp.mean(values, axis=-1, keepdims=True)
    root = lax.rsqrt(jnp.mean(centre * centre, axis=-1, keepdims=True) + LN_EPS)
    return centre * root, root


def norm_pull(grad, gain, unit, root):
    scaled = grad * gain
    mean = jnp.mean(scaled, axis=-1, keepdims=True)
    slope = jnp.mean(scaled * unit, axis=-1, keepdims=True)
    return root * (scaled - mean - unit * slope), jnp.sum(grad * unit, axis=0)


def per_device(
    seq_size, tokens, w_qkv, w_out, w_up, w_down, gain_one, gain_two, cotangent, bucket, lengths
):
    rows, width = tokens.shape
    t = lax.axis_index("tp")
    middle = (t == 1) | (t == 2)
    s8 = lax.axis_index("seq") % 8
    plane = Plane(seq_size)
    swap = plane.swap
    hid = w_out.shape[0]
    ff = w_down.shape[0]
    qp, fp = hid // 8, ff // 8
    up = lambda a: a.astype(F32)
    across = lambda a, j: along(a, [(i, i ^ j) for i in range(4)])

    w_attn_own = jnp.concatenate([w_qkv.transpose(1, 2, 0), w_out[None]])

    def attn_piece(i):
        return lax.dynamic_slice_in_dim(w_attn_own, reverse(s8 ^ i) * qp, qp, axis=1)

    def up_piece(i):
        return lax.dynamic_slice_in_dim(w_up, (s8 ^ i) * fp, fp, axis=1).T

    def down_piece(i):
        return lax.dynamic_slice_in_dim(w_down, (s8 ^ i) * fp, fp, axis=0)

    attn_own = attn_piece(0).reshape(4 * qp, width)
    up_own = jnp.concatenate([up_piece(2 * i) for i in range(4)])
    down_own = jnp.concatenate([down_piece(2 * i) for i in range(4)])
    ff_own = jnp.concatenate([up_own[:fp], down_own[:fp]])

    upper = rows // 2
    gathered = [
        lax.all_gather(tokens[n * upper : (n + 1) * upper], "tp", axis=0, tiled=True)
        for n in range(2)
    ]
    a_far = [across(attn_own, j) for j in (1, 2, 3)]
    whole = bucket[0] == 1
    place = jnp.arange(rows, dtype=jnp.int32)
    seen = []
    for u in range(4):
        alone = jnp.where(t == u, lengths[0, u], 0)
        limit = jnp.where(whole, lengths[0, 0] - u * rows, alone)
        seen.append((place < limit).reshape(2, upper))
    bias = jnp.where(jnp.stack(seen, axis=1), 0.0, -1e9).astype(F32).reshape(4 * rows)
    bias, *a_far = fence(bias, *a_far)
    bias_cols = jnp.broadcast_to(bias[:, None], (4 * rows, 128))

    attn_three = jnp.concatenate(a_far)
    half = attn_three.shape[0] // 2
    a_x, a_y = swap(attn_three, 2), swap(attn_three, 4)
    attn_three, a_x, a_y = fence(attn_three, a_x, a_y)
    a_d1, a_d2 = swap(a_y[:half], 2), swap(a_x[half:], 4)
    others = [swap(attn_three, 1), swap(a_x, 1), swap(a_y, 1)]
    a_d1, a_d2, *others = fence(a_d1, a_d2, *others)
    others += fence(swap(a_d1, 1), swap(a_d2, 1))

    four = [attn_three, a_x, a_y, a_d1, a_d2]
    pieces = []
    for i in range(8):
        part = others if i & 1 else four
        far = part[i >> 1] if i < 6 else jnp.concatenate(part[3:])
        pieces.append(jnp.concatenate([attn_piece(i)[None], far.reshape(3, 4, qp, width)]))
    w_attn = jnp.stack(pieces).reshape(2, 2, 2, 4, 4, qp, width).transpose(4, 2, 3, 1, 0, 5, 6)
    w_attn = w_attn.reshape(4, width, width)
    wq, wk, wv, wo = [w_attn[n] for n in range(4)]
    wkv = w_attn[1:3].reshape(2 * width, width)

    q = mm(tokens, wq, NT, BF)
    tokens_peer = swap(tokens, 1)
    upper_kv = mm(gathered[0], wkv, NT, BF)
    upper_kv, q, tokens_peer, ff_own, up_own, down_own, *gathered = fence(
        upper_kv, q, tokens_peer, ff_own, up_own, down_own, *gathered
    )
    f_one, f_far = along(ff_own, PAIR), along(ff_own, MIDDLE)
    f_one, f_far, *kvs = fence(f_one, f_far, upper_kv, mm(gathered[1], wkv, NT, BF))
    bias_row = bias[None]
    f_two, f_two_end = along(f_one, MIDDLE), along(f_far, OUTWARD)
    one_x, one_y = swap(f_one, 2), swap(f_one, 4)
    held = attention_forward(q, kvs, bias_row, 0, 2)
    f_two, f_two_end, one_x, one_y, *held = fence(f_two, f_two_end, one_x, one_y, *held)
    f_three_end = along(f_two, OUTWARD)
    f_two = jnp.where(middle, f_two, f_two_end)
    two_x, two_y = swap(f_two, 2), swap(f_two, 4)
    one_d1, one_d2 = swap(one_y[:fp], 2), swap(one_x[fp:], 4)
    held = attention_forward(q, kvs, bias_row, 2, 2, held)
    f_three_end, one_d1, one_d2, two_x, two_y, *held = fence(
        f_three_end, one_d1, one_d2, two_x, two_y, *held
    )
    f_three = jnp.where(middle, f_far, f_three_end)
    three_x, three_y = swap(f_three, 2), swap(f_three, 4)
    two_d1, two_d2 = swap(two_y[:fp], 2), swap(two_x[fp:], 4)

    def moves(j, block):
        own, by_x, by_y, d1, d2 = block
        last = (d1, d2, fp if d1 is d2 else 0)
        sources = [(own, own, fp), (by_x, by_x, fp), (by_y, by_y, fp), last]
        for i, (a, b, at) in enumerate(sources):
            yield (a, 0, fp, 0, (4 * i + j) * fp)
            yield (b, at, fp, 1, (4 * i + j) * fp)

    own = []
    for i in range(4):
        own.append((up_own, i * fp, fp, 0, 4 * i * fp))
        own.append((down_own, i * fp, fp, 1, 4 * i * fp))
    one = moves(1, (f_one, one_x, one_y, one_d1, one_d2))
    w_ff = put_rows([*own, *one], (ff * 2, width), 2)
    w_ff = fence(*w_ff, *held)
    w_ff, held = w_ff[:2], w_ff[2:]
    held = attention_forward(q, kvs, bias_row, 4, 2, held)
    two_d1, two_d2, three_x, three_y, *held = fence(two_d1, two_d2, three_x, three_y, *held)
    three_d1, three_d2 = swap(three_y[:fp], 2), swap(three_x[fp:], 4)
    held = attention_forward(q, kvs, bias_row, 6, 2, held)
    three_d1, three_d2, *held = fence(three_d1, three_d2, *held)
    attended, lse = held
    first_sum = up(tokens) + mm(attended, wo, NN)
    unit_one, root_one = centred(first_sum)
    normed = unit_one * gain_one
    normed_low = normed.astype(BF)

    two = moves(2, (f_two, two_x, two_y, two_d1, two_d2))
    three = moves(3, (f_three, three_x, three_y, three_d1, three_d2))
    wu, wd = put_rows([*two, *three], (ff * 2, width), 2, w_ff)

    normed_peer = swap(normed_low, 1)
    gathered_peer = [swap(part, 1) for part in gathered]
    attended_peer = swap(attended[:, width // 2 :], 1)
    act, slope = gelu_tile(mm(normed_low, wu, NT))
    act_peer, slope_peer = gelu_tile(mm(normed_peer, wu, NT))
    shrunk_peer = swap(mm(act_peer, wd, NN, BF), 1)
    unit_two, root_two = centred(normed + mm(act, wd, NN) + up(shrunk_peer))
    mixed = (unit_two * gain_two).astype(BF)

    grad_second, gain_grad_two = norm_pull(up(cotangent), gain_two, unit_two, root_two)
    second_low = grad_second.astype(BF)
    second_peer = swap(second_low, 1)
    grad_exp = (mm(second_low, wd, NT) * up(slope)).astype(BF)
    grad_exp_peer = (mm(second_peer, wd, NT) * up(slope_peer)).astype(BF)
    normed_part_peer = swap(mm(grad_exp_peer, wu, NN, BF), 1)
    normed_part = mm(grad_exp, wu, NN)
    twos = outer_four(act, second_low, act_peer, second_peer)
    normed_part, normed_part_peer, *twos = fence(normed_part, normed_part_peer, *twos)
    diag_y, two_y = swap(twos[3], 4), swap(twos[2], 4)
    ones = outer_four(grad_exp, normed_low, grad_exp_peer, normed_peer)
    grad_normed = grad_second + normed_part + up(normed_part_peer)
    normed_part, *ones = fence(normed_part, *ones)
    diag_x, one_x = swap(ones[3], 2), swap(ones[1], 2)
    grad_first, gain_grad_one = norm_pull(grad_normed, gain_one, unit_one, root_one)
    first_low = grad_first.astype(BF)
    first_peer = swap(first_low, 1)
    go = mm(first_low, wo, NT, BF)
    core = width // 2
    go, first_peer, attended_peer, *gathered_peer = fence(
        go, first_peer, attended_peer, *gathered_peer
    )

    def pull(n, held):
        keys = bias_cols[2 * n * rows : 2 * (n + 1) * rows]
        *held, send, part = attention_backward(
            q, kvs[n], go, attended, lse, keys, wkv, n, 2, held
        )
        return held, send, part

    def line_sum(part):
        return lax.psum_scatter(part, "tp", scatter_dimension=0, tiled=True)

    gains = jnp.stack([gain_grad_one, gain_grad_two])
    gains_came = across(gains, 1)
    held, send, part = pull(0, None)
    diag_x, diag_y, one_x, two_y, send, part, gains_came, *held = fence(
        diag_x, diag_y, one_x, two_y, send, part, gains_came, *held
    )
    upper_sum = line_sum(part)
    came = [swap(send, 1)]
    gains = gains + gains_came
    gains_came = across(gains, 2)
    two_x = (up(twos[1]) + up(diag_y)).astype(BF)
    one_y = (up(ones[2]) + up(diag_x)).astype(BF)
    two_x, one_y, *held = fence(two_x, one_y, *held)
    two_x, one_y = swap(two_x, 2), swap(one_y, 4)
    held, send, part = pull(1, held)
    two_x, one_y, came[0], send, part, gains_came, *held = fence(
        two_x, one_y, came[0], send, part, gains_came, *held
    )
    gq, gk, gv = held
    gq_peer = swap(gq[:, core:], 1)
    gains = gains + gains_came
    gains_came = swap(gains, 1)
    part = part.reshape(4, 2, upper // 2, width)
    part_one, part_two = [part[:, n].reshape(rows, width) for n in range(2)]
    lower_one = line_sum(part_one)
    ff_total = plane.higher(totals((ones[0], one_x, one_y), (twos[0], two_x, two_y), t))
    upper_sum, ff_total = fence(upper_sum, ff_total)
    ff_total = line_sum(ff_total)
    gq_peer, gains_came, send = fence(gq_peer, gains_came, send)
    came.append(swap(send, 1))
    gains = gains + gains_came
    light = head_grads(
        [gq, gq_peer, attended, attended_peer],
        [],
        [tokens, tokens_peer, first_low, first_peer],
        False,
        (0, 1, 4, 5, 2, 3, 6, 7),
    )
    came[1], *light = fence(came[1], *light)
    to_x, to_y = swap(light[0], 2), swap(light[1], 4)
    heavy = head_grads([gk, gv], came, [*gathered, *gathered_peer], True)
    to_x, to_y, gq, *heavy = fence(to_x, to_y, gq, *heavy)
    half = 4 * qp
    add = lambda *arrays: sum(up(a) for a in arrays).astype(BF)

    def second_hop(parts, to_x, to_y):
        return add(parts[2], to_y[:half]), add(parts[3], to_x[:half])

    def mine_of(parts, to_x, to_y, on_x, on_y):
        own = parts[4]
        total = [add(own[:half], to_x[half:], on_y), add(own[half:], to_y[half:], on_x)]
        return plane.higher(jnp.concatenate(total)).reshape(4, 2 * qp, width)

    next_x, next_y = second_hop(light, to_x, to_y)
    next_x, next_y, *heavy = fence(next_x, next_y, *heavy)
    on_x, on_y = swap(next_x, 2), swap(next_y, 4)
    far_x, far_y = swap(heavy[0], 2), swap(heavy[1], 4)
    gains_came = swap(gains, 2)
    first = mm(gq, wq, NN) + grad_first
    on_x, on_y, far_x, far_y, first = fence(on_x, on_y, far_x, far_y, first)
    next_x, next_y = second_hop(heavy, far_x, far_y)
    next_x, next_y, ff_total = fence(next_x, next_y, ff_total)
    last_x, last_y = swap(next_x, 2), swap(next_y, 4)
    f_x, f_y = swap(ff_total, 2), swap(ff_total, 4)
    light_mine = mine_of(light, to_x, to_y, on_x, on_y)
    last_x, last_y, light_mine, gains_came = fence(last_x, last_y, light_mine, gains_came)
    gains = gains + gains_came
    heavy_mine = mine_of(heavy, far_x, far_y, last_x, last_y)
    a_mine = jnp.concatenate([light_mine, heavy_mine], axis=1)
    pairs = a_mine.reshape(2, 2, 4 * qp, width)
    pairs = jnp.where((t & 1) == 1, pairs[:, ::-1], pairs)
    a_mine = fence(jnp.where((t & 2) == 2, pairs[::-1], pairs).reshape(a_mine.shape))[0]
    a_came = lax.all_to_all(a_mine, "tp", split_axis=0, concat_axis=0, tiled=True)
    f_core = [swap(ff_total, 1)]
    f_d1, f_d2 = swap(f_y[:fp], 2), swap(f_x[fp:], 4)
    f_core += [swap(f_x, 1), swap(f_y, 1)]
    a_came, part_two, f_d1, f_d2, b0, b1, b2 = fence(a_came, part_two, f_d1, f_d2, *f_core)
    f_core = [b0, b1, b2]
    lower_two = line_sum(part_two)
    a_total, gains = fence(jnp.sum(up(a_came), axis=0).astype(BF), gains)
    gains = gains + swap(gains, 4)
    bit = 8
    while bit < seq_size:
        gains = gains + swap(gains, bit)
        bit *= 2
    a_four = [a_total, swap(a_total, 2), swap(a_total, 4), swap(a_total, 6)]
    a_core = [swap(a_total, 1)]
    f_core += [swap(f_d1, 1), swap(f_d2, 1)]
    f_four = [ff_total, f_x, f_y, f_d1, f_d2]
    ups, downs = [], []
    for i in range(8):
        part = f_core if i & 1 else f_four
        ups.append((part[i >> 1], 0))
        downs.append((part[i >> 1], 1) if i < 6 else (part[4], 0))
    grad_up = placed(ups, fp, s8, True)
    grad_down = placed(downs, fp, s8, False)
    grad_up, grad_down, *a_four = fence(grad_up, grad_down, *a_four)
    a_core += [swap(a, 1) for a in a_four[1:]]
    a_all = [(a_core if i & 1 else a_four)[i >> 1] for i in range(8)]
    grad_qkv, grad_out = heads_placed(a_all, s8)
    tokens_grad = (first + up(jnp.concatenate([upper_sum, lower_one, lower_two]))).astype(BF)
    return (
        mixed,
        tokens_grad,
        grad_qkv.transpose(1, 0, 2),
        grad_out,
        grad_up,
        grad_down,
        gains[0],
        gains[1],
    )


def solution(mesh):
    rows = P(("seq", "tp"), None)
    weights = (P(None, None, "tp"), P("tp", None), P(None, "tp"), P("tp", None), P(), P())
    return jax.shard_map(
        functools.partial(per_device, mesh.shape["seq"]),
        mesh=mesh,
        in_specs=(rows,) + weights + (rows, P("seq"), P("seq", None)),
        out_specs=(rows, rows) + weights,
        check_vma=False,
    )
```

```python
import functools

import jax
import jax.numpy as jnp
from jax import lax
from jax.experimental import pallas as pl
from jax.experimental.pallas import tpu as pltpu
from jax.sharding import PartitionSpec as P

HEAD = 64
SLOTS = 4
BF = jnp.bfloat16
F32 = jnp.float32
LOG2E = 1.4426950408889634
LN_EPS = 1e-5
LIGHT = pl.CostEstimate(flops=10**9, bytes_accessed=10**6, transcendentals=0)
NT = (((1,), (1,)), ((), ()))
NN = (((1,), (0,)), ((), ()))
TN = (((0,), (0,)), ((), ()))

PAIR = [(0, 1), (1, 0), (2, 3), (3, 2)]
MIDDLE = [(1, 2), (2, 1)]
OUTWARD = [(1, 0), (2, 3)]


def in_hbm(*arrays):
    return [pltpu.with_memory_space_constraint(a, pltpu.HBM) for a in arrays]


def mm(a, b, dims, out=F32):
    return lax.dot_general(a, b, dims, preferred_element_type=F32).astype(out)


def along(array, pairs):
    return lax.ppermute(array, "tp", pairs)


def fence(*arrays):
    return lax.optimization_barrier(arrays)


class Plane:
    def __init__(self, size):
        self.size = size

    def swap(self, array, bit):
        return lax.ppermute(array, "seq", [(i, i ^ bit) for i in range(self.size)])

    def higher_exact(self, total):
        bit = 8
        while bit < self.size:
            total = total + self.swap(total, bit)
            bit *= 2
        return total

    def higher(self, total):
        bit = 8
        while bit < self.size:
            total = (total.astype(F32) + self.swap(total, bit).astype(F32)).astype(BF)
            bit *= 2
        return total


def forward_kernel(blocks, q_ref, *refs):
    k_refs, v_refs = refs[:blocks], refs[blocks : 2 * blocks]
    bias_ref, out_ref, lse_ref = refs[2 * blocks], refs[-2], refs[-1]
    scale = HEAD**-0.5 * LOG2E
    rows = q_ref.shape[0]
    lane = lax.broadcasted_iota(jnp.int32, (1, 2 * HEAD), 1)
    zero = jnp.zeros((), BF)
    keys = jnp.concatenate([ref[...] for ref in k_refs])
    values = jnp.concatenate([ref[...] for ref in v_refs])
    bias = bias_ref[...]
    sub = 256
    mine = [(lane < HEAD) == (head == 0) for head in range(2)]
    k = [jnp.where(m, keys, zero) for m in mine]
    v = [jnp.where(m, values, zero) for m in mine]
    for at in range(rows // sub):
        span = pl.ds(at * sub, sub)
        q = q_ref[span, :]
        outs, lses = [], []
        for head in range(2):
            s = lax.dot_general(q, k[head], NT, preferred_element_type=F32)
            s = s * scale + bias
            top = jnp.max(s, axis=1, keepdims=True)
            p = jnp.exp2(s - top)
            total = jnp.sum(p, axis=1, keepdims=True)
            o = lax.dot_general(p.astype(BF), v[head], NN, preferred_element_type=F32)
            outs.append(o / total)
            lses.append(top + jnp.log2(total))
        out_ref[span, :] = (outs[0] + outs[1]).astype(BF)
        wide = jnp.where(lane < HEAD, lses[0], lses[1])
        flat = jnp.transpose(wide)
        lse_ref[0, :, span] = jnp.concatenate(
            [flat[0:1], flat[HEAD : HEAD + 1]], axis=0
        )


def attention_forward(q, kvs, bias, first, count, held=()):
    rows, width = q.shape
    keys = bias.shape[1]
    pairs = width // (2 * HEAD)
    wide = 2 * HEAD
    at = lambda shift: lambda h: (0, h + first + shift)
    return pl.pallas_call(
        functools.partial(forward_kernel, len(kvs)),
        grid=(count,),
        in_specs=[pl.BlockSpec((rows, wide), at(0))]
        + [pl.BlockSpec((kv.shape[0], wide), at(0)) for kv in kvs]
        + [pl.BlockSpec((kv.shape[0], wide), at(pairs)) for kv in kvs]
        + [pl.BlockSpec((1, keys), lambda h: (0, 0))]
        + [pl.BlockSpec(memory_space=pl.ANY)] * len(held),
        out_specs=[
            pl.BlockSpec((rows, wide), at(0)),
            pl.BlockSpec((1, 2, rows), lambda h: (h + first, 0, 0)),
        ],
        out_shape=[
            jax.ShapeDtypeStruct((rows, width), BF),
            jax.ShapeDtypeStruct((pairs, 2, rows), F32),
        ],
        input_output_aliases={2 * len(kvs) + 2 + n: n for n in range(len(held))},
        compiler_params=pltpu.CompilerParams(vmem_limit_bytes=24 * 2**20),
        cost_estimate=LIGHT,
        name="attention_forward",
    )(q, *kvs, *kvs, bias, *held)


def backward_kernel(
    q_ref, k_ref, v_ref, go_ref, att_ref, lse_ref, bias_ref, wkv_ref, *refs
):
    add_ref = refs[0] if len(refs) == 9 else None
    gq_ref, keep_k_ref, keep_v_ref, send_ref, part_ref, all_ref = refs[-6:]
    step, pairs = pl.program_id(0), pl.num_programs(0)
    scale = HEAD**-0.5
    wide = 2 * HEAD
    keys = k_ref.shape[0]
    lane = lax.broadcasted_iota(jnp.int32, (1, wide), 1)
    q, go = q_ref[...], go_ref[...]
    zero = jnp.zeros((), BF)
    mine = [(lane < HEAD) == (head == 0) for head in range(2)]
    qs = [jnp.where(m, q, zero) for m in mine]
    gos = [jnp.where(m, go, zero) for m in mine]
    product = go.T.astype(F32) * att_ref[...].T.astype(F32)
    inner = [
        jnp.sum(product[head * HEAD : (head + 1) * HEAD], axis=0, keepdims=True)
        for head in range(2)
    ]
    total_q = [0.0, 0.0]
    gks, gvs = [], []
    sub = 512
    for at in range(keys // sub):
        span = pl.ds(at * sub, sub)
        bias = bias_ref[span, 0:1]
        keys_t = k_ref[span, :].T
        total_k, total_v = 0.0, 0.0
        for head in range(2):
            k = jnp.where(mine[head], k_ref[span, :], zero)
            v = jnp.where(mine[head], v_ref[span, :], zero)
            s = lax.dot_general(k, q, NT, preferred_element_type=F32)
            p = jnp.exp2(s * (scale * LOG2E) + (bias - lse_ref[0, head : head + 1, :]))
            gp = lax.dot_general(v, go, NT, preferred_element_type=F32)
            gs = (p * (gp - inner[head])).astype(BF)
            total_v += lax.dot_general(p.astype(BF), gos[head], NN, preferred_element_type=F32)
            total_k += lax.dot_general(gs, qs[head], NN, preferred_element_type=F32)
            own_keys = keys_t[head * HEAD : (head + 1) * HEAD]
            total_q[head] += lax.dot_general(own_keys, gs, NN, preferred_element_type=F32)
        gks.append((total_k * scale).astype(BF))
        gvs.append(total_v.astype(BF))
    gk, gv = jnp.concatenate(gks), jnp.concatenate(gvs)
    gq = jnp.concatenate(total_q).T * scale
    gq_ref[...] = (gq if add_ref is None else gq + add_ref[...]).astype(gq_ref.dtype)
    half = pairs // 2

    @pl.when(step < half)
    def _():
        keep_k_ref[...] = gk
        keep_v_ref[...] = gv

    @pl.when(step >= half)
    def _():
        send_ref[0] = gk
        send_ref[1] = gv

    lanes = pl.multiple_of(step * wide, wide)
    all_ref[:, pl.ds(lanes, wide)] = gk
    all_ref[:, pl.ds(pl.multiple_of(lanes + q_width(part_ref), wide), wide)] = gv

    @pl.when(step == pairs - 1)
    def _():
        for at in range(keys // 256):
            span = pl.ds(at * 256, 256)
            part = lax.dot_general(
                all_ref[span, :], wkv_ref[...], NN, preferred_element_type=F32
            )
            part_ref[span, :] = part.astype(BF)


def q_width(part_ref):
    return part_ref.shape[1]


def attention_backward(q, kv, go, attended, lse, bias, wkv, block, blocks, held):
    rows, width = q.shape
    keys = kv.shape[0]
    pairs = width // (2 * HEAD)
    wide = 2 * HEAD
    half = pairs // 2
    by_pair = pl.BlockSpec((rows, wide), lambda h: (0, h))
    stats = pl.BlockSpec((1, 2, rows), lambda h: (h, 0, 0))
    whole = pl.BlockSpec(memory_space=pl.ANY)
    keep = pl.BlockSpec((keys, wide), lambda h: (block, jnp.minimum(h, half - 1)))
    send = pl.BlockSpec((2, keys, wide), lambda h: (0, 0, jnp.maximum(h - half, 0)))
    return pl.pallas_call(
        backward_kernel,
        grid=(pairs,),
        in_specs=[
            by_pair,
            pl.BlockSpec((keys, wide), lambda h: (0, h)),
            pl.BlockSpec((keys, wide), lambda h: (0, h + pairs)),
            by_pair,
            by_pair,
            stats,
            pl.BlockSpec((keys, 128), lambda h: (0, 0)),
            pl.BlockSpec((2 * width, width), lambda h: (0, 0), pipeline_mode=pl.Buffered(1)),
        ]
        + ([by_pair, whole, whole] if held else []),
        out_specs=[by_pair, keep, keep, send, pl.BlockSpec((keys, width), lambda h: (0, 0))],
        out_shape=[
            jax.ShapeDtypeStruct((rows, width), BF if held else F32),
            jax.ShapeDtypeStruct((blocks * keys, width // 2), BF),
            jax.ShapeDtypeStruct((blocks * keys, width // 2), BF),
            jax.ShapeDtypeStruct((2, keys, width // 2), BF),
            jax.ShapeDtypeStruct((keys, width), BF),
        ],
        scratch_shapes=[pltpu.VMEM((keys, 2 * width), BF)],
        input_output_aliases={9: 1, 10: 2} if held else {},
        compiler_params=pltpu.CompilerParams(vmem_limit_bytes=48 * 2**20),
        cost_estimate=LIGHT,
        name="attention_backward",
    )(*in_hbm(q, kv, kv, go, attended), lse, bias, *in_hbm(wkv, *(held or ())))


def gelu_tile(x):
    size = jnp.abs(x)
    t = 1.0 / (1.0 + size * (0.3275911 * 0.5**0.5))
    poly = t * (
        0.127414796
        + t * (-0.142248368 + t * (0.7107068705 + t * (-0.7265760135 + t * 0.5307027145)))
    )
    bell = jnp.exp2(x * x * (-0.5 * LOG2E))
    tail = poly * bell
    cdf = jnp.where(x >= 0, 1.0 - tail, tail)
    return (x * cdf).astype(BF), (cdf + x * (bell * 0.3989422804014327)).astype(BF)


def head_grads_kernel(many, *refs):
    ins, (x_ref, y_ref, near_x_ref, near_y_ref, own_ref) = refs[:-5], refs[-5:]

    def outer(left, right):
        return lax.dot_general(left, right, TN, preferred_element_type=F32)

    if many:
        big_refs, came_refs, row_refs = ins[:2], ins[2:4], ins[4:]
        keys = row_refs[0].shape[0]
        totals_of = []
        for kind in range(2):
            total = 0.0
            for n in range(2):
                part = slice(n * keys, (n + 1) * keys)
                total += outer(big_refs[kind][part, :], row_refs[n][...])
                total += outer(came_refs[n][kind], row_refs[2 + n][...])
            totals_of.append(total.astype(BF))
    else:
        totals_of = []
        for kind in range(2):
            left, left_peer, right, right_peer = [ref[...] for ref in ins[4 * kind : 4 * kind + 4]]
            totals_of.append((outer(left, right) + outer(left_peer, right_peer)).astype(BF))
    size = HEAD // 2

    def chunk(n):
        rows = []
        for at in range(totals_of[0].shape[0] // (4 * size)):
            source = (at * 4 + (n & 1) * 2 + (n >> 1)) * size
            rows += [total[source : source + size] for total in totals_of]
        return jnp.concatenate(rows)

    half = own_ref.shape[0]
    own_ref[...] = chunk(0)

    @pl.when(pl.program_id(0) == 0)
    def _():
        x_ref[:half, :] = chunk(3)
        x_ref[half:, :] = chunk(1)
        near_y_ref[...] = chunk(2)

    @pl.when(pl.program_id(0) == 1)
    def _():
        y_ref[:half, :] = chunk(3)
        y_ref[half:, :] = chunk(2)
        near_x_ref[...] = chunk(1)


def head_grads(columns, arrived, whole_arrays, many, order=None):
    width = whole_arrays[0].shape[1]
    wide = width // 4
    half = wide // 2
    by_column = [pl.BlockSpec((a.shape[0], wide), lambda g: (0, g)) for a in columns]
    by_kind = [pl.BlockSpec((2, a.shape[1], wide), lambda g: (0, 0, g)) for a in arrived]
    whole = [
        pl.BlockSpec(a.shape, lambda g: (0, 0), pipeline_mode=pl.Buffered(1))
        for a in whole_arrays
    ]
    args, specs = [*columns, *arrived, *whole_arrays], by_column + by_kind + whole
    if order:
        args, specs = [args[n] for n in order], [specs[n] for n in order]
    fixed = lambda rows: pl.BlockSpec((rows, width), lambda g: (0, 0))
    shape = lambda rows: jax.ShapeDtypeStruct((rows, width), BF)
    return pl.pallas_call(
        functools.partial(head_grads_kernel, many),
        grid=(2,),
        in_specs=specs,
        out_specs=[fixed(wide), fixed(wide), fixed(half), fixed(half)]
        + [pl.BlockSpec((half, width), lambda g: (g, 0))],
        out_shape=[shape(wide), shape(wide), shape(half), shape(half), shape(wide)],
        compiler_params=pltpu.CompilerParams(vmem_limit_bytes=48 * 2**20),
        cost_estimate=LIGHT,
        name="head_grads",
    )(*in_hbm(*args))


def rows_kernel(moves, n_held, n_out, *refs):
    n_in = len(refs) - n_held - n_out - 1
    ins, outs, sems = refs[:n_in], refs[-1 - n_out : -1], refs[-1]
    copies = []
    for n, (source, at, count, out, place) in enumerate(moves):
        copies.append(
            pltpu.make_async_copy(
                ins[source].at[pl.ds(at, count), :],
                outs[out].at[pl.ds(place, count), :],
                sems.at[n],
            )
        )
    for copy in copies:
        copy.start()
    for copy in copies:
        copy.wait()


def put_rows(moves, shape, n_out, held=()):
    arrays, listed = [], []
    for array, at, count, out, place in moves:
        known = [n for n, a in enumerate(arrays) if a is array]
        if not known:
            arrays.append(array)
        listed.append((known[0] if known else len(arrays) - 1, at, count, out, place))
    whole = pl.BlockSpec(memory_space=pl.ANY)
    return pl.pallas_call(
        functools.partial(rows_kernel, listed, len(held), n_out),
        in_specs=[pl.BlockSpec(memory_space=pltpu.VMEM)] * len(arrays) + [whole] * len(held),
        out_specs=[whole] * n_out,
        out_shape=[jax.ShapeDtypeStruct(shape, BF)] * n_out,
        scratch_shapes=[pltpu.SemaphoreType.DMA((len(listed),))],
        input_output_aliases={len(arrays) + n: n for n in range(len(held))},
        compiler_params=pltpu.CompilerParams(vmem_limit_bytes=32 * 2**20),
        cost_estimate=LIGHT,
        name="put_rows",
    )(*arrays, *held)


def totals_kernel(at_ref, *refs):
    *ins, out_ref = refs
    size = ins[0].shape[0]
    for n in range(2):
        a, b, c = [ref[...].astype(F32) for ref in ins[3 * n : 3 * n + 3]]
        out_ref[n * size : (n + 1) * size, :] = (a + b + c).astype(BF)


def totals(ones, twos, t):
    rows, width = ones[0].shape
    size = rows // 4
    return pl.pallas_call(
        totals_kernel,
        grid_spec=pltpu.PrefetchScalarGridSpec(
            num_scalar_prefetch=1,
            grid=(4,),
            in_specs=[pl.BlockSpec((size, width), lambda u, at: (at[0] ^ u, 0))] * 6,
            out_specs=pl.BlockSpec((2 * size, width), lambda u, at: (u, 0)),
        ),
        out_shape=jax.ShapeDtypeStruct((2 * rows, width), BF),
        cost_estimate=LIGHT,
        name="totals",
    )(t[None].astype(jnp.int32), *ones, *twos)


def outer_kernel(left_ref, right_ref, left_two_ref, right_two_ref, *out_refs):
    total = lax.dot_general(left_ref[...], right_ref[...], TN, preferred_element_type=F32)
    total += lax.dot_general(
        left_two_ref[...], right_two_ref[...], TN, preferred_element_type=F32
    )
    total = total.astype(BF)
    each = pl.num_programs(0) // len(out_refs)
    for n, out_ref in enumerate(out_refs):

        @pl.when(pl.program_id(0) // each == n)
        def _():
            out_ref[...] = total


def outer_four(left, right, left_two, right_two):
    rows, hidden = left.shape
    width = right.shape[1]
    tile = 512
    each = hidden // (4 * tile)
    columns = pl.BlockSpec((rows, tile), lambda i: (0, i))
    whole = pl.BlockSpec((rows, width), lambda i: (0, 0))
    place = lambda n: lambda i: (jnp.clip(i - n * each, 0, each - 1), 0)
    return pl.pallas_call(
        outer_kernel,
        grid=(hidden // tile,),
        in_specs=[columns, whole, columns, whole],
        out_specs=[pl.BlockSpec((tile, width), place(n)) for n in range(4)],
        out_shape=[jax.ShapeDtypeStruct((hidden // 4, width), BF)] * 4,
        compiler_params=pltpu.CompilerParams(vmem_limit_bytes=32 * 2**20),
        cost_estimate=LIGHT,
        name="outer_four",
    )(left, right, left_two, right_two)


def reverse(i):
    return ((i & 1) << 2) | (i & 2) | (i >> 2)


def heads_placed_kernel(at_ref, *refs):
    *pieces, turned_ref, plain_ref, whole_ref = refs
    step, last = pl.program_id(0), pl.num_programs(0) - 1
    for i, piece in enumerate(pieces):
        place = reverse(at_ref[0] ^ i)
        size = piece.shape[0]
        whole_ref[pl.ds(pl.multiple_of(place * size, size), size), :] = piece[...]

    @pl.when(step < last)
    def _():
        turned_ref[0] = whole_ref[...].T.astype(F32)

    @pl.when(step == last)
    def _():
        plain_ref[...] = whole_ref[...].astype(F32)


def heads_placed(pieces, s8):
    kind_at = lambda n: jnp.where(n == 0, 0, jnp.where(n == 3, 1, n + 1))
    width = pieces[0].shape[1]
    size = pieces[0].shape[0] // 4
    rows = 8 * size
    return pl.pallas_call(
        heads_placed_kernel,
        grid=(4,),
        in_specs=[pl.BlockSpec(memory_space=pltpu.SMEM)]
        + [pl.BlockSpec((size, width), lambda n: (kind_at(n), 0)) for _ in pieces],
        out_specs=[
            pl.BlockSpec((1, width, rows), lambda n: (jnp.minimum(n, 2), 0, 0)),
            pl.BlockSpec((rows, width), lambda n: (0, 0)),
        ],
        out_shape=[
            jax.ShapeDtypeStruct((3, width, rows), F32),
            jax.ShapeDtypeStruct((rows, width), F32),
        ],
        scratch_shapes=[pltpu.VMEM((rows, width), BF)],
        compiler_params=pltpu.CompilerParams(vmem_limit_bytes=32 * 2**20),
        cost_estimate=LIGHT,
        name="heads_placed",
    )(s8[None].astype(jnp.int32), *pieces)


def placed_kernel(flips, at_ref, *refs):
    *pieces, out_ref, whole_ref = refs
    for i, piece in enumerate(pieces):
        place = at_ref[0] ^ i
        size = piece.shape[0]
        whole_ref[pl.ds(pl.multiple_of(place * size, size), size), :] = piece[...]
    out = whole_ref[...]
    out = out.T if flips else out
    out_ref[...] = out.astype(F32)


def placed(pieces, size, s8, flips):
    width = pieces[0][0].shape[1]
    tile = 512
    rows = 8 * size
    if flips:
        out_shape, out_spec = (width, rows), pl.BlockSpec((tile, rows), lambda c: (c, 0))
    else:
        out_shape, out_spec = (rows, width), pl.BlockSpec((rows, tile), lambda c: (0, c))
    part = lambda first: pl.BlockSpec((size, tile), lambda c: (first, c))
    return pl.pallas_call(
        functools.partial(placed_kernel, flips),
        grid=(width // tile,),
        in_specs=[pl.BlockSpec(memory_space=pltpu.SMEM)] + [part(first) for _, first in pieces],
        out_specs=out_spec,
        out_shape=jax.ShapeDtypeStruct(out_shape, F32),
        scratch_shapes=[pltpu.VMEM((rows, tile), BF)],
        compiler_params=pltpu.CompilerParams(vmem_limit_bytes=32 * 2**20),
        cost_estimate=LIGHT,
        name="placed",
    )(s8[None].astype(jnp.int32), *[array for array, _ in pieces])


def centred(values):
    centre = values - jnp.mean(values, axis=-1, keepdims=True)
    root = lax.rsqrt(jnp.mean(centre * centre, axis=-1, keepdims=True) + LN_EPS)
    return centre * root, root


def norm_pull(grad, gain, unit, root):
    scaled = grad * gain
    mean = jnp.mean(scaled, axis=-1, keepdims=True)
    slope = jnp.mean(scaled * unit, axis=-1, keepdims=True)
    return root * (scaled - mean - unit * slope), jnp.sum(grad * unit, axis=0)


def per_device(
    seq_size, tokens, w_qkv, w_out, w_up, w_down, gain_one, gain_two, cotangent, bucket, lengths
):
    rows, width = tokens.shape
    t = lax.axis_index("tp")
    middle = (t == 1) | (t == 2)
    s8 = lax.axis_index("seq") % 8
    plane = Plane(seq_size)
    swap = plane.swap
    hid = w_out.shape[0]
    ff = w_down.shape[0]
    qp, fp = hid // 8, ff // 8
    up = lambda a: a.astype(F32)
    across = lambda a, j: along(a, [(i, i ^ j) for i in range(4)])

    w_attn_own = jnp.concatenate([w_qkv.transpose(1, 2, 0), w_out[None]])

    def attn_piece(i):
        return lax.dynamic_slice_in_dim(w_attn_own, reverse(s8 ^ i) * qp, qp, axis=1)

    def up_piece(i):
        return lax.dynamic_slice_in_dim(w_up, (s8 ^ i) * fp, fp, axis=1).T

    def down_piece(i):
        return lax.dynamic_slice_in_dim(w_down, (s8 ^ i) * fp, fp, axis=0)

    attn_own = attn_piece(0).reshape(4 * qp, width)
    up_own = jnp.concatenate([up_piece(2 * i) for i in range(4)])
    down_own = jnp.concatenate([down_piece(2 * i) for i in range(4)])
    ff_own = jnp.concatenate([up_own[:fp], down_own[:fp]])

    upper = rows // 2
    gathered = [
        lax.all_gather(tokens[n * upper : (n + 1) * upper], "tp", axis=0, tiled=True)
        for n in range(2)
    ]
    a_far = [across(attn_own, j) for j in (1, 2, 3)]
    whole = bucket[0] == 1
    place = jnp.arange(rows, dtype=jnp.int32)
    seen = []
    for u in range(4):
        alone = jnp.where(t == u, lengths[0, u], 0)
        limit = jnp.where(whole, lengths[0, 0] - u * rows, alone)
        seen.append((place < limit).reshape(2, upper))
    bias = jnp.where(jnp.stack(seen, axis=1), 0.0, -1e9).astype(F32).reshape(4 * rows)
    bias, *a_far = fence(bias, *a_far)
    bias_cols = jnp.broadcast_to(bias[:, None], (4 * rows, 128))

    attn_three = jnp.concatenate(a_far)
    half = attn_three.shape[0] // 2
    a_x, a_y = swap(attn_three, 2), swap(attn_three, 4)
    attn_three, a_x, a_y = fence(attn_three, a_x, a_y)
    a_d1, a_d2 = swap(a_y[:half], 2), swap(a_x[half:], 4)
    others = [swap(attn_three, 1), swap(a_x, 1), swap(a_y, 1)]
    a_d1, a_d2, *others = fence(a_d1, a_d2, *others)
    others += fence(swap(a_d1, 1), swap(a_d2, 1))

    four = [attn_three, a_x, a_y, a_d1, a_d2]
    pieces = []
    for i in range(8):
        part = others if i & 1 else four
        far = part[i >> 1] if i < 6 else jnp.concatenate(part[3:])
        pieces.append(jnp.concatenate([attn_piece(i)[None], far.reshape(3, 4, qp, width)]))
    w_attn = jnp.stack(pieces).reshape(2, 2, 2, 4, 4, qp, width).transpose(4, 2, 3, 1, 0, 5, 6)
    w_attn = w_attn.reshape(4, width, width)
    wq, wk, wv, wo = [w_attn[n] for n in range(4)]
    wkv = w_attn[1:3].reshape(2 * width, width)

    q = mm(tokens, wq, NT, BF)
    tokens_peer = swap(tokens, 1)
    upper_kv = mm(gathered[0], wkv, NT, BF)
    upper_kv, q, tokens_peer, ff_own, up_own, down_own, *gathered = fence(
        upper_kv, q, tokens_peer, ff_own, up_own, down_own, *gathered
    )
    f_one, f_far = along(ff_own, PAIR), along(ff_own, MIDDLE)
    f_one, f_far, *kvs = fence(f_one, f_far, upper_kv, mm(gathered[1], wkv, NT, BF))
    bias_row = bias[None]
    f_two, f_two_end = along(f_one, MIDDLE), along(f_far, OUTWARD)
    one_x, one_y = swap(f_one, 2), swap(f_one, 4)
    held = attention_forward(q, kvs, bias_row, 0, 2)
    f_two, f_two_end, one_x, one_y, *held = fence(f_two, f_two_end, one_x, one_y, *held)
    f_three_end = along(f_two, OUTWARD)
    f_two = jnp.where(middle, f_two, f_two_end)
    two_x, two_y = swap(f_two, 2), swap(f_two, 4)
    one_d1, one_d2 = swap(one_y[:fp], 2), swap(one_x[fp:], 4)
    held = attention_forward(q, kvs, bias_row, 2, 2, held)
    f_three_end, one_d1, one_d2, two_x, two_y, *held = fence(
        f_three_end, one_d1, one_d2, two_x, two_y, *held
    )
    f_three = jnp.where(middle, f_far, f_three_end)
    three_x, three_y = swap(f_three, 2), swap(f_three, 4)
    two_d1, two_d2 = swap(two_y[:fp], 2), swap(two_x[fp:], 4)

    def moves(j, block):
        own, by_x, by_y, d1, d2 = block
        last = (d1, d2, fp if d1 is d2 else 0)
        sources = [(own, own, fp), (by_x, by_x, fp), (by_y, by_y, fp), last]
        for i, (a, b, at) in enumerate(sources):
            yield (a, 0, fp, 0, (4 * i + j) * fp)
            yield (b, at, fp, 1, (4 * i + j) * fp)

    own = []
    for i in range(4):
        own.append((up_own, i * fp, fp, 0, 4 * i * fp))
        own.append((down_own, i * fp, fp, 1, 4 * i * fp))
    one = moves(1, (f_one, one_x, one_y, one_d1, one_d2))
    w_ff = put_rows([*own, *one], (ff * 2, width), 2)
    w_ff = fence(*w_ff, *held)
    w_ff, held = w_ff[:2], w_ff[2:]
    held = attention_forward(q, kvs, bias_row, 4, 2, held)
    two_d1, two_d2, three_x, three_y, *held = fence(two_d1, two_d2, three_x, three_y, *held)
    three_d1, three_d2 = swap(three_y[:fp], 2), swap(three_x[fp:], 4)
    held = attention_forward(q, kvs, bias_row, 6, 2, held)
    three_d1, three_d2, *held = fence(three_d1, three_d2, *held)
    attended, lse = held
    first_sum = up(tokens) + mm(attended, wo, NN)
    unit_one, root_one = centred(first_sum)
    normed = unit_one * gain_one
    normed_low = normed.astype(BF)

    two = moves(2, (f_two, two_x, two_y, two_d1, two_d2))
    three = moves(3, (f_three, three_x, three_y, three_d1, three_d2))
    wu, wd = put_rows([*two, *three], (ff * 2, width), 2, w_ff)

    normed_peer = swap(normed_low, 1)
    gathered_peer = [swap(part, 1) for part in gathered]
    attended_peer = swap(attended[:, width // 2 :], 1)
    act, slope = gelu_tile(mm(normed_low, wu, NT))
    act_peer, slope_peer = gelu_tile(mm(normed_peer, wu, NT))
    shrunk_peer = swap(mm(act_peer, wd, NN, BF), 1)
    unit_two, root_two = centred(normed + mm(act, wd, NN) + up(shrunk_peer))
    mixed = (unit_two * gain_two).astype(BF)

    grad_second, gain_grad_two = norm_pull(up(cotangent), gain_two, unit_two, root_two)
    second_low = grad_second.astype(BF)
    second_peer = swap(second_low, 1)
    grad_exp = (mm(second_low, wd, NT) * up(slope)).astype(BF)
    grad_exp_peer = (mm(second_peer, wd, NT) * up(slope_peer)).astype(BF)
    normed_part_peer = swap(mm(grad_exp_peer, wu, NN, BF), 1)
    normed_part = mm(grad_exp, wu, NN)
    twos = outer_four(act, second_low, act_peer, second_peer)
    normed_part, normed_part_peer, *twos = fence(normed_part, normed_part_peer, *twos)
    diag_y, two_y = swap(twos[3], 4), swap(twos[2], 4)
    ones = outer_four(grad_exp, normed_low, grad_exp_peer, normed_peer)
    grad_normed = grad_second + normed_part + up(normed_part_peer)
    normed_part, *ones = fence(normed_part, *ones)
    diag_x, one_x = swap(ones[3], 2), swap(ones[1], 2)
    grad_first, gain_grad_one = norm_pull(grad_normed, gain_one, unit_one, root_one)
    first_low = grad_first.astype(BF)
    first_peer = swap(first_low, 1)
    go = mm(first_low, wo, NT, BF)
    core = width // 2
    go, first_peer, attended_peer, *gathered_peer = fence(
        go, first_peer, attended_peer, *gathered_peer
    )

    def pull(n, held):
        keys = bias_cols[2 * n * rows : 2 * (n + 1) * rows]
        *held, send, part = attention_backward(
            q, kvs[n], go, attended, lse, keys, wkv, n, 2, held
        )
        return held, send, part

    def line_sum(part):
        return lax.psum_scatter(part, "tp", scatter_dimension=0, tiled=True)

    gains = jnp.stack([gain_grad_one, gain_grad_two])
    gains_came = swap(gains, 1)
    held, send, part = pull(0, None)
    diag_x, diag_y, one_x, two_y, send, part, gains_came, *held = fence(
        diag_x, diag_y, one_x, two_y, send, part, gains_came, *held
    )
    upper_sum = line_sum(part)
    came = [swap(send, 1)]
    gains = gains + gains_came
    gains_came = swap(gains, 2)
    two_x = (up(twos[1]) + up(diag_y)).astype(BF)
    one_y = (up(ones[2]) + up(diag_x)).astype(BF)
    two_x, one_y, *held = fence(two_x, one_y, *held)
    two_x, one_y = swap(two_x, 2), swap(one_y, 4)
    held, send, part = pull(1, held)
    two_x, one_y, came[0], send, part, gains_came, *held = fence(
        two_x, one_y, came[0], send, part, gains_came, *held
    )
    gq, gk, gv = held
    gq_peer = swap(gq[:, core:], 1)
    gains = gains + gains_came
    gains_came = swap(gains, 4)
    part = part.reshape(4, 2, upper // 2, width)
    part_one, part_two = [part[:, n].reshape(rows, width) for n in range(2)]
    lower_one = line_sum(part_one)
    ff_total = plane.higher(totals((ones[0], one_x, one_y), (twos[0], two_x, two_y), t))
    upper_sum, ff_total = fence(upper_sum, ff_total)
    ff_total = line_sum(ff_total)
    gq_peer, gains_came, send = fence(gq_peer, gains_came, send)
    came.append(swap(send, 1))
    gains = plane.higher_exact(gains + gains_came)
    coarse = lax.reduce_precision(gains, exponent_bits=8, mantissa_bits=7)
    gains = jnp.concatenate([coarse, gains - coarse, jnp.zeros((12, width), F32)]).astype(BF)
    light = head_grads(
        [gq, gq_peer, attended, attended_peer],
        [],
        [tokens, tokens_peer, first_low, first_peer],
        False,
        (0, 1, 4, 5, 2, 3, 6, 7),
    )
    came[1], *light = fence(came[1], *light)
    to_x, to_y = swap(light[0], 2), swap(light[1], 4)
    heavy = head_grads([gk, gv], came, [*gathered, *gathered_peer], True)
    to_x, to_y, gq, *heavy = fence(to_x, to_y, gq, *heavy)
    half = 4 * qp
    add = lambda *arrays: sum(up(a) for a in arrays).astype(BF)

    def second_hop(parts, to_x, to_y):
        return add(parts[2], to_y[:half]), add(parts[3], to_x[:half])

    def mine_of(parts, to_x, to_y, on_x, on_y):
        own = parts[4]
        total = [add(own[:half], to_x[half:], on_y), add(own[half:], to_y[half:], on_x)]
        return plane.higher(jnp.concatenate(total)).reshape(4, 2 * qp, width)

    next_x, next_y = second_hop(light, to_x, to_y)
    next_x, next_y, *heavy = fence(next_x, next_y, *heavy)
    on_x, on_y = swap(next_x, 2), swap(next_y, 4)
    far_x, far_y = swap(heavy[0], 2), swap(heavy[1], 4)
    first = mm(gq, wq, NN) + grad_first
    on_x, on_y, far_x, far_y, first = fence(on_x, on_y, far_x, far_y, first)
    next_x, next_y = second_hop(heavy, far_x, far_y)
    next_x, next_y, ff_total = fence(next_x, next_y, ff_total)
    last_x, last_y = swap(next_x, 2), swap(next_y, 4)
    f_x, f_y = swap(ff_total, 2), swap(ff_total, 4)
    light_mine = mine_of(light, to_x, to_y, on_x, on_y)
    last_x, last_y, light_mine = fence(last_x, last_y, light_mine)
    heavy_mine = mine_of(heavy, far_x, far_y, last_x, last_y)
    a_mine = jnp.concatenate([light_mine, heavy_mine], axis=1)
    pairs = a_mine.reshape(2, 2, 4 * qp, width)
    pairs = jnp.where((t & 1) == 1, pairs[:, ::-1], pairs)
    a_mine = jnp.where((t & 2) == 2, pairs[::-1], pairs).reshape(a_mine.shape)
    gains = jnp.broadcast_to(gains[None], (4, 16, width))
    a_mine = fence(jnp.concatenate([a_mine, gains], axis=1))[0]
    a_came = lax.all_to_all(a_mine, "tp", split_axis=0, concat_axis=0, tiled=True)
    f_core = [swap(ff_total, 1)]
    f_d1, f_d2 = swap(f_y[:fp], 2), swap(f_x[fp:], 4)
    f_core += [swap(f_x, 1), swap(f_y, 1)]
    a_came, part_two, f_d1, f_d2, b0, b1, b2 = fence(a_came, part_two, f_d1, f_d2, *f_core)
    f_core = [b0, b1, b2]
    lower_two = line_sum(part_two)
    a_total = fence(jnp.sum(up(a_came[:, : 4 * qp]), axis=0).astype(BF))[0]
    gains = jnp.sum(up(a_came[:, 4 * qp : 4 * qp + 4]), axis=0)
    gains = gains[:2] + gains[2:]
    a_four = [a_total, swap(a_total, 2), swap(a_total, 4), swap(a_total, 6)]
    a_core = [swap(a_total, 1)]
    f_core += [swap(f_d1, 1), swap(f_d2, 1)]
    f_four = [ff_total, f_x, f_y, f_d1, f_d2]
    ups, downs = [], []
    for i in range(8):
        part = f_core if i & 1 else f_four
        ups.append((part[i >> 1], 0))
        downs.append((part[i >> 1], 1) if i < 6 else (part[4], 0))
    grad_up = placed(ups, fp, s8, True)
    grad_down = placed(downs, fp, s8, False)
    grad_up, grad_down, *a_four = fence(grad_up, grad_down, *a_four)
    a_core += [swap(a, 1) for a in a_four[1:]]
    a_all = [(a_core if i & 1 else a_four)[i >> 1] for i in range(8)]
    grad_qkv, grad_out = heads_placed(a_all, s8)
    tokens_grad = (first + up(jnp.concatenate([upper_sum, lower_one, lower_two]))).astype(BF)
    return (
        mixed,
        tokens_grad,
        grad_qkv.transpose(1, 0, 2),
        grad_out,
        grad_up,
        grad_down,
        gains[0],
        gains[1],
    )


def solution(mesh):
    rows = P(("seq", "tp"), None)
    weights = (P(None, None, "tp"), P("tp", None), P(None, "tp"), P("tp", None), P(), P())
    return jax.shard_map(
        functools.partial(per_device, mesh.shape["seq"]),
        mesh=mesh,
        in_specs=(rows,) + weights + (rows, P("seq"), P("seq", None)),
        out_specs=(rows, rows) + weights,
        check_vma=False,
    )
```

```python
import functools

import jax
import jax.numpy as jnp
from jax import lax
from jax.experimental import pallas as pl
from jax.experimental.pallas import tpu as pltpu
from jax.sharding import PartitionSpec as P

HEAD = 64
SLOTS = 4
BF = jnp.bfloat16
F32 = jnp.float32
LOG2E = 1.4426950408889634
LN_EPS = 1e-5
LIGHT = pl.CostEstimate(flops=10**9, bytes_accessed=10**6, transcendentals=0)
NT = (((1,), (1,)), ((), ()))
NN = (((1,), (0,)), ((), ()))
TN = (((0,), (0,)), ((), ()))

PAIR = [(0, 1), (1, 0), (2, 3), (3, 2)]
MIDDLE = [(1, 2), (2, 1)]
OUTWARD = [(1, 0), (2, 3)]


def in_hbm(*arrays):
    return [pltpu.with_memory_space_constraint(a, pltpu.HBM) for a in arrays]


def mm(a, b, dims, out=F32):
    return lax.dot_general(a, b, dims, preferred_element_type=F32).astype(out)


def along(array, pairs):
    return lax.ppermute(array, "tp", pairs)


def fence(*arrays):
    return lax.optimization_barrier(arrays)


class Plane:
    def __init__(self, size):
        self.size = size

    def swap(self, array, bit):
        return lax.ppermute(array, "seq", [(i, i ^ bit) for i in range(self.size)])

    def higher_exact(self, total):
        bit = 8
        while bit < self.size:
            total = total + self.swap(total, bit)
            bit *= 2
        return total

    def higher(self, total):
        bit = 8
        while bit < self.size:
            total = (total.astype(F32) + self.swap(total, bit).astype(F32)).astype(BF)
            bit *= 2
        return total


def forward_kernel(blocks, q_ref, *refs):
    k_refs, v_refs = refs[:blocks], refs[blocks : 2 * blocks]
    bias_ref, out_ref, lse_ref = refs[2 * blocks], refs[-2], refs[-1]
    scale = HEAD**-0.5 * LOG2E
    rows = q_ref.shape[0]
    lane = lax.broadcasted_iota(jnp.int32, (1, 2 * HEAD), 1)
    zero = jnp.zeros((), BF)
    keys = jnp.concatenate([ref[...] for ref in k_refs])
    values = jnp.concatenate([ref[...] for ref in v_refs])
    bias = bias_ref[...]
    sub = 256
    mine = [(lane < HEAD) == (head == 0) for head in range(2)]
    k = [jnp.where(m, keys, zero) for m in mine]
    v = [jnp.where(m, values, zero) for m in mine]
    for at in range(rows // sub):
        span = pl.ds(at * sub, sub)
        q = q_ref[span, :]
        outs, lses = [], []
        for head in range(2):
            s = lax.dot_general(q, k[head], NT, preferred_element_type=F32)
            s = s * scale + bias
            top = jnp.max(s, axis=1, keepdims=True)
            p = jnp.exp2(s - top)
            total = jnp.sum(p, axis=1, keepdims=True)
            o = lax.dot_general(p.astype(BF), v[head], NN, preferred_element_type=F32)
            outs.append(o / total)
            lses.append(top + jnp.log2(total))
        out_ref[span, :] = (outs[0] + outs[1]).astype(BF)
        wide = jnp.where(lane < HEAD, lses[0], lses[1])
        flat = jnp.transpose(wide)
        lse_ref[0, :, span] = jnp.concatenate(
            [flat[0:1], flat[HEAD : HEAD + 1]], axis=0
        )


def attention_forward(q, kvs, bias, first, count, held=()):
    rows, width = q.shape
    keys = bias.shape[1]
    pairs = width // (2 * HEAD)
    wide = 2 * HEAD
    at = lambda shift: lambda h: (0, h + first + shift)
    return pl.pallas_call(
        functools.partial(forward_kernel, len(kvs)),
        grid=(count,),
        in_specs=[pl.BlockSpec((rows, wide), at(0))]
        + [pl.BlockSpec((kv.shape[0], wide), at(0)) for kv in kvs]
        + [pl.BlockSpec((kv.shape[0], wide), at(pairs)) for kv in kvs]
        + [pl.BlockSpec((1, keys), lambda h: (0, 0))]
        + [pl.BlockSpec(memory_space=pl.ANY)] * len(held),
        out_specs=[
            pl.BlockSpec((rows, wide), at(0)),
            pl.BlockSpec((1, 2, rows), lambda h: (h + first, 0, 0)),
        ],
        out_shape=[
            jax.ShapeDtypeStruct((rows, width), BF),
            jax.ShapeDtypeStruct((pairs, 2, rows), F32),
        ],
        input_output_aliases={2 * len(kvs) + 2 + n: n for n in range(len(held))},
        compiler_params=pltpu.CompilerParams(vmem_limit_bytes=24 * 2**20),
        cost_estimate=LIGHT,
        name="attention_forward",
    )(q, *kvs, *kvs, bias, *held)


def backward_kernel(
    q_ref, k_ref, v_ref, go_ref, att_ref, lse_ref, bias_ref, wkv_ref, *refs
):
    add_ref = refs[0] if len(refs) == 9 else None
    gq_ref, keep_k_ref, keep_v_ref, send_ref, part_ref, all_ref = refs[-6:]
    step, pairs = pl.program_id(0), pl.num_programs(0)
    scale = HEAD**-0.5
    wide = 2 * HEAD
    keys = k_ref.shape[0]
    lane = lax.broadcasted_iota(jnp.int32, (1, wide), 1)
    q, go = q_ref[...], go_ref[...]
    zero = jnp.zeros((), BF)
    mine = [(lane < HEAD) == (head == 0) for head in range(2)]
    qs = [jnp.where(m, q, zero) for m in mine]
    gos = [jnp.where(m, go, zero) for m in mine]
    product = go.T.astype(F32) * att_ref[...].T.astype(F32)
    inner = [
        jnp.sum(product[head * HEAD : (head + 1) * HEAD], axis=0, keepdims=True)
        for head in range(2)
    ]
    total_q = [0.0, 0.0]
    gks, gvs = [], []
    sub = 512
    for at in range(keys // sub):
        span = pl.ds(at * sub, sub)
        bias = bias_ref[span, 0:1]
        keys_t = k_ref[span, :].T
        total_k, total_v = 0.0, 0.0
        for head in range(2):
            k = jnp.where(mine[head], k_ref[span, :], zero)
            v = jnp.where(mine[head], v_ref[span, :], zero)
            s = lax.dot_general(k, q, NT, preferred_element_type=F32)
            p = jnp.exp2(s * (scale * LOG2E) + (bias - lse_ref[0, head : head + 1, :]))
            gp = lax.dot_general(v, go, NT, preferred_element_type=F32)
            gs = (p * (gp - inner[head])).astype(BF)
            total_v += lax.dot_general(p.astype(BF), gos[head], NN, preferred_element_type=F32)
            total_k += lax.dot_general(gs, qs[head], NN, preferred_element_type=F32)
            own_keys = keys_t[head * HEAD : (head + 1) * HEAD]
            total_q[head] += lax.dot_general(own_keys, gs, NN, preferred_element_type=F32)
        gks.append((total_k * scale).astype(BF))
        gvs.append(total_v.astype(BF))
    gk, gv = jnp.concatenate(gks), jnp.concatenate(gvs)
    gq = jnp.concatenate(total_q).T * scale
    gq_ref[...] = (gq if add_ref is None else gq + add_ref[...]).astype(gq_ref.dtype)
    half = pairs // 2

    @pl.when(step < half)
    def _():
        keep_k_ref[...] = gk
        keep_v_ref[...] = gv

    @pl.when(step >= half)
    def _():
        send_ref[0] = gk
        send_ref[1] = gv

    lanes = pl.multiple_of(step * wide, wide)
    all_ref[:, pl.ds(lanes, wide)] = gk
    all_ref[:, pl.ds(pl.multiple_of(lanes + q_width(part_ref), wide), wide)] = gv

    @pl.when(step == pairs - 1)
    def _():
        for at in range(keys // 256):
            span = pl.ds(at * 256, 256)
            part = lax.dot_general(
                all_ref[span, :], wkv_ref[...], NN, preferred_element_type=F32
            )
            part_ref[span, :] = part.astype(BF)


def q_width(part_ref):
    return part_ref.shape[1]


def attention_backward(q, kv, go, attended, lse, bias, wkv, block, blocks, held):
    rows, width = q.shape
    keys = kv.shape[0]
    pairs = width // (2 * HEAD)
    wide = 2 * HEAD
    half = pairs // 2
    by_pair = pl.BlockSpec((rows, wide), lambda h: (0, h))
    stats = pl.BlockSpec((1, 2, rows), lambda h: (h, 0, 0))
    whole = pl.BlockSpec(memory_space=pl.ANY)
    keep = pl.BlockSpec((keys, wide), lambda h: (block, jnp.minimum(h, half - 1)))
    send = pl.BlockSpec((2, keys, wide), lambda h: (0, 0, jnp.maximum(h - half, 0)))
    return pl.pallas_call(
        backward_kernel,
        grid=(pairs,),
        in_specs=[
            by_pair,
            pl.BlockSpec((keys, wide), lambda h: (0, h)),
            pl.BlockSpec((keys, wide), lambda h: (0, h + pairs)),
            by_pair,
            by_pair,
            stats,
            pl.BlockSpec((keys, 128), lambda h: (0, 0)),
            pl.BlockSpec((2 * width, width), lambda h: (0, 0), pipeline_mode=pl.Buffered(1)),
        ]
        + ([by_pair, whole, whole] if held else []),
        out_specs=[by_pair, keep, keep, send, pl.BlockSpec((keys, width), lambda h: (0, 0))],
        out_shape=[
            jax.ShapeDtypeStruct((rows, width), BF if held else F32),
            jax.ShapeDtypeStruct((blocks * keys, width // 2), BF),
            jax.ShapeDtypeStruct((blocks * keys, width // 2), BF),
            jax.ShapeDtypeStruct((2, keys, width // 2), BF),
            jax.ShapeDtypeStruct((keys, width), BF),
        ],
        scratch_shapes=[pltpu.VMEM((keys, 2 * width), BF)],
        input_output_aliases={9: 1, 10: 2} if held else {},
        compiler_params=pltpu.CompilerParams(vmem_limit_bytes=48 * 2**20),
        cost_estimate=LIGHT,
        name="attention_backward",
    )(*in_hbm(q, kv, kv, go, attended), lse, bias, *in_hbm(wkv, *(held or ())))


def gelu_tile(x):
    size = jnp.abs(x)
    t = 1.0 / (1.0 + size * (0.3275911 * 0.5**0.5))
    poly = t * (
        0.127414796
        + t * (-0.142248368 + t * (0.7107068705 + t * (-0.7265760135 + t * 0.5307027145)))
    )
    bell = jnp.exp2(x * x * (-0.5 * LOG2E))
    tail = poly * bell
    cdf = jnp.where(x >= 0, 1.0 - tail, tail)
    return (x * cdf).astype(BF), (cdf + x * (bell * 0.3989422804014327)).astype(BF)


def head_grads_kernel(many, *refs):
    ins, (x_ref, y_ref, near_x_ref, near_y_ref, own_ref) = refs[:-5], refs[-5:]

    def outer(left, right):
        return lax.dot_general(left, right, TN, preferred_element_type=F32)

    if many:
        big_refs, came_refs, row_refs = ins[:2], ins[2:4], ins[4:]
        keys = row_refs[0].shape[0]
        totals_of = []
        for kind in range(2):
            total = 0.0
            for n in range(2):
                part = slice(n * keys, (n + 1) * keys)
                total += outer(big_refs[kind][part, :], row_refs[n][...])
                total += outer(came_refs[n][kind], row_refs[2 + n][...])
            totals_of.append(total.astype(BF))
    else:
        totals_of = []
        for kind in range(2):
            left, left_peer, right, right_peer = [ref[...] for ref in ins[4 * kind : 4 * kind + 4]]
            totals_of.append((outer(left, right) + outer(left_peer, right_peer)).astype(BF))
    size = HEAD // 2

    def chunk(n):
        rows = []
        for at in range(totals_of[0].shape[0] // (4 * size)):
            source = (at * 4 + (n & 1) * 2 + (n >> 1)) * size
            rows += [total[source : source + size] for total in totals_of]
        return jnp.concatenate(rows)

    half = own_ref.shape[0]
    own_ref[...] = chunk(0)

    @pl.when(pl.program_id(0) == 0)
    def _():
        x_ref[:half, :] = chunk(3)
        x_ref[half:, :] = chunk(1)
        near_y_ref[...] = chunk(2)

    @pl.when(pl.program_id(0) == 1)
    def _():
        y_ref[:half, :] = chunk(3)
        y_ref[half:, :] = chunk(2)
        near_x_ref[...] = chunk(1)


def head_grads(columns, arrived, whole_arrays, many, order=None):
    width = whole_arrays[0].shape[1]
    wide = width // 4
    half = wide // 2
    by_column = [pl.BlockSpec((a.shape[0], wide), lambda g: (0, g)) for a in columns]
    by_kind = [pl.BlockSpec((2, a.shape[1], wide), lambda g: (0, 0, g)) for a in arrived]
    whole = [
        pl.BlockSpec(a.shape, lambda g: (0, 0), pipeline_mode=pl.Buffered(1))
        for a in whole_arrays
    ]
    args, specs = [*columns, *arrived, *whole_arrays], by_column + by_kind + whole
    if order:
        args, specs = [args[n] for n in order], [specs[n] for n in order]
    fixed = lambda rows: pl.BlockSpec((rows, width), lambda g: (0, 0))
    shape = lambda rows: jax.ShapeDtypeStruct((rows, width), BF)
    return pl.pallas_call(
        functools.partial(head_grads_kernel, many),
        grid=(2,),
        in_specs=specs,
        out_specs=[fixed(wide), fixed(wide), fixed(half), fixed(half)]
        + [pl.BlockSpec((half, width), lambda g: (g, 0))],
        out_shape=[shape(wide), shape(wide), shape(half), shape(half), shape(wide)],
        compiler_params=pltpu.CompilerParams(vmem_limit_bytes=48 * 2**20),
        cost_estimate=LIGHT,
        name="head_grads",
    )(*in_hbm(*args))


def rows_kernel(moves, n_held, n_out, *refs):
    n_in = len(refs) - n_held - n_out - 1
    ins, outs, sems = refs[:n_in], refs[-1 - n_out : -1], refs[-1]
    copies = []
    for n, (source, at, count, out, place) in enumerate(moves):
        copies.append(
            pltpu.make_async_copy(
                ins[source].at[pl.ds(at, count), :],
                outs[out].at[pl.ds(place, count), :],
                sems.at[n],
            )
        )
    for copy in copies:
        copy.start()
    for copy in copies:
        copy.wait()


def put_rows(moves, shape, n_out, held=()):
    arrays, listed = [], []
    for array, at, count, out, place in moves:
        known = [n for n, a in enumerate(arrays) if a is array]
        if not known:
            arrays.append(array)
        listed.append((known[0] if known else len(arrays) - 1, at, count, out, place))
    whole = pl.BlockSpec(memory_space=pl.ANY)
    return pl.pallas_call(
        functools.partial(rows_kernel, listed, len(held), n_out),
        in_specs=[pl.BlockSpec(memory_space=pltpu.VMEM)] * len(arrays) + [whole] * len(held),
        out_specs=[whole] * n_out,
        out_shape=[jax.ShapeDtypeStruct(shape, BF)] * n_out,
        scratch_shapes=[pltpu.SemaphoreType.DMA((len(listed),))],
        input_output_aliases={len(arrays) + n: n for n in range(len(held))},
        compiler_params=pltpu.CompilerParams(vmem_limit_bytes=32 * 2**20),
        cost_estimate=LIGHT,
        name="put_rows",
    )(*arrays, *held)


def totals_kernel(at_ref, *refs):
    *ins, out_ref = refs
    size = ins[0].shape[0]
    for n in range(2):
        a, b, c = [ref[...].astype(F32) for ref in ins[3 * n : 3 * n + 3]]
        out_ref[n * size : (n + 1) * size, :] = (a + b + c).astype(BF)


def totals(ones, twos, t):
    rows, width = ones[0].shape
    size = rows // 4
    return pl.pallas_call(
        totals_kernel,
        grid_spec=pltpu.PrefetchScalarGridSpec(
            num_scalar_prefetch=1,
            grid=(4,),
            in_specs=[pl.BlockSpec((size, width), lambda u, at: (at[0] ^ u, 0))] * 6,
            out_specs=pl.BlockSpec((2 * size, width), lambda u, at: (u, 0)),
        ),
        out_shape=jax.ShapeDtypeStruct((2 * rows, width), BF),
        cost_estimate=LIGHT,
        name="totals",
    )(t[None].astype(jnp.int32), *ones, *twos)


def outer_kernel(left_ref, right_ref, left_two_ref, right_two_ref, *out_refs):
    total = lax.dot_general(left_ref[...], right_ref[...], TN, preferred_element_type=F32)
    total += lax.dot_general(
        left_two_ref[...], right_two_ref[...], TN, preferred_element_type=F32
    )
    total = total.astype(BF)
    each = pl.num_programs(0) // len(out_refs)
    for n, out_ref in enumerate(out_refs):

        @pl.when(pl.program_id(0) // each == n)
        def _():
            out_ref[...] = total


def outer_four(left, right, left_two, right_two):
    rows, hidden = left.shape
    width = right.shape[1]
    tile = 512
    each = hidden // (4 * tile)
    columns = pl.BlockSpec((rows, tile), lambda i: (0, i))
    whole = pl.BlockSpec((rows, width), lambda i: (0, 0))
    place = lambda n: lambda i: (jnp.clip(i - n * each, 0, each - 1), 0)
    return pl.pallas_call(
        outer_kernel,
        grid=(hidden // tile,),
        in_specs=[columns, whole, columns, whole],
        out_specs=[pl.BlockSpec((tile, width), place(n)) for n in range(4)],
        out_shape=[jax.ShapeDtypeStruct((hidden // 4, width), BF)] * 4,
        compiler_params=pltpu.CompilerParams(vmem_limit_bytes=32 * 2**20),
        cost_estimate=LIGHT,
        name="outer_four",
    )(left, right, left_two, right_two)


def reverse(i):
    return ((i & 1) << 2) | (i & 2) | (i >> 2)


def heads_placed_kernel(at_ref, *refs):
    *pieces, turned_ref, plain_ref, whole_ref = refs
    step, last = pl.program_id(0), pl.num_programs(0) - 1
    for i, piece in enumerate(pieces):
        place = reverse(at_ref[0] ^ i)
        size = piece.shape[0]
        whole_ref[pl.ds(pl.multiple_of(place * size, size), size), :] = piece[...]

    @pl.when(step < last)
    def _():
        turned_ref[0] = whole_ref[...].T.astype(F32)

    @pl.when(step == last)
    def _():
        plain_ref[...] = whole_ref[...].astype(F32)


def heads_placed(pieces, s8):
    kind_at = lambda n: jnp.where(n == 0, 0, jnp.where(n == 3, 1, n + 1))
    width = pieces[0].shape[1]
    size = pieces[0].shape[0] // 4
    rows = 8 * size
    return pl.pallas_call(
        heads_placed_kernel,
        grid=(4,),
        in_specs=[pl.BlockSpec(memory_space=pltpu.SMEM)]
        + [pl.BlockSpec((size, width), lambda n: (kind_at(n), 0)) for _ in pieces],
        out_specs=[
            pl.BlockSpec((1, width, rows), lambda n: (jnp.minimum(n, 2), 0, 0)),
            pl.BlockSpec((rows, width), lambda n: (0, 0)),
        ],
        out_shape=[
            jax.ShapeDtypeStruct((3, width, rows), F32),
            jax.ShapeDtypeStruct((rows, width), F32),
        ],
        scratch_shapes=[pltpu.VMEM((rows, width), BF)],
        compiler_params=pltpu.CompilerParams(vmem_limit_bytes=32 * 2**20),
        cost_estimate=LIGHT,
        name="heads_placed",
    )(s8[None].astype(jnp.int32), *pieces)


def placed_kernel(flips, at_ref, *refs):
    *pieces, out_ref, whole_ref = refs
    for i, piece in enumerate(pieces):
        place = at_ref[0] ^ i
        size = piece.shape[0]
        whole_ref[pl.ds(pl.multiple_of(place * size, size), size), :] = piece[...]
    out = whole_ref[...]
    out = out.T if flips else out
    out_ref[...] = out.astype(F32)


def placed(pieces, size, s8, flips):
    width = pieces[0][0].shape[1]
    tile = 512
    rows = 8 * size
    if flips:
        out_shape, out_spec = (width, rows), pl.BlockSpec((tile, rows), lambda c: (c, 0))
    else:
        out_shape, out_spec = (rows, width), pl.BlockSpec((rows, tile), lambda c: (0, c))
    part = lambda first: pl.BlockSpec((size, tile), lambda c: (first, c))
    return pl.pallas_call(
        functools.partial(placed_kernel, flips),
        grid=(width // tile,),
        in_specs=[pl.BlockSpec(memory_space=pltpu.SMEM)] + [part(first) for _, first in pieces],
        out_specs=out_spec,
        out_shape=jax.ShapeDtypeStruct(out_shape, F32),
        scratch_shapes=[pltpu.VMEM((rows, tile), BF)],
        compiler_params=pltpu.CompilerParams(vmem_limit_bytes=32 * 2**20),
        cost_estimate=LIGHT,
        name="placed",
    )(s8[None].astype(jnp.int32), *[array for array, _ in pieces])


def centred(values):
    centre = values - jnp.mean(values, axis=-1, keepdims=True)
    root = lax.rsqrt(jnp.mean(centre * centre, axis=-1, keepdims=True) + LN_EPS)
    return centre * root, root


def norm_pull(grad, gain, unit, root):
    scaled = grad * gain
    mean = jnp.mean(scaled, axis=-1, keepdims=True)
    slope = jnp.mean(scaled * unit, axis=-1, keepdims=True)
    return root * (scaled - mean - unit * slope), jnp.sum(grad * unit, axis=0)


def per_device(
    seq_size, tokens, w_qkv, w_out, w_up, w_down, gain_one, gain_two, cotangent, bucket, lengths
):
    rows, width = tokens.shape
    t = lax.axis_index("tp")
    middle = (t == 1) | (t == 2)
    s8 = lax.axis_index("seq") % 8
    plane = Plane(seq_size)
    swap = plane.swap
    hid = w_out.shape[0]
    ff = w_down.shape[0]
    qp, fp = hid // 8, ff // 8
    up = lambda a: a.astype(F32)
    across = lambda a, j: along(a, [(i, i ^ j) for i in range(4)])

    w_attn_own = jnp.concatenate([w_qkv.transpose(1, 2, 0), w_out[None]])

    def attn_piece(i):
        return lax.dynamic_slice_in_dim(w_attn_own, reverse(s8 ^ i) * qp, qp, axis=1)

    def up_piece(i):
        return lax.dynamic_slice_in_dim(w_up, (s8 ^ i) * fp, fp, axis=1).T

    def down_piece(i):
        return lax.dynamic_slice_in_dim(w_down, (s8 ^ i) * fp, fp, axis=0)

    attn_own = attn_piece(0).reshape(4 * qp, width)
    up_own = jnp.concatenate([up_piece(2 * i) for i in range(4)])
    down_own = jnp.concatenate([down_piece(2 * i) for i in range(4)])
    ff_own = jnp.concatenate([up_own[:fp], down_own[:fp]])

    upper = rows // 2
    gathered = [
        lax.all_gather(tokens[n * upper : (n + 1) * upper], "tp", axis=0, tiled=True)
        for n in range(2)
    ]
    a_far = [across(attn_own, j) for j in (1, 2, 3)]
    whole = bucket[0] == 1
    place = jnp.arange(rows, dtype=jnp.int32)
    seen = []
    for u in range(4):
        alone = jnp.where(t == u, lengths[0, u], 0)
        limit = jnp.where(whole, lengths[0, 0] - u * rows, alone)
        seen.append((place < limit).reshape(2, upper))
    bias = jnp.where(jnp.stack(seen, axis=1), 0.0, -1e9).astype(F32).reshape(4 * rows)
    bias, *a_far = fence(bias, *a_far)
    bias_cols = jnp.broadcast_to(bias[:, None], (4 * rows, 128))

    attn_three = jnp.concatenate(a_far)
    half = attn_three.shape[0] // 2
    a_x, a_y = swap(attn_three, 2), swap(attn_three, 4)
    attn_three, a_x, a_y = fence(attn_three, a_x, a_y)
    a_d1, a_d2 = swap(a_y[:half], 2), swap(a_x[half:], 4)
    others = [swap(attn_three, 1), swap(a_x, 1), swap(a_y, 1)]
    a_d1, a_d2, *others = fence(a_d1, a_d2, *others)
    others += fence(swap(a_d1, 1), swap(a_d2, 1))

    four = [attn_three, a_x, a_y, a_d1, a_d2]
    pieces = []
    for i in range(8):
        part = others if i & 1 else four
        far = part[i >> 1] if i < 6 else jnp.concatenate(part[3:])
        pieces.append(jnp.concatenate([attn_piece(i)[None], far.reshape(3, 4, qp, width)]))
    w_attn = jnp.stack(pieces).reshape(2, 2, 2, 4, 4, qp, width).transpose(4, 2, 3, 1, 0, 5, 6)
    w_attn = w_attn.reshape(4, width, width)
    wq, wk, wv, wo = [w_attn[n] for n in range(4)]
    wkv = w_attn[1:3].reshape(2 * width, width)

    wq, wkv, ff_own, up_own, down_own = fence(wq, wkv, ff_own, up_own, down_own)
    f_one, f_far = along(ff_own, PAIR), along(ff_own, MIDDLE)
    q = mm(tokens, wq, NT, BF)
    upper_kv = mm(gathered[0], wkv, NT, BF)
    f_one, f_far, q, upper_kv = fence(f_one, f_far, q, upper_kv)
    f_two, f_two_end = along(f_one, MIDDLE), along(f_far, OUTWARD)
    one_x, one_y = swap(f_one, 2), swap(f_one, 4)
    tokens_peer = swap(tokens, 1)
    f_two, f_two_end, one_x, one_y, tokens_peer, *kvs = fence(
        f_two, f_two_end, one_x, one_y, tokens_peer, upper_kv, mm(gathered[1], wkv, NT, BF)
    )
    f_three_end = along(f_two, OUTWARD)
    f_two = jnp.where(middle, f_two, f_two_end)
    two_x, two_y = swap(f_two, 2), swap(f_two, 4)
    one_d1, one_d2 = swap(one_y[:fp], 2), swap(one_x[fp:], 4)
    bias_row = bias[None]
    held = attention_forward(q, kvs, bias_row, 0, 3)
    f_three_end, one_d1, one_d2, two_x, two_y, *held = fence(
        f_three_end, one_d1, one_d2, two_x, two_y, *held
    )
    f_three = jnp.where(middle, f_far, f_three_end)
    three_x, three_y = swap(f_three, 2), swap(f_three, 4)
    two_d1, two_d2 = swap(two_y[:fp], 2), swap(two_x[fp:], 4)

    def moves(j, block):
        own, by_x, by_y, d1, d2 = block
        sources = [(own, own, fp), (by_x, by_x, fp), (by_y, by_y, fp), (d1, d2, 0)]
        for i, (a, b, at) in enumerate(sources):
            yield (a, 0, fp, 0, (4 * i + j) * fp)
            yield (b, at, fp, 1, (4 * i + j) * fp)

    own = []
    for i in range(4):
        own.append((up_own, i * fp, fp, 0, 4 * i * fp))
        own.append((down_own, i * fp, fp, 1, 4 * i * fp))
    one = moves(1, (f_one, one_x, one_y, one_d1, one_d2))
    w_ff = put_rows([*own, *one], (ff * 2, width), 2)
    w_ff = fence(*w_ff, *held)
    w_ff, held = w_ff[:2], w_ff[2:]
    held = attention_forward(q, kvs, bias_row, 3, 3, held)
    two_d1, two_d2, three_x, three_y, *held = fence(two_d1, two_d2, three_x, three_y, *held)
    three_d1, three_d2 = swap(three_y[:fp], 2), swap(three_x[fp:], 4)
    held = attention_forward(q, kvs, bias_row, 6, 2, held)
    three_d1, three_d2, *held = fence(three_d1, three_d2, *held)
    attended, lse = held
    first_sum = up(tokens) + mm(attended, wo, NN)
    unit_one, root_one = centred(first_sum)
    normed = unit_one * gain_one
    normed_low = normed.astype(BF)

    two = moves(2, (f_two, two_x, two_y, two_d1, two_d2))
    three = moves(3, (f_three, three_x, three_y, three_d1, three_d2))
    wu, wd = put_rows([*two, *three], (ff * 2, width), 2, w_ff)

    normed_peer = swap(normed_low, 1)
    gathered_peer = [swap(part, 1) for part in gathered]
    attended_peer = swap(attended[:, width // 2 :], 1)
    act, slope = gelu_tile(mm(normed_low, wu, NT))
    act_peer, slope_peer = gelu_tile(mm(normed_peer, wu, NT))
    shrunk_peer = swap(mm(act_peer, wd, NN, BF), 1)
    unit_two, root_two = centred(normed + mm(act, wd, NN) + up(shrunk_peer))
    mixed = (unit_two * gain_two).astype(BF)

    grad_second, gain_grad_two = norm_pull(up(cotangent), gain_two, unit_two, root_two)
    second_low = grad_second.astype(BF)
    second_peer = swap(second_low, 1)
    grad_exp = (mm(second_low, wd, NT) * up(slope)).astype(BF)
    grad_exp_peer = (mm(second_peer, wd, NT) * up(slope_peer)).astype(BF)
    normed_part_peer = swap(mm(grad_exp_peer, wu, NN, BF), 1)
    normed_part = mm(grad_exp, wu, NN)
    twos = outer_four(act, second_low, act_peer, second_peer)
    normed_part, normed_part_peer, *twos = fence(normed_part, normed_part_peer, *twos)
    diag_y, two_y = swap(twos[3], 4), swap(twos[2], 4)
    ones = outer_four(grad_exp, normed_low, grad_exp_peer, normed_peer)
    grad_normed = grad_second + normed_part + up(normed_part_peer)
    normed_part, *ones = fence(normed_part, *ones)
    diag_x, one_x = swap(ones[3], 2), swap(ones[1], 2)
    grad_first, gain_grad_one = norm_pull(grad_normed, gain_one, unit_one, root_one)
    first_low = grad_first.astype(BF)
    first_peer = swap(first_low, 1)
    go = mm(first_low, wo, NT, BF)
    core = width // 2
    go, first_peer, attended_peer, *gathered_peer = fence(
        go, first_peer, attended_peer, *gathered_peer
    )

    def pull(n, held):
        keys = bias_cols[2 * n * rows : 2 * (n + 1) * rows]
        *held, send, part = attention_backward(
            q, kvs[n], go, attended, lse, keys, wkv, n, 2, held
        )
        return held, send, part

    def line_sum(part):
        return lax.psum_scatter(part, "tp", scatter_dimension=0, tiled=True)

    gains = jnp.stack([gain_grad_one, gain_grad_two])
    gains_came = swap(gains, 1)
    held, send, part = pull(0, None)
    diag_x, diag_y, one_x, two_y, send, part, gains_came, *held = fence(
        diag_x, diag_y, one_x, two_y, send, part, gains_came, *held
    )
    upper_sum = line_sum(part)
    came = [swap(send, 1)]
    gains = gains + gains_came
    gains_came = swap(gains, 2)
    two_x = (up(twos[1]) + up(diag_y)).astype(BF)
    one_y = (up(ones[2]) + up(diag_x)).astype(BF)
    two_x, one_y, *held = fence(two_x, one_y, *held)
    two_x, one_y = swap(two_x, 2), swap(one_y, 4)
    held, send, part = pull(1, held)
    two_x, one_y, came[0], send, part, gains_came, *held = fence(
        two_x, one_y, came[0], send, part, gains_came, *held
    )
    gq, gk, gv = held
    gq_peer = swap(gq[:, core:], 1)
    gains = gains + gains_came
    gains_came = swap(gains, 4)
    part = part.reshape(4, 2, upper // 2, width)
    part_one, part_two = [part[:, n].reshape(rows, width) for n in range(2)]
    lower_one = line_sum(part_one)
    ff_total = plane.higher(totals((ones[0], one_x, one_y), (twos[0], two_x, two_y), t))
    upper_sum, ff_total = fence(upper_sum, ff_total)
    ff_total = line_sum(ff_total)
    gq_peer, gains_came, send = fence(gq_peer, gains_came, send)
    came.append(swap(send, 1))
    gains = plane.higher_exact(gains + gains_came)
    coarse = lax.reduce_precision(gains, exponent_bits=8, mantissa_bits=7)
    gains = jnp.concatenate([coarse, gains - coarse, jnp.zeros((12, width), F32)]).astype(BF)
    light = head_grads(
        [gq, gq_peer, attended, attended_peer],
        [],
        [tokens, tokens_peer, first_low, first_peer],
        False,
        (0, 1, 4, 5, 2, 3, 6, 7),
    )
    came[1], *light = fence(came[1], *light)
    to_x, to_y = swap(light[0], 2), swap(light[1], 4)
    heavy = head_grads([gk, gv], came, [*gathered, *gathered_peer], True)
    to_x, to_y, gq, *heavy = fence(to_x, to_y, gq, *heavy)
    half = 4 * qp
    add = lambda *arrays: sum(up(a) for a in arrays).astype(BF)

    def second_hop(parts, to_x, to_y):
        return add(parts[2], to_y[:half]), add(parts[3], to_x[:half])

    def mine_of(parts, to_x, to_y, on_x, on_y):
        own = parts[4]
        total = [add(own[:half], to_x[half:], on_y), add(own[half:], to_y[half:], on_x)]
        return plane.higher(jnp.concatenate(total)).reshape(4, 2 * qp, width)

    next_x, next_y = second_hop(light, to_x, to_y)
    next_x, next_y, *heavy = fence(next_x, next_y, *heavy)
    on_x, on_y = swap(next_x, 2), swap(next_y, 4)
    far_x, far_y = swap(heavy[0], 2), swap(heavy[1], 4)
    first = mm(gq, wq, NN) + grad_first
    on_x, on_y, far_x, far_y, first = fence(on_x, on_y, far_x, far_y, first)
    next_x, next_y = second_hop(heavy, far_x, far_y)
    next_x, next_y, ff_total = fence(next_x, next_y, ff_total)
    last_x, last_y = swap(next_x, 2), swap(next_y, 4)
    f_x, f_y = swap(ff_total, 2), swap(ff_total, 4)
    light_mine = mine_of(light, to_x, to_y, on_x, on_y)
    last_x, last_y, light_mine = fence(last_x, last_y, light_mine)
    heavy_mine = mine_of(heavy, far_x, far_y, last_x, last_y)
    a_mine = jnp.concatenate([light_mine, heavy_mine], axis=1)
    pairs = a_mine.reshape(2, 2, 4 * qp, width)
    pairs = jnp.where((t & 1) == 1, pairs[:, ::-1], pairs)
    a_mine = jnp.where((t & 2) == 2, pairs[::-1], pairs).reshape(a_mine.shape)
    gains = jnp.broadcast_to(gains[None], (4, 16, width))
    a_mine = fence(jnp.concatenate([a_mine, gains], axis=1))[0]
    a_came = lax.all_to_all(a_mine, "tp", split_axis=0, concat_axis=0, tiled=True)
    f_core = [swap(ff_total, 1)]
    f_d1, f_d2 = swap(f_y[:fp], 2), swap(f_x[fp:], 4)
    f_core += [swap(f_x, 1), swap(f_y, 1)]
    a_came, part_two, f_d1, f_d2, b0, b1, b2 = fence(a_came, part_two, f_d1, f_d2, *f_core)
    f_core = [b0, b1, b2]
    lower_two = line_sum(part_two)
    a_total = fence(jnp.sum(up(a_came[:, : 4 * qp]), axis=0).astype(BF))[0]
    gains = jnp.sum(up(a_came[:, 4 * qp : 4 * qp + 4]), axis=0)
    gains = gains[:2] + gains[2:]
    a_four = [a_total, swap(a_total, 2), swap(a_total, 4), swap(a_total, 6)]
    a_core = [swap(a_total, 1)]
    f_core += [swap(f_d1, 1), swap(f_d2, 1)]
    f_four = [ff_total, f_x, f_y, f_d1, f_d2]
    ups, downs = [], []
    for i in range(8):
        part = f_core if i & 1 else f_four
        ups.append((part[i >> 1], 0))
        downs.append((part[i >> 1], 1) if i < 6 else (part[4], 0))
    grad_up = placed(ups, fp, s8, True)
    grad_down = placed(downs, fp, s8, False)
    grad_up, grad_down, *a_four = fence(grad_up, grad_down, *a_four)
    a_core += [swap(a, 1) for a in a_four[1:]]
    a_all = [(a_core if i & 1 else a_four)[i >> 1] for i in range(8)]
    grad_qkv, grad_out = heads_placed(a_all, s8)
    tokens_grad = (first + up(jnp.concatenate([upper_sum, lower_one, lower_two]))).astype(BF)
    return (
        mixed,
        tokens_grad,
        grad_qkv.transpose(1, 0, 2),
        grad_out,
        grad_up,
        grad_down,
        gains[0],
        gains[1],
    )


def solution(mesh):
    rows = P(("seq", "tp"), None)
    weights = (P(None, None, "tp"), P("tp", None), P(None, "tp"), P("tp", None), P(), P())
    return jax.shard_map(
        functools.partial(per_device, mesh.shape["seq"]),
        mesh=mesh,
        in_specs=(rows,) + weights + (rows, P("seq"), P("seq", None)),
        out_specs=(rows, rows) + weights,
        check_vma=False,
    )
```

```python
import functools

import jax
import jax.numpy as jnp
from jax import lax
from jax.experimental import pallas as pl
from jax.experimental.pallas import tpu as pltpu
from jax.sharding import PartitionSpec as P

HEAD = 64
SLOTS = 4
BF = jnp.bfloat16
F32 = jnp.float32
LOG2E = 1.4426950408889634
LN_EPS = 1e-5
LIGHT = pl.CostEstimate(flops=10**9, bytes_accessed=10**6, transcendentals=0)
NT = (((1,), (1,)), ((), ()))
NN = (((1,), (0,)), ((), ()))
TN = (((0,), (0,)), ((), ()))

PAIR = [(0, 1), (1, 0), (2, 3), (3, 2)]
MIDDLE = [(1, 2), (2, 1)]
OUTWARD = [(1, 0), (2, 3)]


def in_hbm(*arrays):
    return [pltpu.with_memory_space_constraint(a, pltpu.HBM) for a in arrays]


def mm(a, b, dims, out=F32):
    return lax.dot_general(a, b, dims, preferred_element_type=F32).astype(out)


def along(array, pairs):
    return lax.ppermute(array, "tp", pairs)


def fence(*arrays):
    return lax.optimization_barrier(arrays)


class Plane:
    def __init__(self, size):
        self.size = size

    def swap(self, array, bit):
        return lax.ppermute(array, "seq", [(i, i ^ bit) for i in range(self.size)])

    def higher_exact(self, total):
        bit = 8
        while bit < self.size:
            total = total + self.swap(total, bit)
            bit *= 2
        return total

    def higher(self, total):
        bit = 8
        while bit < self.size:
            total = (total.astype(F32) + self.swap(total, bit).astype(F32)).astype(BF)
            bit *= 2
        return total


def forward_kernel(blocks, q_ref, *refs):
    k_refs, v_refs = refs[:blocks], refs[blocks : 2 * blocks]
    bias_ref, out_ref, lse_ref = refs[2 * blocks], refs[-2], refs[-1]
    scale = HEAD**-0.5 * LOG2E
    rows = q_ref.shape[0]
    lane = lax.broadcasted_iota(jnp.int32, (1, 2 * HEAD), 1)
    zero = jnp.zeros((), BF)
    keys = jnp.concatenate([ref[...] for ref in k_refs])
    values = jnp.concatenate([ref[...] for ref in v_refs])
    bias = bias_ref[...]
    sub = 256
    mine = [(lane < HEAD) == (head == 0) for head in range(2)]
    k = [jnp.where(m, keys, zero) for m in mine]
    v = [jnp.where(m, values, zero) for m in mine]
    for at in range(rows // sub):
        span = pl.ds(at * sub, sub)
        q = q_ref[span, :]
        outs, lses = [], []
        for head in range(2):
            s = lax.dot_general(q, k[head], NT, preferred_element_type=F32)
            s = s * scale + bias
            top = jnp.max(s, axis=1, keepdims=True)
            p = jnp.exp2(s - top)
            total = jnp.sum(p, axis=1, keepdims=True)
            o = lax.dot_general(p.astype(BF), v[head], NN, preferred_element_type=F32)
            outs.append(o / total)
            lses.append(top + jnp.log2(total))
        out_ref[span, :] = (outs[0] + outs[1]).astype(BF)
        wide = jnp.where(lane < HEAD, lses[0], lses[1])
        flat = jnp.transpose(wide)
        lse_ref[0, :, span] = jnp.concatenate(
            [flat[0:1], flat[HEAD : HEAD + 1]], axis=0
        )


def attention_forward(q, kvs, bias, first, count, held=()):
    rows, width = q.shape
    keys = bias.shape[1]
    pairs = width // (2 * HEAD)
    wide = 2 * HEAD
    at = lambda shift: lambda h: (0, h + first + shift)
    return pl.pallas_call(
        functools.partial(forward_kernel, len(kvs)),
        grid=(count,),
        in_specs=[pl.BlockSpec((rows, wide), at(0))]
        + [pl.BlockSpec((kv.shape[0], wide), at(0)) for kv in kvs]
        + [pl.BlockSpec((kv.shape[0], wide), at(pairs)) for kv in kvs]
        + [pl.BlockSpec((1, keys), lambda h: (0, 0))]
        + [pl.BlockSpec(memory_space=pl.ANY)] * len(held),
        out_specs=[
            pl.BlockSpec((rows, wide), at(0)),
            pl.BlockSpec((1, 2, rows), lambda h: (h + first, 0, 0)),
        ],
        out_shape=[
            jax.ShapeDtypeStruct((rows, width), BF),
            jax.ShapeDtypeStruct((pairs, 2, rows), F32),
        ],
        input_output_aliases={2 * len(kvs) + 2 + n: n for n in range(len(held))},
        compiler_params=pltpu.CompilerParams(vmem_limit_bytes=24 * 2**20),
        cost_estimate=LIGHT,
        name="attention_forward",
    )(q, *kvs, *kvs, bias, *held)


def backward_kernel(
    q_ref, k_ref, v_ref, go_ref, att_ref, lse_ref, bias_ref, wkv_ref, *refs
):
    add_ref = refs[0] if len(refs) == 9 else None
    gq_ref, keep_k_ref, keep_v_ref, send_ref, part_ref, all_ref = refs[-6:]
    step, pairs = pl.program_id(0), pl.num_programs(0)
    scale = HEAD**-0.5
    wide = 2 * HEAD
    keys = k_ref.shape[0]
    lane = lax.broadcasted_iota(jnp.int32, (1, wide), 1)
    q, go = q_ref[...], go_ref[...]
    zero = jnp.zeros((), BF)
    mine = [(lane < HEAD) == (head == 0) for head in range(2)]
    qs = [jnp.where(m, q, zero) for m in mine]
    gos = [jnp.where(m, go, zero) for m in mine]
    product = go.T.astype(F32) * att_ref[...].T.astype(F32)
    inner = [
        jnp.sum(product[head * HEAD : (head + 1) * HEAD], axis=0, keepdims=True)
        for head in range(2)
    ]
    total_q = [0.0, 0.0]
    gks, gvs = [], []
    sub = 1024
    for at in range(keys // sub):
        span = pl.ds(at * sub, sub)
        bias = bias_ref[span, 0:1]
        keys_t = k_ref[span, :].T
        total_k, total_v = 0.0, 0.0
        for head in range(2):
            k = jnp.where(mine[head], k_ref[span, :], zero)
            v = jnp.where(mine[head], v_ref[span, :], zero)
            s = lax.dot_general(k, q, NT, preferred_element_type=F32)
            p = jnp.exp2(s * (scale * LOG2E) + (bias - lse_ref[0, head : head + 1, :]))
            gp = lax.dot_general(v, go, NT, preferred_element_type=F32)
            gs = (p * (gp - inner[head])).astype(BF)
            total_v += lax.dot_general(p.astype(BF), gos[head], NN, preferred_element_type=F32)
            total_k += lax.dot_general(gs, qs[head], NN, preferred_element_type=F32)
            own_keys = keys_t[head * HEAD : (head + 1) * HEAD]
            total_q[head] += lax.dot_general(own_keys, gs, NN, preferred_element_type=F32)
        gks.append((total_k * scale).astype(BF))
        gvs.append(total_v.astype(BF))
    gk, gv = jnp.concatenate(gks), jnp.concatenate(gvs)
    gq = jnp.concatenate(total_q).T * scale
    gq_ref[...] = (gq if add_ref is None else gq + add_ref[...]).astype(gq_ref.dtype)
    half = pairs // 2

    @pl.when(step < half)
    def _():
        keep_k_ref[...] = gk
        keep_v_ref[...] = gv

    @pl.when(step >= half)
    def _():
        send_ref[0] = gk
        send_ref[1] = gv

    lanes = pl.multiple_of(step * wide, wide)
    all_ref[:, pl.ds(lanes, wide)] = gk
    all_ref[:, pl.ds(pl.multiple_of(lanes + q_width(part_ref), wide), wide)] = gv

    @pl.when(step == pairs - 1)
    def _():
        for at in range(keys // 256):
            span = pl.ds(at * 256, 256)
            part = lax.dot_general(
                all_ref[span, :], wkv_ref[...], NN, preferred_element_type=F32
            )
            part_ref[span, :] = part.astype(BF)


def q_width(part_ref):
    return part_ref.shape[1]


def attention_backward(q, kv, go, attended, lse, bias, wkv, block, blocks, held):
    rows, width = q.shape
    keys = kv.shape[0]
    pairs = width // (2 * HEAD)
    wide = 2 * HEAD
    half = pairs // 2
    by_pair = pl.BlockSpec((rows, wide), lambda h: (0, h))
    stats = pl.BlockSpec((1, 2, rows), lambda h: (h, 0, 0))
    whole = pl.BlockSpec(memory_space=pl.ANY)
    keep = pl.BlockSpec((keys, wide), lambda h: (block, jnp.minimum(h, half - 1)))
    send = pl.BlockSpec((2, keys, wide), lambda h: (0, 0, jnp.maximum(h - half, 0)))
    return pl.pallas_call(
        backward_kernel,
        grid=(pairs,),
        in_specs=[
            by_pair,
            pl.BlockSpec((keys, wide), lambda h: (0, h)),
            pl.BlockSpec((keys, wide), lambda h: (0, h + pairs)),
            by_pair,
            by_pair,
            stats,
            pl.BlockSpec((keys, 128), lambda h: (0, 0)),
            pl.BlockSpec((2 * width, width), lambda h: (0, 0), pipeline_mode=pl.Buffered(1)),
        ]
        + ([by_pair, whole, whole] if held else []),
        out_specs=[by_pair, keep, keep, send, pl.BlockSpec((keys, width), lambda h: (0, 0))],
        out_shape=[
            jax.ShapeDtypeStruct((rows, width), BF if held else F32),
            jax.ShapeDtypeStruct((blocks * keys, width // 2), BF),
            jax.ShapeDtypeStruct((blocks * keys, width // 2), BF),
            jax.ShapeDtypeStruct((2, keys, width // 2), BF),
            jax.ShapeDtypeStruct((keys, width), BF),
        ],
        scratch_shapes=[pltpu.VMEM((keys, 2 * width), BF)],
        input_output_aliases={9: 1, 10: 2} if held else {},
        compiler_params=pltpu.CompilerParams(vmem_limit_bytes=48 * 2**20),
        cost_estimate=LIGHT,
        name="attention_backward",
    )(*in_hbm(q, kv, kv, go, attended), lse, bias, *in_hbm(wkv, *(held or ())))


def gelu_tile(x):
    size = jnp.abs(x)
    t = 1.0 / (1.0 + size * (0.3275911 * 0.5**0.5))
    poly = t * (
        0.127414796
        + t * (-0.142248368 + t * (0.7107068705 + t * (-0.7265760135 + t * 0.5307027145)))
    )
    bell = jnp.exp2(x * x * (-0.5 * LOG2E))
    tail = poly * bell
    cdf = jnp.where(x >= 0, 1.0 - tail, tail)
    return (x * cdf).astype(BF), (cdf + x * (bell * 0.3989422804014327)).astype(BF)


def head_grads_kernel(many, *refs):
    ins, (x_ref, y_ref, near_x_ref, near_y_ref, own_ref) = refs[:-5], refs[-5:]

    def outer(left, right):
        return lax.dot_general(left, right, TN, preferred_element_type=F32)

    if many:
        big_refs, came_refs, row_refs = ins[:2], ins[2:4], ins[4:]
        keys = row_refs[0].shape[0]
        totals_of = []
        for kind in range(2):
            total = 0.0
            for n in range(2):
                part = slice(n * keys, (n + 1) * keys)
                total += outer(big_refs[kind][part, :], row_refs[n][...])
                total += outer(came_refs[n][kind], row_refs[2 + n][...])
            totals_of.append(total.astype(BF))
    else:
        totals_of = []
        for kind in range(2):
            left, left_peer, right, right_peer = [ref[...] for ref in ins[4 * kind : 4 * kind + 4]]
            totals_of.append((outer(left, right) + outer(left_peer, right_peer)).astype(BF))
    size = HEAD // 2

    def chunk(n):
        rows = []
        for at in range(totals_of[0].shape[0] // (4 * size)):
            source = (at * 4 + (n & 1) * 2 + (n >> 1)) * size
            rows += [total[source : source + size] for total in totals_of]
        return jnp.concatenate(rows)

    half = own_ref.shape[0]
    own_ref[...] = chunk(0)

    @pl.when(pl.program_id(0) == 0)
    def _():
        x_ref[:half, :] = chunk(3)
        x_ref[half:, :] = chunk(1)
        near_y_ref[...] = chunk(2)

    @pl.when(pl.program_id(0) == 1)
    def _():
        y_ref[:half, :] = chunk(3)
        y_ref[half:, :] = chunk(2)
        near_x_ref[...] = chunk(1)


def head_grads(columns, arrived, whole_arrays, many, order=None):
    width = whole_arrays[0].shape[1]
    wide = width // 4
    half = wide // 2
    by_column = [pl.BlockSpec((a.shape[0], wide), lambda g: (0, g)) for a in columns]
    by_kind = [pl.BlockSpec((2, a.shape[1], wide), lambda g: (0, 0, g)) for a in arrived]
    whole = [
        pl.BlockSpec(a.shape, lambda g: (0, 0), pipeline_mode=pl.Buffered(1))
        for a in whole_arrays
    ]
    args, specs = [*columns, *arrived, *whole_arrays], by_column + by_kind + whole
    if order:
        args, specs = [args[n] for n in order], [specs[n] for n in order]
    fixed = lambda rows: pl.BlockSpec((rows, width), lambda g: (0, 0))
    shape = lambda rows: jax.ShapeDtypeStruct((rows, width), BF)
    return pl.pallas_call(
        functools.partial(head_grads_kernel, many),
        grid=(2,),
        in_specs=specs,
        out_specs=[fixed(wide), fixed(wide), fixed(half), fixed(half)]
        + [pl.BlockSpec((half, width), lambda g: (g, 0))],
        out_shape=[shape(wide), shape(wide), shape(half), shape(half), shape(wide)],
        compiler_params=pltpu.CompilerParams(vmem_limit_bytes=48 * 2**20),
        cost_estimate=LIGHT,
        name="head_grads",
    )(*in_hbm(*args))


def rows_kernel(moves, n_held, n_out, *refs):
    n_in = len(refs) - n_held - n_out - 1
    ins, outs, sems = refs[:n_in], refs[-1 - n_out : -1], refs[-1]
    copies = []
    for n, (source, at, count, out, place) in enumerate(moves):
        copies.append(
            pltpu.make_async_copy(
                ins[source].at[pl.ds(at, count), :],
                outs[out].at[pl.ds(place, count), :],
                sems.at[n],
            )
        )
    for copy in copies:
        copy.start()
    for copy in copies:
        copy.wait()


def put_rows(moves, shape, n_out, held=()):
    arrays, listed = [], []
    for array, at, count, out, place in moves:
        known = [n for n, a in enumerate(arrays) if a is array]
        if not known:
            arrays.append(array)
        listed.append((known[0] if known else len(arrays) - 1, at, count, out, place))
    whole = pl.BlockSpec(memory_space=pl.ANY)
    return pl.pallas_call(
        functools.partial(rows_kernel, listed, len(held), n_out),
        in_specs=[pl.BlockSpec(memory_space=pltpu.VMEM)] * len(arrays) + [whole] * len(held),
        out_specs=[whole] * n_out,
        out_shape=[jax.ShapeDtypeStruct(shape, BF)] * n_out,
        scratch_shapes=[pltpu.SemaphoreType.DMA((len(listed),))],
        input_output_aliases={len(arrays) + n: n for n in range(len(held))},
        compiler_params=pltpu.CompilerParams(vmem_limit_bytes=32 * 2**20),
        cost_estimate=LIGHT,
        name="put_rows",
    )(*arrays, *held)


def totals_kernel(at_ref, *refs):
    *ins, out_ref = refs
    size = ins[0].shape[0]
    for n in range(2):
        a, b, c = [ref[...].astype(F32) for ref in ins[3 * n : 3 * n + 3]]
        out_ref[n * size : (n + 1) * size, :] = (a + b + c).astype(BF)


def totals(ones, twos, t):
    rows, width = ones[0].shape
    size = rows // 4
    return pl.pallas_call(
        totals_kernel,
        grid_spec=pltpu.PrefetchScalarGridSpec(
            num_scalar_prefetch=1,
            grid=(4,),
            in_specs=[pl.BlockSpec((size, width), lambda u, at: (at[0] ^ u, 0))] * 6,
            out_specs=pl.BlockSpec((2 * size, width), lambda u, at: (u, 0)),
        ),
        out_shape=jax.ShapeDtypeStruct((2 * rows, width), BF),
        cost_estimate=LIGHT,
        name="totals",
    )(t[None].astype(jnp.int32), *ones, *twos)


def outer_kernel(left_ref, right_ref, left_two_ref, right_two_ref, *out_refs):
    total = lax.dot_general(left_ref[...], right_ref[...], TN, preferred_element_type=F32)
    total += lax.dot_general(
        left_two_ref[...], right_two_ref[...], TN, preferred_element_type=F32
    )
    total = total.astype(BF)
    each = pl.num_programs(0) // len(out_refs)
    for n, out_ref in enumerate(out_refs):

        @pl.when(pl.program_id(0) // each == n)
        def _():
            out_ref[...] = total


def outer_four(left, right, left_two, right_two):
    rows, hidden = left.shape
    width = right.shape[1]
    tile = 512
    each = hidden // (4 * tile)
    columns = pl.BlockSpec((rows, tile), lambda i: (0, i))
    whole = pl.BlockSpec((rows, width), lambda i: (0, 0))
    place = lambda n: lambda i: (jnp.clip(i - n * each, 0, each - 1), 0)
    return pl.pallas_call(
        outer_kernel,
        grid=(hidden // tile,),
        in_specs=[columns, whole, columns, whole],
        out_specs=[pl.BlockSpec((tile, width), place(n)) for n in range(4)],
        out_shape=[jax.ShapeDtypeStruct((hidden // 4, width), BF)] * 4,
        compiler_params=pltpu.CompilerParams(vmem_limit_bytes=32 * 2**20),
        cost_estimate=LIGHT,
        name="outer_four",
    )(left, right, left_two, right_two)


def reverse(i):
    return ((i & 1) << 2) | (i & 2) | (i >> 2)


def heads_placed_kernel(at_ref, *refs):
    *pieces, turned_ref, plain_ref, whole_ref = refs
    step, last = pl.program_id(0), pl.num_programs(0) - 1
    for i, piece in enumerate(pieces):
        place = reverse(at_ref[0] ^ i)
        size = piece.shape[0]
        whole_ref[pl.ds(pl.multiple_of(place * size, size), size), :] = piece[...]

    @pl.when(step < last)
    def _():
        turned_ref[0] = whole_ref[...].T.astype(F32)

    @pl.when(step == last)
    def _():
        plain_ref[...] = whole_ref[...].astype(F32)


def heads_placed(pieces, s8):
    kind_at = lambda n: jnp.where(n == 0, 0, jnp.where(n == 3, 1, n + 1))
    width = pieces[0].shape[1]
    size = pieces[0].shape[0] // 4
    rows = 8 * size
    return pl.pallas_call(
        heads_placed_kernel,
        grid=(4,),
        in_specs=[pl.BlockSpec(memory_space=pltpu.SMEM)]
        + [pl.BlockSpec((size, width), lambda n: (kind_at(n), 0)) for _ in pieces],
        out_specs=[
            pl.BlockSpec((1, width, rows), lambda n: (jnp.minimum(n, 2), 0, 0)),
            pl.BlockSpec((rows, width), lambda n: (0, 0)),
        ],
        out_shape=[
            jax.ShapeDtypeStruct((3, width, rows), F32),
            jax.ShapeDtypeStruct((rows, width), F32),
        ],
        scratch_shapes=[pltpu.VMEM((rows, width), BF)],
        compiler_params=pltpu.CompilerParams(vmem_limit_bytes=32 * 2**20),
        cost_estimate=LIGHT,
        name="heads_placed",
    )(s8[None].astype(jnp.int32), *pieces)


def placed_kernel(flips, at_ref, *refs):
    *pieces, out_ref, whole_ref = refs
    for i, piece in enumerate(pieces):
        place = at_ref[0] ^ i
        size = piece.shape[0]
        whole_ref[pl.ds(pl.multiple_of(place * size, size), size), :] = piece[...]
    out = whole_ref[...]
    out = out.T if flips else out
    out_ref[...] = out.astype(F32)


def placed(pieces, size, s8, flips):
    width = pieces[0][0].shape[1]
    tile = 512
    rows = 8 * size
    if flips:
        out_shape, out_spec = (width, rows), pl.BlockSpec((tile, rows), lambda c: (c, 0))
    else:
        out_shape, out_spec = (rows, width), pl.BlockSpec((rows, tile), lambda c: (0, c))
    part = lambda first: pl.BlockSpec((size, tile), lambda c: (first, c))
    return pl.pallas_call(
        functools.partial(placed_kernel, flips),
        grid=(width // tile,),
        in_specs=[pl.BlockSpec(memory_space=pltpu.SMEM)] + [part(first) for _, first in pieces],
        out_specs=out_spec,
        out_shape=jax.ShapeDtypeStruct(out_shape, F32),
        scratch_shapes=[pltpu.VMEM((rows, tile), BF)],
        compiler_params=pltpu.CompilerParams(vmem_limit_bytes=32 * 2**20),
        cost_estimate=LIGHT,
        name="placed",
    )(s8[None].astype(jnp.int32), *[array for array, _ in pieces])


def centred(values):
    centre = values - jnp.mean(values, axis=-1, keepdims=True)
    root = lax.rsqrt(jnp.mean(centre * centre, axis=-1, keepdims=True) + LN_EPS)
    return centre * root, root


def norm_pull(grad, gain, unit, root):
    scaled = grad * gain
    mean = jnp.mean(scaled, axis=-1, keepdims=True)
    slope = jnp.mean(scaled * unit, axis=-1, keepdims=True)
    return root * (scaled - mean - unit * slope), jnp.sum(grad * unit, axis=0)


def per_device(
    seq_size, tokens, w_qkv, w_out, w_up, w_down, gain_one, gain_two, cotangent, bucket, lengths
):
    rows, width = tokens.shape
    t = lax.axis_index("tp")
    middle = (t == 1) | (t == 2)
    s8 = lax.axis_index("seq") % 8
    plane = Plane(seq_size)
    swap = plane.swap
    hid = w_out.shape[0]
    ff = w_down.shape[0]
    qp, fp = hid // 8, ff // 8
    up = lambda a: a.astype(F32)
    across = lambda a, j: along(a, [(i, i ^ j) for i in range(4)])

    w_attn_own = jnp.concatenate([w_qkv.transpose(1, 2, 0), w_out[None]])

    def attn_piece(i):
        return lax.dynamic_slice_in_dim(w_attn_own, reverse(s8 ^ i) * qp, qp, axis=1)

    def up_piece(i):
        return lax.dynamic_slice_in_dim(w_up, (s8 ^ i) * fp, fp, axis=1).T

    def down_piece(i):
        return lax.dynamic_slice_in_dim(w_down, (s8 ^ i) * fp, fp, axis=0)

    attn_own = attn_piece(0).reshape(4 * qp, width)
    up_own = jnp.concatenate([up_piece(2 * i) for i in range(4)])
    down_own = jnp.concatenate([down_piece(2 * i) for i in range(4)])
    ff_own = jnp.concatenate([up_own[:fp], down_own[:fp]])

    upper = rows // 2
    gathered = [
        lax.all_gather(tokens[n * upper : (n + 1) * upper], "tp", axis=0, tiled=True)
        for n in range(2)
    ]
    a_far = [across(attn_own, j) for j in (1, 2, 3)]
    whole = bucket[0] == 1
    place = jnp.arange(rows, dtype=jnp.int32)
    seen = []
    for u in range(4):
        alone = jnp.where(t == u, lengths[0, u], 0)
        limit = jnp.where(whole, lengths[0, 0] - u * rows, alone)
        seen.append((place < limit).reshape(2, upper))
    bias = jnp.where(jnp.stack(seen, axis=1), 0.0, -1e9).astype(F32).reshape(4 * rows)
    bias, *a_far = fence(bias, *a_far)
    bias_cols = jnp.broadcast_to(bias[:, None], (4 * rows, 128))

    attn_three = jnp.concatenate(a_far)
    half = attn_three.shape[0] // 2
    a_x, a_y = swap(attn_three, 2), swap(attn_three, 4)
    attn_three, a_x, a_y = fence(attn_three, a_x, a_y)
    a_d1, a_d2 = swap(a_y[:half], 2), swap(a_x[half:], 4)
    others = [swap(attn_three, 1), swap(a_x, 1), swap(a_y, 1)]
    a_d1, a_d2, *others = fence(a_d1, a_d2, *others)
    others += fence(swap(a_d1, 1), swap(a_d2, 1))

    four = [attn_three, a_x, a_y, a_d1, a_d2]
    pieces = []
    for i in range(8):
        part = others if i & 1 else four
        far = part[i >> 1] if i < 6 else jnp.concatenate(part[3:])
        pieces.append(jnp.concatenate([attn_piece(i)[None], far.reshape(3, 4, qp, width)]))
    w_attn = jnp.stack(pieces).reshape(2, 2, 2, 4, 4, qp, width).transpose(4, 2, 3, 1, 0, 5, 6)
    w_attn = w_attn.reshape(4, width, width)
    wq, wk, wv, wo = [w_attn[n] for n in range(4)]
    wkv = w_attn[1:3].reshape(2 * width, width)

    wq, wkv, ff_own, up_own, down_own = fence(wq, wkv, ff_own, up_own, down_own)
    f_one, f_far = along(ff_own, PAIR), along(ff_own, MIDDLE)
    q = mm(tokens, wq, NT, BF)
    upper_kv = mm(gathered[0], wkv, NT, BF)
    f_one, f_far, q, upper_kv = fence(f_one, f_far, q, upper_kv)
    f_two, f_two_end = along(f_one, MIDDLE), along(f_far, OUTWARD)
    one_x, one_y = swap(f_one, 2), swap(f_one, 4)
    tokens_peer = swap(tokens, 1)
    f_two, f_two_end, one_x, one_y, tokens_peer, *kvs = fence(
        f_two, f_two_end, one_x, one_y, tokens_peer, upper_kv, mm(gathered[1], wkv, NT, BF)
    )
    f_three_end = along(f_two, OUTWARD)
    f_two = jnp.where(middle, f_two, f_two_end)
    two_x, two_y = swap(f_two, 2), swap(f_two, 4)
    one_d1, one_d2 = swap(one_y[:fp], 2), swap(one_x[fp:], 4)
    bias_row = bias[None]
    held = attention_forward(q, kvs, bias_row, 0, 3)
    f_three_end, one_d1, one_d2, two_x, two_y, *held = fence(
        f_three_end, one_d1, one_d2, two_x, two_y, *held
    )
    f_three = jnp.where(middle, f_far, f_three_end)
    three_x, three_y = swap(f_three, 2), swap(f_three, 4)
    two_d1, two_d2 = swap(two_y[:fp], 2), swap(two_x[fp:], 4)

    def moves(j, block):
        own, by_x, by_y, d1, d2 = block
        sources = [(own, own, fp), (by_x, by_x, fp), (by_y, by_y, fp), (d1, d2, 0)]
        for i, (a, b, at) in enumerate(sources):
            yield (a, 0, fp, 0, (4 * i + j) * fp)
            yield (b, at, fp, 1, (4 * i + j) * fp)

    own = []
    for i in range(4):
        own.append((up_own, i * fp, fp, 0, 4 * i * fp))
        own.append((down_own, i * fp, fp, 1, 4 * i * fp))
    one = moves(1, (f_one, one_x, one_y, one_d1, one_d2))
    w_ff = put_rows([*own, *one], (ff * 2, width), 2)
    w_ff = fence(*w_ff, *held)
    w_ff, held = w_ff[:2], w_ff[2:]
    held = attention_forward(q, kvs, bias_row, 3, 3, held)
    two_d1, two_d2, three_x, three_y, *held = fence(two_d1, two_d2, three_x, three_y, *held)
    three_d1, three_d2 = swap(three_y[:fp], 2), swap(three_x[fp:], 4)
    held = attention_forward(q, kvs, bias_row, 6, 2, held)
    three_d1, three_d2, *held = fence(three_d1, three_d2, *held)
    attended, lse = held
    first_sum = up(tokens) + mm(attended, wo, NN)
    unit_one, root_one = centred(first_sum)
    normed = unit_one * gain_one
    normed_low = normed.astype(BF)

    two = moves(2, (f_two, two_x, two_y, two_d1, two_d2))
    three = moves(3, (f_three, three_x, three_y, three_d1, three_d2))
    wu, wd = put_rows([*two, *three], (ff * 2, width), 2, w_ff)

    normed_peer = swap(normed_low, 1)
    gathered_peer = [swap(part, 1) for part in gathered]
    attended_peer = swap(attended[:, width // 2 :], 1)
    act, slope = gelu_tile(mm(normed_low, wu, NT))
    act_peer, slope_peer = gelu_tile(mm(normed_peer, wu, NT))
    shrunk_peer = swap(mm(act_peer, wd, NN, BF), 1)
    unit_two, root_two = centred(normed + mm(act, wd, NN) + up(shrunk_peer))
    mixed = (unit_two * gain_two).astype(BF)

    grad_second, gain_grad_two = norm_pull(up(cotangent), gain_two, unit_two, root_two)
    second_low = grad_second.astype(BF)
    second_peer = swap(second_low, 1)
    grad_exp = (mm(second_low, wd, NT) * up(slope)).astype(BF)
    grad_exp_peer = (mm(second_peer, wd, NT) * up(slope_peer)).astype(BF)
    normed_part_peer = swap(mm(grad_exp_peer, wu, NN, BF), 1)
    normed_part = mm(grad_exp, wu, NN)
    twos = outer_four(act, second_low, act_peer, second_peer)
    normed_part, normed_part_peer, *twos = fence(normed_part, normed_part_peer, *twos)
    diag_y, two_y = swap(twos[3], 4), swap(twos[2], 4)
    ones = outer_four(grad_exp, normed_low, grad_exp_peer, normed_peer)
    grad_normed = grad_second + normed_part + up(normed_part_peer)
    normed_part, *ones = fence(normed_part, *ones)
    diag_x, one_x = swap(ones[3], 2), swap(ones[1], 2)
    grad_first, gain_grad_one = norm_pull(grad_normed, gain_one, unit_one, root_one)
    first_low = grad_first.astype(BF)
    first_peer = swap(first_low, 1)
    go = mm(first_low, wo, NT, BF)
    core = width // 2
    go, first_peer, attended_peer, *gathered_peer = fence(
        go, first_peer, attended_peer, *gathered_peer
    )

    def pull(n, held):
        keys = bias_cols[2 * n * rows : 2 * (n + 1) * rows]
        *held, send, part = attention_backward(
            q, kvs[n], go, attended, lse, keys, wkv, n, 2, held
        )
        return held, send, part

    def line_sum(part):
        return lax.psum_scatter(part, "tp", scatter_dimension=0, tiled=True)

    gains = jnp.stack([gain_grad_one, gain_grad_two])
    gains_came = swap(gains, 1)
    held, send, part = pull(0, None)
    diag_x, diag_y, one_x, two_y, send, part, gains_came, *held = fence(
        diag_x, diag_y, one_x, two_y, send, part, gains_came, *held
    )
    upper_sum = line_sum(part)
    came = [swap(send, 1)]
    gains = gains + gains_came
    gains_came = swap(gains, 2)
    two_x = (up(twos[1]) + up(diag_y)).astype(BF)
    one_y = (up(ones[2]) + up(diag_x)).astype(BF)
    two_x, one_y, *held = fence(two_x, one_y, *held)
    two_x, one_y = swap(two_x, 2), swap(one_y, 4)
    held, send, part = pull(1, held)
    two_x, one_y, came[0], send, part, gains_came, *held = fence(
        two_x, one_y, came[0], send, part, gains_came, *held
    )
    gq, gk, gv = held
    gq_peer = swap(gq[:, core:], 1)
    gains = gains + gains_came
    gains_came = swap(gains, 4)
    part = part.reshape(4, 2, upper // 2, width)
    part_one, part_two = [part[:, n].reshape(rows, width) for n in range(2)]
    lower_one = line_sum(part_one)
    ff_total = plane.higher(totals((ones[0], one_x, one_y), (twos[0], two_x, two_y), t))
    upper_sum, ff_total = fence(upper_sum, ff_total)
    ff_total = line_sum(ff_total)
    gq_peer, gains_came, send = fence(gq_peer, gains_came, send)
    came.append(swap(send, 1))
    gains = plane.higher_exact(gains + gains_came)
    coarse = lax.reduce_precision(gains, exponent_bits=8, mantissa_bits=7)
    gains = jnp.concatenate([coarse, gains - coarse, jnp.zeros((12, width), F32)]).astype(BF)
    light = head_grads(
        [gq, gq_peer, attended, attended_peer],
        [],
        [tokens, tokens_peer, first_low, first_peer],
        False,
        (0, 1, 4, 5, 2, 3, 6, 7),
    )
    came[1], *light = fence(came[1], *light)
    to_x, to_y = swap(light[0], 2), swap(light[1], 4)
    heavy = head_grads([gk, gv], came, [*gathered, *gathered_peer], True)
    to_x, to_y, gq, *heavy = fence(to_x, to_y, gq, *heavy)
    half = 4 * qp
    add = lambda *arrays: sum(up(a) for a in arrays).astype(BF)

    def second_hop(parts, to_x, to_y):
        return add(parts[2], to_y[:half]), add(parts[3], to_x[:half])

    def mine_of(parts, to_x, to_y, on_x, on_y):
        own = parts[4]
        total = [add(own[:half], to_x[half:], on_y), add(own[half:], to_y[half:], on_x)]
        return plane.higher(jnp.concatenate(total)).reshape(4, 2 * qp, width)

    next_x, next_y = second_hop(light, to_x, to_y)
    next_x, next_y, *heavy = fence(next_x, next_y, *heavy)
    on_x, on_y = swap(next_x, 2), swap(next_y, 4)
    far_x, far_y = swap(heavy[0], 2), swap(heavy[1], 4)
    first = mm(gq, wq, NN) + grad_first
    on_x, on_y, far_x, far_y, first = fence(on_x, on_y, far_x, far_y, first)
    next_x, next_y = second_hop(heavy, far_x, far_y)
    next_x, next_y, ff_total = fence(next_x, next_y, ff_total)
    last_x, last_y = swap(next_x, 2), swap(next_y, 4)
    f_x, f_y = swap(ff_total, 2), swap(ff_total, 4)
    light_mine = mine_of(light, to_x, to_y, on_x, on_y)
    last_x, last_y, light_mine = fence(last_x, last_y, light_mine)
    heavy_mine = mine_of(heavy, far_x, far_y, last_x, last_y)
    a_mine = jnp.concatenate([light_mine, heavy_mine], axis=1)
    pairs = a_mine.reshape(2, 2, 4 * qp, width)
    pairs = jnp.where((t & 1) == 1, pairs[:, ::-1], pairs)
    a_mine = jnp.where((t & 2) == 2, pairs[::-1], pairs).reshape(a_mine.shape)
    gains = jnp.broadcast_to(gains[None], (4, 16, width))
    a_mine = fence(jnp.concatenate([a_mine, gains], axis=1))[0]
    a_came = lax.all_to_all(a_mine, "tp", split_axis=0, concat_axis=0, tiled=True)
    f_core = [swap(ff_total, 1)]
    f_d1, f_d2 = swap(f_y[:fp], 2), swap(f_x[fp:], 4)
    f_core += [swap(f_x, 1), swap(f_y, 1)]
    a_came, part_two, f_d1, f_d2, b0, b1, b2 = fence(a_came, part_two, f_d1, f_d2, *f_core)
    f_core = [b0, b1, b2]
    lower_two = line_sum(part_two)
    a_total = fence(jnp.sum(up(a_came[:, : 4 * qp]), axis=0).astype(BF))[0]
    gains = jnp.sum(up(a_came[:, 4 * qp : 4 * qp + 4]), axis=0)
    gains = gains[:2] + gains[2:]
    a_four = [a_total, swap(a_total, 2), swap(a_total, 4), swap(a_total, 6)]
    a_core = [swap(a_total, 1)]
    f_core += [swap(f_d1, 1), swap(f_d2, 1)]
    f_four = [ff_total, f_x, f_y, f_d1, f_d2]
    ups, downs = [], []
    for i in range(8):
        part = f_core if i & 1 else f_four
        ups.append((part[i >> 1], 0))
        downs.append((part[i >> 1], 1) if i < 6 else (part[4], 0))
    grad_up = placed(ups, fp, s8, True)
    grad_down = placed(downs, fp, s8, False)
    grad_up, grad_down, *a_four = fence(grad_up, grad_down, *a_four)
    a_core += [swap(a, 1) for a in a_four[1:]]
    a_all = [(a_core if i & 1 else a_four)[i >> 1] for i in range(8)]
    grad_qkv, grad_out = heads_placed(a_all, s8)
    tokens_grad = (first + up(jnp.concatenate([upper_sum, lower_one, lower_two]))).astype(BF)
    return (
        mixed,
        tokens_grad,
        grad_qkv.transpose(1, 0, 2),
        grad_out,
        grad_up,
        grad_down,
        gains[0],
        gains[1],
    )


def solution(mesh):
    rows = P(("seq", "tp"), None)
    weights = (P(None, None, "tp"), P("tp", None), P(None, "tp"), P("tp", None), P(), P())
    return jax.shard_map(
        functools.partial(per_device, mesh.shape["seq"]),
        mesh=mesh,
        in_specs=(rows,) + weights + (rows, P("seq"), P("seq", None)),
        out_specs=(rows, rows) + weights,
        check_vma=False,
    )
```

```python
import functools

import jax
import jax.numpy as jnp
from jax import lax
from jax.experimental import pallas as pl
from jax.experimental.pallas import tpu as pltpu
from jax.sharding import PartitionSpec as P

HEAD = 64
SLOTS = 4
BF = jnp.bfloat16
F32 = jnp.float32
LOG2E = 1.4426950408889634
LN_EPS = 1e-5
LIGHT = pl.CostEstimate(flops=10**9, bytes_accessed=10**6, transcendentals=0)
NT = (((1,), (1,)), ((), ()))
NN = (((1,), (0,)), ((), ()))
TN = (((0,), (0,)), ((), ()))

PAIR = [(0, 1), (1, 0), (2, 3), (3, 2)]
MIDDLE = [(1, 2), (2, 1)]
OUTWARD = [(1, 0), (2, 3)]


def in_hbm(*arrays):
    return [pltpu.with_memory_space_constraint(a, pltpu.HBM) for a in arrays]


def mm(a, b, dims, out=F32):
    return lax.dot_general(a, b, dims, preferred_element_type=F32).astype(out)


def along(array, pairs):
    return lax.ppermute(array, "tp", pairs)


def fence(*arrays):
    return lax.optimization_barrier(arrays)


class Plane:
    def __init__(self, size):
        self.size = size

    def swap(self, array, bit):
        return lax.ppermute(array, "seq", [(i, i ^ bit) for i in range(self.size)])

    def higher_exact(self, total):
        bit = 8
        while bit < self.size:
            total = total + self.swap(total, bit)
            bit *= 2
        return total

    def higher(self, total):
        bit = 8
        while bit < self.size:
            total = (total.astype(F32) + self.swap(total, bit).astype(F32)).astype(BF)
            bit *= 2
        return total


def forward_kernel(blocks, q_ref, *refs):
    k_refs, v_refs = refs[:blocks], refs[blocks : 2 * blocks]
    bias_ref, out_ref, lse_ref = refs[2 * blocks], refs[-2], refs[-1]
    scale = HEAD**-0.5 * LOG2E
    rows = q_ref.shape[0]
    lane = lax.broadcasted_iota(jnp.int32, (1, 2 * HEAD), 1)
    zero = jnp.zeros((), BF)
    keys = jnp.concatenate([ref[...] for ref in k_refs])
    values = jnp.concatenate([ref[...] for ref in v_refs])
    bias = bias_ref[...]
    sub = 512
    mine = [(lane < HEAD) == (head == 0) for head in range(2)]
    k = [jnp.where(m, keys, zero) for m in mine]
    v = [jnp.where(m, values, zero) for m in mine]
    for at in range(rows // sub):
        span = pl.ds(at * sub, sub)
        q = q_ref[span, :]
        outs, lses = [], []
        for head in range(2):
            s = lax.dot_general(q, k[head], NT, preferred_element_type=F32)
            s = s * scale + bias
            top = jnp.max(s, axis=1, keepdims=True)
            p = jnp.exp2(s - top)
            total = jnp.sum(p, axis=1, keepdims=True)
            o = lax.dot_general(p.astype(BF), v[head], NN, preferred_element_type=F32)
            outs.append(o / total)
            lses.append(top + jnp.log2(total))
        out_ref[span, :] = (outs[0] + outs[1]).astype(BF)
        wide = jnp.where(lane < HEAD, lses[0], lses[1])
        flat = jnp.transpose(wide)
        lse_ref[0, :, span] = jnp.concatenate(
            [flat[0:1], flat[HEAD : HEAD + 1]], axis=0
        )


def attention_forward(q, kvs, bias, first, count, held=()):
    rows, width = q.shape
    keys = bias.shape[1]
    pairs = width // (2 * HEAD)
    wide = 2 * HEAD
    at = lambda shift: lambda h: (0, h + first + shift)
    return pl.pallas_call(
        functools.partial(forward_kernel, len(kvs)),
        grid=(count,),
        in_specs=[pl.BlockSpec((rows, wide), at(0))]
        + [pl.BlockSpec((kv.shape[0], wide), at(0)) for kv in kvs]
        + [pl.BlockSpec((kv.shape[0], wide), at(pairs)) for kv in kvs]
        + [pl.BlockSpec((1, keys), lambda h: (0, 0))]
        + [pl.BlockSpec(memory_space=pl.ANY)] * len(held),
        out_specs=[
            pl.BlockSpec((rows, wide), at(0)),
            pl.BlockSpec((1, 2, rows), lambda h: (h + first, 0, 0)),
        ],
        out_shape=[
            jax.ShapeDtypeStruct((rows, width), BF),
            jax.ShapeDtypeStruct((pairs, 2, rows), F32),
        ],
        input_output_aliases={2 * len(kvs) + 2 + n: n for n in range(len(held))},
        compiler_params=pltpu.CompilerParams(vmem_limit_bytes=32 * 2**20),
        cost_estimate=LIGHT,
        name="attention_forward",
    )(q, *kvs, *kvs, bias, *held)


def backward_kernel(
    q_ref, k_ref, v_ref, go_ref, att_ref, lse_ref, bias_ref, wkv_ref, *refs
):
    add_ref = refs[0] if len(refs) == 9 else None
    gq_ref, keep_k_ref, keep_v_ref, send_ref, part_ref, all_ref = refs[-6:]
    step, pairs = pl.program_id(0), pl.num_programs(0)
    scale = HEAD**-0.5
    wide = 2 * HEAD
    keys = k_ref.shape[0]
    lane = lax.broadcasted_iota(jnp.int32, (1, wide), 1)
    q, go = q_ref[...], go_ref[...]
    zero = jnp.zeros((), BF)
    mine = [(lane < HEAD) == (head == 0) for head in range(2)]
    qs = [jnp.where(m, q, zero) for m in mine]
    gos = [jnp.where(m, go, zero) for m in mine]
    product = go.T.astype(F32) * att_ref[...].T.astype(F32)
    inner = [
        jnp.sum(product[head * HEAD : (head + 1) * HEAD], axis=0, keepdims=True)
        for head in range(2)
    ]
    total_q = [0.0, 0.0]
    gks, gvs = [], []
    sub = 1024
    for at in range(keys // sub):
        span = pl.ds(at * sub, sub)
        bias = bias_ref[span, 0:1]
        keys_t = k_ref[span, :].T
        total_k, total_v = 0.0, 0.0
        for head in range(2):
            k = jnp.where(mine[head], k_ref[span, :], zero)
            v = jnp.where(mine[head], v_ref[span, :], zero)
            s = lax.dot_general(k, q, NT, preferred_element_type=F32)
            p = jnp.exp2(s * (scale * LOG2E) + (bias - lse_ref[0, head : head + 1, :]))
            gp = lax.dot_general(v, go, NT, preferred_element_type=F32)
            gs = (p * (gp - inner[head])).astype(BF)
            total_v += lax.dot_general(p.astype(BF), gos[head], NN, preferred_element_type=F32)
            total_k += lax.dot_general(gs, qs[head], NN, preferred_element_type=F32)
            own_keys = keys_t[head * HEAD : (head + 1) * HEAD]
            total_q[head] += lax.dot_general(own_keys, gs, NN, preferred_element_type=F32)
        gks.append((total_k * scale).astype(BF))
        gvs.append(total_v.astype(BF))
    gk, gv = jnp.concatenate(gks), jnp.concatenate(gvs)
    gq = jnp.concatenate(total_q).T * scale
    gq_ref[...] = (gq if add_ref is None else gq + add_ref[...]).astype(gq_ref.dtype)
    half = pairs // 2

    @pl.when(step < half)
    def _():
        keep_k_ref[...] = gk
        keep_v_ref[...] = gv

    @pl.when(step >= half)
    def _():
        send_ref[0] = gk
        send_ref[1] = gv

    lanes = pl.multiple_of(step * wide, wide)
    all_ref[:, pl.ds(lanes, wide)] = gk
    all_ref[:, pl.ds(pl.multiple_of(lanes + q_width(part_ref), wide), wide)] = gv

    @pl.when(step == pairs - 1)
    def _():
        for at in range(keys // 256):
            span = pl.ds(at * 256, 256)
            part = lax.dot_general(
                all_ref[span, :], wkv_ref[...], NN, preferred_element_type=F32
            )
            part_ref[span, :] = part.astype(BF)


def q_width(part_ref):
    return part_ref.shape[1]


def attention_backward(q, kv, go, attended, lse, bias, wkv, block, blocks, held):
    rows, width = q.shape
    keys = kv.shape[0]
    pairs = width // (2 * HEAD)
    wide = 2 * HEAD
    half = pairs // 2
    by_pair = pl.BlockSpec((rows, wide), lambda h: (0, h))
    stats = pl.BlockSpec((1, 2, rows), lambda h: (h, 0, 0))
    whole = pl.BlockSpec(memory_space=pl.ANY)
    keep = pl.BlockSpec((keys, wide), lambda h: (block, jnp.minimum(h, half - 1)))
    send = pl.BlockSpec((2, keys, wide), lambda h: (0, 0, jnp.maximum(h - half, 0)))
    return pl.pallas_call(
        backward_kernel,
        grid=(pairs,),
        in_specs=[
            by_pair,
            pl.BlockSpec((keys, wide), lambda h: (0, h)),
            pl.BlockSpec((keys, wide), lambda h: (0, h + pairs)),
            by_pair,
            by_pair,
            stats,
            pl.BlockSpec((keys, 128), lambda h: (0, 0)),
            pl.BlockSpec((2 * width, width), lambda h: (0, 0), pipeline_mode=pl.Buffered(1)),
        ]
        + ([by_pair, whole, whole] if held else []),
        out_specs=[by_pair, keep, keep, send, pl.BlockSpec((keys, width), lambda h: (0, 0))],
        out_shape=[
            jax.ShapeDtypeStruct((rows, width), BF if held else F32),
            jax.ShapeDtypeStruct((blocks * keys, width // 2), BF),
            jax.ShapeDtypeStruct((blocks * keys, width // 2), BF),
            jax.ShapeDtypeStruct((2, keys, width // 2), BF),
            jax.ShapeDtypeStruct((keys, width), BF),
        ],
        scratch_shapes=[pltpu.VMEM((keys, 2 * width), BF)],
        input_output_aliases={9: 1, 10: 2} if held else {},
        compiler_params=pltpu.CompilerParams(vmem_limit_bytes=48 * 2**20),
        cost_estimate=LIGHT,
        name="attention_backward",
    )(*in_hbm(q, kv, kv, go, attended), lse, bias, *in_hbm(wkv, *(held or ())))


def gelu_tile(x):
    size = jnp.abs(x)
    t = 1.0 / (1.0 + size * (0.3275911 * 0.5**0.5))
    poly = t * (
        0.127414796
        + t * (-0.142248368 + t * (0.7107068705 + t * (-0.7265760135 + t * 0.5307027145)))
    )
    bell = jnp.exp2(x * x * (-0.5 * LOG2E))
    tail = poly * bell
    cdf = jnp.where(x >= 0, 1.0 - tail, tail)
    return (x * cdf).astype(BF), (cdf + x * (bell * 0.3989422804014327)).astype(BF)


def head_grads_kernel(many, *refs):
    ins, (x_ref, y_ref, near_x_ref, near_y_ref, own_ref) = refs[:-5], refs[-5:]

    def outer(left, right):
        return lax.dot_general(left, right, TN, preferred_element_type=F32)

    if many:
        big_refs, came_refs, row_refs = ins[:2], ins[2:4], ins[4:]
        keys = row_refs[0].shape[0]
        totals_of = []
        for kind in range(2):
            total = 0.0
            for n in range(2):
                part = slice(n * keys, (n + 1) * keys)
                total += outer(big_refs[kind][part, :], row_refs[n][...])
                total += outer(came_refs[n][kind], row_refs[2 + n][...])
            totals_of.append(total.astype(BF))
    else:
        totals_of = []
        for kind in range(2):
            left, left_peer, right, right_peer = [ref[...] for ref in ins[4 * kind : 4 * kind + 4]]
            totals_of.append((outer(left, right) + outer(left_peer, right_peer)).astype(BF))
    size = HEAD // 2

    def chunk(n):
        rows = []
        for at in range(totals_of[0].shape[0] // (4 * size)):
            source = (at * 4 + (n & 1) * 2 + (n >> 1)) * size
            rows += [total[source : source + size] for total in totals_of]
        return jnp.concatenate(rows)

    half = own_ref.shape[0]
    own_ref[...] = chunk(0)

    @pl.when(pl.program_id(0) == 0)
    def _():
        x_ref[:half, :] = chunk(3)
        x_ref[half:, :] = chunk(1)
        near_y_ref[...] = chunk(2)

    @pl.when(pl.program_id(0) == 1)
    def _():
        y_ref[:half, :] = chunk(3)
        y_ref[half:, :] = chunk(2)
        near_x_ref[...] = chunk(1)


def head_grads(columns, arrived, whole_arrays, many, order=None):
    width = whole_arrays[0].shape[1]
    wide = width // 4
    half = wide // 2
    by_column = [pl.BlockSpec((a.shape[0], wide), lambda g: (0, g)) for a in columns]
    by_kind = [pl.BlockSpec((2, a.shape[1], wide), lambda g: (0, 0, g)) for a in arrived]
    whole = [
        pl.BlockSpec(a.shape, lambda g: (0, 0), pipeline_mode=pl.Buffered(1))
        for a in whole_arrays
    ]
    args, specs = [*columns, *arrived, *whole_arrays], by_column + by_kind + whole
    if order:
        args, specs = [args[n] for n in order], [specs[n] for n in order]
    fixed = lambda rows: pl.BlockSpec((rows, width), lambda g: (0, 0))
    shape = lambda rows: jax.ShapeDtypeStruct((rows, width), BF)
    return pl.pallas_call(
        functools.partial(head_grads_kernel, many),
        grid=(2,),
        in_specs=specs,
        out_specs=[fixed(wide), fixed(wide), fixed(half), fixed(half)]
        + [pl.BlockSpec((half, width), lambda g: (g, 0))],
        out_shape=[shape(wide), shape(wide), shape(half), shape(half), shape(wide)],
        compiler_params=pltpu.CompilerParams(vmem_limit_bytes=48 * 2**20),
        cost_estimate=LIGHT,
        name="head_grads",
    )(*in_hbm(*args))


def rows_kernel(moves, n_held, n_out, *refs):
    n_in = len(refs) - n_held - n_out - 1
    ins, outs, sems = refs[:n_in], refs[-1 - n_out : -1], refs[-1]
    copies = []
    for n, (source, at, count, out, place) in enumerate(moves):
        copies.append(
            pltpu.make_async_copy(
                ins[source].at[pl.ds(at, count), :],
                outs[out].at[pl.ds(place, count), :],
                sems.at[n],
            )
        )
    for copy in copies:
        copy.start()
    for copy in copies:
        copy.wait()


def put_rows(moves, shape, n_out, held=()):
    arrays, listed = [], []
    for array, at, count, out, place in moves:
        known = [n for n, a in enumerate(arrays) if a is array]
        if not known:
            arrays.append(array)
        listed.append((known[0] if known else len(arrays) - 1, at, count, out, place))
    whole = pl.BlockSpec(memory_space=pl.ANY)
    return pl.pallas_call(
        functools.partial(rows_kernel, listed, len(held), n_out),
        in_specs=[pl.BlockSpec(memory_space=pltpu.VMEM)] * len(arrays) + [whole] * len(held),
        out_specs=[whole] * n_out,
        out_shape=[jax.ShapeDtypeStruct(shape, BF)] * n_out,
        scratch_shapes=[pltpu.SemaphoreType.DMA((len(listed),))],
        input_output_aliases={len(arrays) + n: n for n in range(len(held))},
        compiler_params=pltpu.CompilerParams(vmem_limit_bytes=32 * 2**20),
        cost_estimate=LIGHT,
        name="put_rows",
    )(*arrays, *held)


def totals_kernel(at_ref, *refs):
    *ins, out_ref = refs
    size = ins[0].shape[0]
    for n in range(2):
        a, b, c = [ref[...].astype(F32) for ref in ins[3 * n : 3 * n + 3]]
        out_ref[n * size : (n + 1) * size, :] = (a + b + c).astype(BF)


def totals(ones, twos, t):
    rows, width = ones[0].shape
    size = rows // 4
    return pl.pallas_call(
        totals_kernel,
        grid_spec=pltpu.PrefetchScalarGridSpec(
            num_scalar_prefetch=1,
            grid=(4,),
            in_specs=[pl.BlockSpec((size, width), lambda u, at: (at[0] ^ u, 0))] * 6,
            out_specs=pl.BlockSpec((2 * size, width), lambda u, at: (u, 0)),
        ),
        out_shape=jax.ShapeDtypeStruct((2 * rows, width), BF),
        cost_estimate=LIGHT,
        name="totals",
    )(t[None].astype(jnp.int32), *ones, *twos)


def outer_kernel(left_ref, right_ref, left_two_ref, right_two_ref, *out_refs):
    total = lax.dot_general(left_ref[...], right_ref[...], TN, preferred_element_type=F32)
    total += lax.dot_general(
        left_two_ref[...], right_two_ref[...], TN, preferred_element_type=F32
    )
    total = total.astype(BF)
    each = pl.num_programs(0) // len(out_refs)
    for n, out_ref in enumerate(out_refs):

        @pl.when(pl.program_id(0) // each == n)
        def _():
            out_ref[...] = total


def outer_four(left, right, left_two, right_two):
    rows, hidden = left.shape
    width = right.shape[1]
    tile = 512
    each = hidden // (4 * tile)
    columns = pl.BlockSpec((rows, tile), lambda i: (0, i))
    whole = pl.BlockSpec((rows, width), lambda i: (0, 0))
    place = lambda n: lambda i: (jnp.clip(i - n * each, 0, each - 1), 0)
    return pl.pallas_call(
        outer_kernel,
        grid=(hidden // tile,),
        in_specs=[columns, whole, columns, whole],
        out_specs=[pl.BlockSpec((tile, width), place(n)) for n in range(4)],
        out_shape=[jax.ShapeDtypeStruct((hidden // 4, width), BF)] * 4,
        compiler_params=pltpu.CompilerParams(vmem_limit_bytes=32 * 2**20),
        cost_estimate=LIGHT,
        name="outer_four",
    )(left, right, left_two, right_two)


def reverse(i):
    return ((i & 1) << 2) | (i & 2) | (i >> 2)


def heads_placed_kernel(at_ref, *refs):
    *pieces, turned_ref, plain_ref, whole_ref = refs
    step, last = pl.program_id(0), pl.num_programs(0) - 1
    for i, piece in enumerate(pieces):
        place = reverse(at_ref[0] ^ i)
        size = piece.shape[0]
        whole_ref[pl.ds(pl.multiple_of(place * size, size), size), :] = piece[...]

    @pl.when(step < last)
    def _():
        turned_ref[0] = whole_ref[...].T.astype(F32)

    @pl.when(step == last)
    def _():
        plain_ref[...] = whole_ref[...].astype(F32)


def heads_placed(pieces, s8):
    kind_at = lambda n: jnp.where(n == 0, 0, jnp.where(n == 3, 1, n + 1))
    width = pieces[0].shape[1]
    size = pieces[0].shape[0] // 4
    rows = 8 * size
    return pl.pallas_call(
        heads_placed_kernel,
        grid=(4,),
        in_specs=[pl.BlockSpec(memory_space=pltpu.SMEM)]
        + [pl.BlockSpec((size, width), lambda n: (kind_at(n), 0)) for _ in pieces],
        out_specs=[
            pl.BlockSpec((1, width, rows), lambda n: (jnp.minimum(n, 2), 0, 0)),
            pl.BlockSpec((rows, width), lambda n: (0, 0)),
        ],
        out_shape=[
            jax.ShapeDtypeStruct((3, width, rows), F32),
            jax.ShapeDtypeStruct((rows, width), F32),
        ],
        scratch_shapes=[pltpu.VMEM((rows, width), BF)],
        compiler_params=pltpu.CompilerParams(vmem_limit_bytes=32 * 2**20),
        cost_estimate=LIGHT,
        name="heads_placed",
    )(s8[None].astype(jnp.int32), *pieces)


def placed_kernel(flips, at_ref, *refs):
    *pieces, out_ref, whole_ref = refs
    for i, piece in enumerate(pieces):
        place = at_ref[0] ^ i
        size = piece.shape[0]
        whole_ref[pl.ds(pl.multiple_of(place * size, size), size), :] = piece[...]
    out = whole_ref[...]
    out = out.T if flips else out
    out_ref[...] = out.astype(F32)


def placed(pieces, size, s8, flips):
    width = pieces[0][0].shape[1]
    tile = 512
    rows = 8 * size
    if flips:
        out_shape, out_spec = (width, rows), pl.BlockSpec((tile, rows), lambda c: (c, 0))
    else:
        out_shape, out_spec = (rows, width), pl.BlockSpec((rows, tile), lambda c: (0, c))
    part = lambda first: pl.BlockSpec((size, tile), lambda c: (first, c))
    return pl.pallas_call(
        functools.partial(placed_kernel, flips),
        grid=(width // tile,),
        in_specs=[pl.BlockSpec(memory_space=pltpu.SMEM)] + [part(first) for _, first in pieces],
        out_specs=out_spec,
        out_shape=jax.ShapeDtypeStruct(out_shape, F32),
        scratch_shapes=[pltpu.VMEM((rows, tile), BF)],
        compiler_params=pltpu.CompilerParams(vmem_limit_bytes=32 * 2**20),
        cost_estimate=LIGHT,
        name="placed",
    )(s8[None].astype(jnp.int32), *[array for array, _ in pieces])


def centred(values):
    centre = values - jnp.mean(values, axis=-1, keepdims=True)
    root = lax.rsqrt(jnp.mean(centre * centre, axis=-1, keepdims=True) + LN_EPS)
    return centre * root, root


def norm_pull(grad, gain, unit, root):
    scaled = grad * gain
    mean = jnp.mean(scaled, axis=-1, keepdims=True)
    slope = jnp.mean(scaled * unit, axis=-1, keepdims=True)
    return root * (scaled - mean - unit * slope), jnp.sum(grad * unit, axis=0)


def per_device(
    seq_size, tokens, w_qkv, w_out, w_up, w_down, gain_one, gain_two, cotangent, bucket, lengths
):
    rows, width = tokens.shape
    t = lax.axis_index("tp")
    middle = (t == 1) | (t == 2)
    s8 = lax.axis_index("seq") % 8
    plane = Plane(seq_size)
    swap = plane.swap
    hid = w_out.shape[0]
    ff = w_down.shape[0]
    qp, fp = hid // 8, ff // 8
    up = lambda a: a.astype(F32)
    across = lambda a, j: along(a, [(i, i ^ j) for i in range(4)])

    w_attn_own = jnp.concatenate([w_qkv.transpose(1, 2, 0), w_out[None]])

    def attn_piece(i):
        return lax.dynamic_slice_in_dim(w_attn_own, reverse(s8 ^ i) * qp, qp, axis=1)

    def up_piece(i):
        return lax.dynamic_slice_in_dim(w_up, (s8 ^ i) * fp, fp, axis=1).T

    def down_piece(i):
        return lax.dynamic_slice_in_dim(w_down, (s8 ^ i) * fp, fp, axis=0)

    attn_own = attn_piece(0).reshape(4 * qp, width)
    up_own = jnp.concatenate([up_piece(2 * i) for i in range(4)])
    down_own = jnp.concatenate([down_piece(2 * i) for i in range(4)])
    ff_own = jnp.concatenate([up_own[:fp], down_own[:fp]])

    upper = rows // 2
    gathered = [
        lax.all_gather(tokens[n * upper : (n + 1) * upper], "tp", axis=0, tiled=True)
        for n in range(2)
    ]
    a_far = [across(attn_own, j) for j in (1, 2, 3)]
    whole = bucket[0] == 1
    place = jnp.arange(rows, dtype=jnp.int32)
    seen = []
    for u in range(4):
        alone = jnp.where(t == u, lengths[0, u], 0)
        limit = jnp.where(whole, lengths[0, 0] - u * rows, alone)
        seen.append((place < limit).reshape(2, upper))
    bias = jnp.where(jnp.stack(seen, axis=1), 0.0, -1e9).astype(F32).reshape(4 * rows)
    bias, *a_far = fence(bias, *a_far)
    bias_cols = jnp.broadcast_to(bias[:, None], (4 * rows, 128))

    attn_three = jnp.concatenate(a_far)
    half = attn_three.shape[0] // 2
    a_x, a_y = swap(attn_three, 2), swap(attn_three, 4)
    attn_three, a_x, a_y = fence(attn_three, a_x, a_y)
    a_d1, a_d2 = swap(a_y[:half], 2), swap(a_x[half:], 4)
    others = [swap(attn_three, 1), swap(a_x, 1), swap(a_y, 1)]
    a_d1, a_d2, *others = fence(a_d1, a_d2, *others)
    others += fence(swap(a_d1, 1), swap(a_d2, 1))

    four = [attn_three, a_x, a_y, a_d1, a_d2]
    pieces = []
    for i in range(8):
        part = others if i & 1 else four
        far = part[i >> 1] if i < 6 else jnp.concatenate(part[3:])
        pieces.append(jnp.concatenate([attn_piece(i)[None], far.reshape(3, 4, qp, width)]))
    w_attn = jnp.stack(pieces).reshape(2, 2, 2, 4, 4, qp, width).transpose(4, 2, 3, 1, 0, 5, 6)
    w_attn = w_attn.reshape(4, width, width)
    wq, wk, wv, wo = [w_attn[n] for n in range(4)]
    wkv = w_attn[1:3].reshape(2 * width, width)

    wq, wkv, ff_own, up_own, down_own = fence(wq, wkv, ff_own, up_own, down_own)
    f_one, f_far = along(ff_own, PAIR), along(ff_own, MIDDLE)
    q = mm(tokens, wq, NT, BF)
    upper_kv = mm(gathered[0], wkv, NT, BF)
    f_one, f_far, q, upper_kv = fence(f_one, f_far, q, upper_kv)
    f_two, f_two_end = along(f_one, MIDDLE), along(f_far, OUTWARD)
    one_x, one_y = swap(f_one, 2), swap(f_one, 4)
    tokens_peer = swap(tokens, 1)
    f_two, f_two_end, one_x, one_y, tokens_peer, *kvs = fence(
        f_two, f_two_end, one_x, one_y, tokens_peer, upper_kv, mm(gathered[1], wkv, NT, BF)
    )
    f_three_end = along(f_two, OUTWARD)
    f_two = jnp.where(middle, f_two, f_two_end)
    two_x, two_y = swap(f_two, 2), swap(f_two, 4)
    one_d1, one_d2 = swap(one_y[:fp], 2), swap(one_x[fp:], 4)
    bias_row = bias[None]
    held = attention_forward(q, kvs, bias_row, 0, 3)
    f_three_end, one_d1, one_d2, two_x, two_y, *held = fence(
        f_three_end, one_d1, one_d2, two_x, two_y, *held
    )
    f_three = jnp.where(middle, f_far, f_three_end)
    three_x, three_y = swap(f_three, 2), swap(f_three, 4)
    two_d1, two_d2 = swap(two_y[:fp], 2), swap(two_x[fp:], 4)

    def moves(j, block):
        own, by_x, by_y, d1, d2 = block
        sources = [(own, own, fp), (by_x, by_x, fp), (by_y, by_y, fp), (d1, d2, 0)]
        for i, (a, b, at) in enumerate(sources):
            yield (a, 0, fp, 0, (4 * i + j) * fp)
            yield (b, at, fp, 1, (4 * i + j) * fp)

    own = []
    for i in range(4):
        own.append((up_own, i * fp, fp, 0, 4 * i * fp))
        own.append((down_own, i * fp, fp, 1, 4 * i * fp))
    one = moves(1, (f_one, one_x, one_y, one_d1, one_d2))
    w_ff = put_rows([*own, *one], (ff * 2, width), 2)
    w_ff = fence(*w_ff, *held)
    w_ff, held = w_ff[:2], w_ff[2:]
    held = attention_forward(q, kvs, bias_row, 3, 3, held)
    two_d1, two_d2, three_x, three_y, *held = fence(two_d1, two_d2, three_x, three_y, *held)
    three_d1, three_d2 = swap(three_y[:fp], 2), swap(three_x[fp:], 4)
    held = attention_forward(q, kvs, bias_row, 6, 2, held)
    three_d1, three_d2, *held = fence(three_d1, three_d2, *held)
    attended, lse = held
    first_sum = up(tokens) + mm(attended, wo, NN)
    unit_one, root_one = centred(first_sum)
    normed = unit_one * gain_one
    normed_low = normed.astype(BF)

    two = moves(2, (f_two, two_x, two_y, two_d1, two_d2))
    three = moves(3, (f_three, three_x, three_y, three_d1, three_d2))
    wu, wd = put_rows([*two, *three], (ff * 2, width), 2, w_ff)

    normed_peer = swap(normed_low, 1)
    gathered_peer = [swap(part, 1) for part in gathered]
    attended_peer = swap(attended[:, width // 2 :], 1)
    act, slope = gelu_tile(mm(normed_low, wu, NT))
    act_peer, slope_peer = gelu_tile(mm(normed_peer, wu, NT))
    shrunk_peer = swap(mm(act_peer, wd, NN, BF), 1)
    unit_two, root_two = centred(normed + mm(act, wd, NN) + up(shrunk_peer))
    mixed = (unit_two * gain_two).astype(BF)

    grad_second, gain_grad_two = norm_pull(up(cotangent), gain_two, unit_two, root_two)
    second_low = grad_second.astype(BF)
    second_peer = swap(second_low, 1)
    grad_exp = (mm(second_low, wd, NT) * up(slope)).astype(BF)
    grad_exp_peer = (mm(second_peer, wd, NT) * up(slope_peer)).astype(BF)
    normed_part_peer = swap(mm(grad_exp_peer, wu, NN, BF), 1)
    normed_part = mm(grad_exp, wu, NN)
    twos = outer_four(act, second_low, act_peer, second_peer)
    normed_part, normed_part_peer, *twos = fence(normed_part, normed_part_peer, *twos)
    diag_y, two_y = swap(twos[3], 4), swap(twos[2], 4)
    ones = outer_four(grad_exp, normed_low, grad_exp_peer, normed_peer)
    grad_normed = grad_second + normed_part + up(normed_part_peer)
    normed_part, *ones = fence(normed_part, *ones)
    diag_x, one_x = swap(ones[3], 2), swap(ones[1], 2)
    grad_first, gain_grad_one = norm_pull(grad_normed, gain_one, unit_one, root_one)
    first_low = grad_first.astype(BF)
    first_peer = swap(first_low, 1)
    go = mm(first_low, wo, NT, BF)
    core = width // 2
    go, first_peer, attended_peer, *gathered_peer = fence(
        go, first_peer, attended_peer, *gathered_peer
    )

    def pull(n, held):
        keys = bias_cols[2 * n * rows : 2 * (n + 1) * rows]
        *held, send, part = attention_backward(
            q, kvs[n], go, attended, lse, keys, wkv, n, 2, held
        )
        return held, send, part

    def line_sum(part):
        return lax.psum_scatter(part, "tp", scatter_dimension=0, tiled=True)

    gains = jnp.stack([gain_grad_one, gain_grad_two])
    gains_came = swap(gains, 1)
    held, send, part = pull(0, None)
    diag_x, diag_y, one_x, two_y, send, part, gains_came, *held = fence(
        diag_x, diag_y, one_x, two_y, send, part, gains_came, *held
    )
    upper_sum = line_sum(part)
    came = [swap(send, 1)]
    gains = gains + gains_came
    gains_came = swap(gains, 2)
    two_x = (up(twos[1]) + up(diag_y)).astype(BF)
    one_y = (up(ones[2]) + up(diag_x)).astype(BF)
    two_x, one_y, *held = fence(two_x, one_y, *held)
    two_x, one_y = swap(two_x, 2), swap(one_y, 4)
    held, send, part = pull(1, held)
    two_x, one_y, came[0], send, part, gains_came, *held = fence(
        two_x, one_y, came[0], send, part, gains_came, *held
    )
    gq, gk, gv = held
    gq_peer = swap(gq[:, core:], 1)
    gains = gains + gains_came
    gains_came = swap(gains, 4)
    part = part.reshape(4, 2, upper // 2, width)
    part_one, part_two = [part[:, n].reshape(rows, width) for n in range(2)]
    lower_one = line_sum(part_one)
    ff_total = plane.higher(totals((ones[0], one_x, one_y), (twos[0], two_x, two_y), t))
    upper_sum, ff_total = fence(upper_sum, ff_total)
    ff_total = line_sum(ff_total)
    gq_peer, gains_came, send = fence(gq_peer, gains_came, send)
    came.append(swap(send, 1))
    gains = plane.higher_exact(gains + gains_came)
    coarse = lax.reduce_precision(gains, exponent_bits=8, mantissa_bits=7)
    gains = jnp.concatenate([coarse, gains - coarse, jnp.zeros((12, width), F32)]).astype(BF)
    light = head_grads(
        [gq, gq_peer, attended, attended_peer],
        [],
        [tokens, tokens_peer, first_low, first_peer],
        False,
        (0, 1, 4, 5, 2, 3, 6, 7),
    )
    came[1], *light = fence(came[1], *light)
    to_x, to_y = swap(light[0], 2), swap(light[1], 4)
    heavy = head_grads([gk, gv], came, [*gathered, *gathered_peer], True)
    to_x, to_y, gq, *heavy = fence(to_x, to_y, gq, *heavy)
    half = 4 * qp
    add = lambda *arrays: sum(up(a) for a in arrays).astype(BF)

    def second_hop(parts, to_x, to_y):
        return add(parts[2], to_y[:half]), add(parts[3], to_x[:half])

    def mine_of(parts, to_x, to_y, on_x, on_y):
        own = parts[4]
        total = [add(own[:half], to_x[half:], on_y), add(own[half:], to_y[half:], on_x)]
        return plane.higher(jnp.concatenate(total)).reshape(4, 2 * qp, width)

    next_x, next_y = second_hop(light, to_x, to_y)
    next_x, next_y, *heavy = fence(next_x, next_y, *heavy)
    on_x, on_y = swap(next_x, 2), swap(next_y, 4)
    far_x, far_y = swap(heavy[0], 2), swap(heavy[1], 4)
    first = mm(gq, wq, NN) + grad_first
    on_x, on_y, far_x, far_y, first = fence(on_x, on_y, far_x, far_y, first)
    next_x, next_y = second_hop(heavy, far_x, far_y)
    next_x, next_y, ff_total = fence(next_x, next_y, ff_total)
    last_x, last_y = swap(next_x, 2), swap(next_y, 4)
    f_x, f_y = swap(ff_total, 2), swap(ff_total, 4)
    light_mine = mine_of(light, to_x, to_y, on_x, on_y)
    last_x, last_y, light_mine = fence(last_x, last_y, light_mine)
    heavy_mine = mine_of(heavy, far_x, far_y, last_x, last_y)
    a_mine = jnp.concatenate([light_mine, heavy_mine], axis=1)
    pairs = a_mine.reshape(2, 2, 4 * qp, width)
    pairs = jnp.where((t & 1) == 1, pairs[:, ::-1], pairs)
    a_mine = jnp.where((t & 2) == 2, pairs[::-1], pairs).reshape(a_mine.shape)
    gains = jnp.broadcast_to(gains[None], (4, 16, width))
    a_mine = fence(jnp.concatenate([a_mine, gains], axis=1))[0]
    a_came = lax.all_to_all(a_mine, "tp", split_axis=0, concat_axis=0, tiled=True)
    f_core = [swap(ff_total, 1)]
    f_d1, f_d2 = swap(f_y[:fp], 2), swap(f_x[fp:], 4)
    f_core += [swap(f_x, 1), swap(f_y, 1)]
    a_came, part_two, f_d1, f_d2, b0, b1, b2 = fence(a_came, part_two, f_d1, f_d2, *f_core)
    f_core = [b0, b1, b2]
    lower_two = line_sum(part_two)
    a_total = fence(jnp.sum(up(a_came[:, : 4 * qp]), axis=0).astype(BF))[0]
    gains = jnp.sum(up(a_came[:, 4 * qp : 4 * qp + 4]), axis=0)
    gains = gains[:2] + gains[2:]
    a_four = [a_total, swap(a_total, 2), swap(a_total, 4), swap(a_total, 6)]
    a_core = [swap(a_total, 1)]
    f_core += [swap(f_d1, 1), swap(f_d2, 1)]
    f_four = [ff_total, f_x, f_y, f_d1, f_d2]
    ups, downs = [], []
    for i in range(8):
        part = f_core if i & 1 else f_four
        ups.append((part[i >> 1], 0))
        downs.append((part[i >> 1], 1) if i < 6 else (part[4], 0))
    grad_up = placed(ups, fp, s8, True)
    grad_down = placed(downs, fp, s8, False)
    grad_up, grad_down, *a_four = fence(grad_up, grad_down, *a_four)
    a_core += [swap(a, 1) for a in a_four[1:]]
    a_all = [(a_core if i & 1 else a_four)[i >> 1] for i in range(8)]
    grad_qkv, grad_out = heads_placed(a_all, s8)
    tokens_grad = (first + up(jnp.concatenate([upper_sum, lower_one, lower_two]))).astype(BF)
    return (
        mixed,
        tokens_grad,
        grad_qkv.transpose(1, 0, 2),
        grad_out,
        grad_up,
        grad_down,
        gains[0],
        gains[1],
    )


def solution(mesh):
    rows = P(("seq", "tp"), None)
    weights = (P(None, None, "tp"), P("tp", None), P(None, "tp"), P("tp", None), P(), P())
    return jax.shard_map(
        functools.partial(per_device, mesh.shape["seq"]),
        mesh=mesh,
        in_specs=(rows,) + weights + (rows, P("seq"), P("seq", None)),
        out_specs=(rows, rows) + weights,
        check_vma=False,
    )
```
